128 devices in a mesh: dp: 2 (over core), ctx: 64 (over y, z, x).
Axes of the slice: x: 4, y: 4, z: 4, core: 2. Of those that a mesh axis runs over, the one named last changes fastest.
Arguments:
- queries: bfloat16 [16384, 1024], P(('dp', 'ctx')), may hold values from -5 to 5
- keys_values: bfloat16 [16384, 256], P(('dp', 'ctx')), may hold values from -4 to 4
- grad_out: bfloat16 [16384, 1024], P(('dp', 'ctx')), may hold values from -6 to 6
- placement: int32 [16384], P(('dp', 'ctx')), may hold values from 0 to 16383, as said below
- doc_lengths: int32 [2, 16], P('dp'), may hold values from 1 to 4224, 8192 in all within a row
Outputs:
- attn_out: bfloat16 [16384, 1024], P(('dp', 'ctx'))
- grad_queries: bfloat16 [16384, 1024], P(('dp', 'ctx'))
- grad_keys_values: bfloat16 [16384, 256], P(('dp', 'ctx'))
The draws below stay inside these ranges and needn't reach their ends.
Inputs may be any that keep to these rules, and one draw needn't show every extreme that they name: `placement`: A permutation. Group position p lies on device p // 128 in dp+ctx order; the 128 loader rows of each device go exactly 1 to every device. `doc_lengths`: each row sums to 8192; its longest document has exactly 4224 tokens.
All inputs are finite; a program needn't handle non-finite values.
Results may differ from the reference program's by a relative error of at most 0.03.
Values may be sent and summed in bfloat16 or wider, within the bound.
No kernel may reach another device: no remote copies, remote signals or barrier semaphores. Data moves between devices by JAX's collectives and lax.ppermute only.
A program may use at most 192 MiB of HBM per device.

```python
import math
import jax
import jax.numpy as jnp
import numpy as np
from jax import lax

HD = 128
HQ = 8
TOK_DEV = 128
DOCS = 16
STREAM = 8192
TOKENS = 16384
MOST = 4224
N_DP = 2


def shared_placement(key):
    key = jax.random.fold_in(key, 1)
    first_key, second_key = jax.random.split(key)
    device_count = TOKENS // TOK_DEV
    per_peer = TOK_DEV // device_count
    column_ids = jnp.arange(TOK_DEV, dtype=jnp.int32)
    slot_scores = jax.random.randint(first_key, (device_count, TOK_DEV), 0, 1 << 20) * TOK_DEV + column_ids[None, :]
    slot_order = jnp.argsort(slot_scores, axis=1).astype(jnp.int32)
    row_scores = jax.random.randint(second_key, (device_count, TOK_DEV), 0, 1 << 20) * TOK_DEV + column_ids[None, :]
    row_order = jnp.argsort(row_scores, axis=1).astype(jnp.int32)
    source_ids = jnp.arange(device_count, dtype=jnp.int32)[:, None]
    target_device = column_ids[None, :] // per_peer
    within_peer = column_ids[None, :] % per_peer
    target = target_device * TOK_DEV + slot_order[target_device, source_ids * per_peer + within_peer]
    result = jnp.zeros((device_count, TOK_DEV), jnp.int32).at[source_ids, row_order].set(target)
    return result.reshape(-1)


def draw_placement(key, part):
    return shared_placement(key)


def draw_queries(key, part):
    key = jax.random.fold_in(key, 11)
    values = 2.5 * jax.random.truncated_normal(key, -2.0, 2.0, (TOKENS, HQ * HD), jnp.float32)
    return values.astype(jnp.bfloat16)


def draw_keys_values(key, part):
    key = jax.random.fold_in(key, 12)
    values = jax.random.truncated_normal(key, -4.0, 4.0, (TOKENS, 2 * HD), jnp.float32)
    return values.astype(jnp.bfloat16)


def block_levels(key, shape, pieces, least, high):
    loudness, own = 1.0, jax.random.fold_in(key, 6)
    for position, blocks in pieces:
        steps = jnp.exp(jax.random.uniform(jax.random.fold_in(own, position), (blocks,), jnp.float32, least / len(pieces), high / len(pieces)))
        loudness = loudness * jnp.repeat(steps, shape[position] // blocks).reshape([-1 if axis == position else 1 for axis in range(len(shape))])
    return loudness


def length_profile(number_of, total, reach, lean):
    portions = [(1 << 20) // math.isqrt(rank ** lean) + 1 for rank in range(2, number_of + 1)]
    spare, counts = total - reach - (number_of - 1), [1] * (number_of - 1)
    while spare > 0:
        candidates = [i for i in range(number_of - 1) if counts[i] < reach]
        whole, left = sum([portions[i] for i in candidates]), spare
        for i in candidates:
            more = min(reach - counts[i], max(1, left * portions[i] // whole), spare)
            counts[i] = counts[i] + more
            spare = spare - more
    return np.array([reach] + counts)


def ragged_sizes(stream_key, amount, total, reach, slope):
    if amount == 2:
        one = jax.random.randint(stream_key, (), max(1, total - reach), min(reach, total - 1) + 1)
        return jnp.stack([one, total - one])
    tallies = jnp.asarray(length_profile(amount, total, reach, slope), jnp.int32)
    twos = (amount - 1) // 2
    giver, receiver = tallies[1:1 + 2 * twos:2], tallies[2:2 + 2 * twos:2]
    room = jnp.minimum(giver - 1, reach - receiver)
    passed = jax.random.randint(jax.random.fold_in(stream_key, 1), (twos,), 0, 1 << 20) % (room + 1)
    tallies = tallies.at[1:1 + 2 * twos:2].set(giver - passed).at[2:2 + 2 * twos:2].set(receiver + passed)
    return tallies[jax.random.permutation(jax.random.fold_in(stream_key, 2), amount)]


def gaussian(key, extent, scale, most, pieces=(), kind=jnp.bfloat16):
    level = block_levels(key, extent, pieces, -0.22, 0.18) if pieces else 1.0
    values = jax.random.normal(key, extent, jnp.float32) * scale * level
    return jnp.minimum(jnp.maximum(values, -most), most).astype(kind)


def setup_inputs(seed: int = 0) -> dict:
    key_of = jax.random.split(jax.random.key(seed), 6)
    return {
        "queries": draw_queries(jax.random.fold_in(key_of[5], 71), 0),
        "keys_values": draw_keys_values(jax.random.fold_in(key_of[5], 71), 0),
        "grad_out": gaussian(key_of[2], (TOKENS, HQ * HD), 1.0, 6.0, ((0, 128),)),
        "placement": draw_placement(jax.random.fold_in(key_of[5], 71), 0),
        "doc_lengths": jax.vmap(lambda own: ragged_sizes(own, DOCS, STREAM, MOST, 2))(jax.random.split(key_of[4], N_DP)).reshape((N_DP, DOCS)).astype(jnp.int32),
    }


query_block = 256
masked_score = -1e30


def document_starts(positions, lengths):
    doc_ends = jnp.cumsum(lengths).astype(jnp.int32)
    earlier = jnp.where(doc_ends[None, :] <= positions[:, None], lengths[None, :], 0)
    return jnp.sum(earlier, axis=1).astype(jnp.int32)


def attend_stream(stream_q, stream_kv, stream_g, lengths):
    stream_len = stream_q.shape[0]
    window_len = MOST + query_block
    score_scale = HD ** -0.5
    padded_kv = jnp.concatenate([jnp.zeros((window_len, 2 * HD), jnp.bfloat16), stream_kv], axis=0)
    start_grads = jnp.zeros((window_len + stream_len, 2 * HD), jnp.float32)

    def one_block(key_grads, block_index):
        block_begin = block_index * query_block
        query_heads = lax.dynamic_slice_in_dim(stream_q, block_begin, query_block, 0).reshape(query_block, HQ, HD).astype(jnp.float32)
        grad_heads = lax.dynamic_slice_in_dim(stream_g, block_begin, query_block, 0).reshape(query_block, HQ, HD).astype(jnp.float32)
        key_window = lax.dynamic_slice_in_dim(padded_kv, block_begin + query_block, window_len, 0).astype(jnp.float32)
        keys_part = key_window[:, :HD]
        values_part = key_window[:, HD:]
        key_pos = block_begin + query_block - window_len + jnp.arange(window_len, dtype=jnp.int32)
        query_pos = block_begin + jnp.arange(query_block, dtype=jnp.int32)
        query_start = document_starts(query_pos, lengths)
        allowed = ((key_pos[None, :] <= query_pos[:, None]) & (key_pos[None, :] >= query_start[:, None]))[:, None, :]
        scores = jnp.einsum("thd,kd->thk", query_heads, keys_part) * score_scale
        masked = jnp.where(allowed, scores, masked_score)
        row_top = jnp.max(masked, axis=2)
        row_total = jnp.sum(jnp.where(allowed, jnp.exp(masked - row_top[..., None]), 0.0), axis=2)
        log_total = row_top + jnp.log(row_total)
        weights_full = jnp.where(allowed, jnp.exp(scores - log_total[..., None]), 0.0)
        weights_half = lax.optimization_barrier(weights_full.astype(jnp.bfloat16)).astype(jnp.float32)
        attended = jnp.einsum("thk,kd->thd", weights_half, values_part).astype(jnp.bfloat16)
        out_dot = jnp.sum(grad_heads * attended.astype(jnp.float32), axis=2)
        grad_weights = jnp.einsum("thd,kd->thk", grad_heads, values_part)
        grad_scores = weights_full * (grad_weights - out_dot[..., None]) * score_scale
        grad_half = lax.optimization_barrier(grad_scores.astype(jnp.bfloat16)).astype(jnp.float32)
        grad_query = jnp.einsum("thk,kd->thd", grad_half, keys_part).astype(jnp.bfloat16)
        grad_pair = jnp.concatenate([jnp.einsum("thk,thd->kd", grad_half, query_heads), jnp.einsum("thk,thd->kd", weights_half, grad_heads)], axis=1)
        offset = block_begin + query_block
        current = lax.dynamic_slice_in_dim(key_grads, offset, window_len, 0)
        key_grads = lax.dynamic_update_slice_in_dim(key_grads, current + grad_pair, offset, 0)
        return key_grads, (attended.reshape(query_block, HQ * HD), grad_query.reshape(query_block, HQ * HD))

    block_ids = jnp.arange(stream_len // query_block, dtype=jnp.int32)
    key_grads, outputs = lax.scan(one_block, start_grads, block_ids)
    attended_all = outputs[0].reshape(stream_len, HQ * HD)
    grad_query_all = outputs[1].reshape(stream_len, HQ * HD)
    return attended_all, grad_query_all, key_grads[window_len:].astype(jnp.bfloat16)


def reference(queries, keys_values, grad_out, placement, doc_lengths):
    total_rows = queries.shape[0]
    source = jnp.zeros((total_rows,), jnp.int32).at[placement].set(jnp.arange(total_rows, dtype=jnp.int32))
    group_q = queries[source]
    group_kv = keys_values[source]
    group_g = grad_out[source]
    attended_parts = []
    grad_query_parts = []
    grad_pair_parts = []
    for stream_index in range(N_DP):
        lower = stream_index * STREAM
        results = attend_stream(group_q[lower:lower + STREAM], group_kv[lower:lower + STREAM], group_g[lower:lower + STREAM], doc_lengths[stream_index])
        attended_parts.append(results[0])
        grad_query_parts.append(results[1])
        grad_pair_parts.append(results[2])
    attended_all = jnp.concatenate(attended_parts, axis=0)
    grad_query_all = jnp.concatenate(grad_query_parts, axis=0)
    grad_pair_all = jnp.concatenate(grad_pair_parts, axis=0)
    return attended_all[placement], grad_query_all[placement], grad_pair_all[placement]
```

```python
import functools

import jax
import jax.numpy as jnp
import numpy as np
from jax import lax
from jax.experimental import pallas as pl
from jax.experimental.pallas import tpu as pltpu
from jax.sharding import PartitionSpec as P

block = 128
head = 128
window = 18
kv_rows = 2 * window
slot_row = kv_rows
end_rows = kv_rows + 1
head_rows = 40
send_rows = 56
group = 16
other_half = 1000
nothing = -100000
masked_score = -1e30
vmem_bytes = 60 * 1024 * 1024


def kv_code():
    i = lax.broadcasted_iota(jnp.int32, (group, head_rows, block), 0)
    r = lax.broadcasted_iota(jnp.int32, (group, head_rows, block), 1)
    code = 2 * i + (r >> 1) * 2 + (r & 1) * other_half
    return jnp.where(r < kv_rows, code, nothing).reshape(group * head_rows, block)


def kv_offset(t):
    chip = t % 64
    return 2 * (chip - (window - 1)) + t // 64, chip // 32


def one_hot(mask):
    return jnp.where(mask, 1.0, 0.0).astype(jnp.bfloat16)


def pack_kernel(place_ref, ends_ref, q_ref, kv_ref, g_ref, out_ref):
    place = place_ref[...]
    rows = place >> 7
    slots = place & (block - 1)
    lane = lax.broadcasted_iota(jnp.int32, (block, block), 1)
    rows_down = jnp.broadcast_to(rows.astype(jnp.float32), (block, block)).T.astype(jnp.int32)
    slots_down = jnp.broadcast_to(slots.astype(jnp.float32), (block, block)).T
    slot_line = jnp.sum(jnp.where(rows_down == lane, slots_down, 0.0), axis=0, keepdims=True)
    lane8 = lax.broadcasted_iota(jnp.int32, (8, block), 1)
    row8 = lax.broadcasted_iota(jnp.int32, (8, block), 0)
    extra = jnp.where(row8 == slot_row % 8, jnp.broadcast_to(slot_line, (8, block)), 0.0)
    end = jnp.int32(0)
    for i in range(16):
        end = end + ends_ref[0, i]
        extra = jnp.where((lane8 == i) & (row8 == end_rows % 8), (end >> 6).astype(jnp.float32), extra)
        extra = jnp.where((lane8 == i) & (row8 == end_rows % 8 + 1), (end & 63).astype(jnp.float32), extra)
    code = kv_code()
    kv = jnp.concatenate([kv_ref[:, :head], kv_ref[:, head:]], axis=0)
    for t in range(0, 128, group):
        offset, stream = kv_offset(t)
        line = jnp.where((rows >> 6) == stream, rows - offset, 2 * nothing)
        pick = jnp.concatenate([one_hot(code == line), one_hot(code == line + other_half)], axis=1)
        got = jnp.dot(pick, kv, preferred_element_type=jnp.float32).reshape(group, head_rows, head)
        tail = got[:, head_rows - 8 :, :] + extra[None]
        got = jnp.concatenate([got[:, : head_rows - 8, :], tail], axis=1)
        out_ref[t : t + group, :head_rows, :] = got.astype(jnp.bfloat16)
    i = lax.broadcasted_iota(jnp.int32, (group * 8, block), 0)
    codes = [
        jnp.where(((i & 7) >> 1) == h, 2 * (i >> 3) + (i & 1), nothing) for h in range(4)
    ]
    for core in range(2):
        both = jnp.concatenate(
            [
                jnp.concatenate(
                    [
                        q_ref[:, (4 * core + h) * head : (4 * core + h + 1) * head],
                        g_ref[:, (4 * core + h) * head : (4 * core + h + 1) * head],
                    ],
                    axis=1,
                )
                for h in range(4)
            ],
            axis=0,
        )
        for c in range(0, 64, group):
            line = rows - 2 * c
            pick = jnp.concatenate([one_hot(codes[h] == line) for h in range(4)], axis=1)
            got = jnp.dot(pick, both, preferred_element_type=jnp.float32).astype(jnp.bfloat16)
            t = core * 64 + c
            out_ref[t : t + group, head_rows : head_rows + 8, :] = got[:, :head].reshape(group, 8, head)
            out_ref[t : t + group, head_rows + 8 :, :] = got[:, head:].reshape(group, 8, head)


def unpack_kernel(place_ref, code_ref, got_ref, out_ref, dq_ref, dkv_ref):
    rows_down = jnp.broadcast_to((place_ref[...] >> 7).astype(jnp.float32), (block, block)).T.astype(jnp.int32)
    wide = jnp.concatenate([rows_down] * (group * head_rows // block), axis=1)
    code = code_ref[0:1, :]
    sums = [jnp.zeros((block, head), jnp.float32), jnp.zeros((block, head), jnp.float32)]
    for t in range(0, 128, group):
        offset, stream = kv_offset(t)
        down = jnp.where((wide >> 6) == stream, wide - offset, 2 * nothing)
        terms = got_ref[t : t + group, :head_rows, :].reshape(group * head_rows, head)
        for half in range(2):
            pick = one_hot(code == down + half * other_half)
            sums[half] = sums[half] + jnp.dot(pick, terms, preferred_element_type=jnp.float32)
    dkv_ref[...] = jnp.concatenate(sums, axis=1).astype(jnp.bfloat16)
    lane = lax.broadcasted_iota(jnp.int32, (block, 512), 1)
    wide = jnp.concatenate([rows_down] * 4, axis=1)
    chip_code = 2 * (lane >> 3) + (lane & 1)
    for core in range(2):
        both = jnp.concatenate(
            [
                got_ref[core * 64 : core * 64 + 64, head_rows : head_rows + 8, :].reshape(512, head),
                got_ref[core * 64 : core * 64 + 64, head_rows + 8 :, :].reshape(512, head),
            ],
            axis=1,
        )
        for h in range(4):
            pick = one_hot((chip_code == wide) & (((lane & 7) >> 1) == h))
            got = jnp.dot(pick, both, preferred_element_type=jnp.float32).astype(jnp.bfloat16)
            at = (4 * core + h) * head
            out_ref[:, at : at + head] = got[:, :head]
            dq_ref[:, at : at + head] = got[:, head:]


def nt(a, b):
    return lax.dot_general(a, b, (((1,), (1,)), ((), ())), preferred_element_type=jnp.float32)


def tn(a, b):
    return lax.dot_general(a, b, (((0,), (0,)), ((), ())), preferred_element_type=jnp.float32)


def attention_kernel(
    where_ref, mine_ref, other_ref, info_ref, qg_ref,
    dmine_ref, dother_ref, out_ref, dq_ref,
    scores, weights, top, total, acc, dot, qs, gs, key_pos, bound,
):
    core = where_ref[0]
    chip = where_ref[1]
    first = 2 * (chip - (window - 1))
    scale = head ** (-0.5)
    to_exp2 = scale * 1.4426950408889634
    slots = info_ref[0].astype(jnp.float32)
    by_block = slots.T
    ends = info_ref[1, pl.ds(64 * (chip // 32), 16), :].astype(jnp.float32)[0:1] * 64.0
    ends = ends + info_ref[2, pl.ds(64 * (chip // 32), 16), :].astype(jnp.float32)[0:1]
    stream_base = (64 * (chip // 32)).astype(jnp.float32)
    block_row = lax.broadcasted_iota(jnp.int32, (block, block), 0).astype(jnp.float32)
    key_pos[...] = by_block + 128.0 * (block_row - stream_base)
    lane = lax.broadcasted_iota(jnp.int32, (block, block), 1)
    starts = []
    for par in range(2):
        slot = jnp.sum(jnp.where(lane == 2 * chip + par, slots, 0.0), axis=1, keepdims=True)
        pos = slot + 128.0 * ((2 * chip + par).astype(jnp.float32) - stream_base)
        start = jnp.max(jnp.where(ends <= pos, ends, 0.0), axis=1, keepdims=True)
        starts.append(start)
        bound[0, par * block : (par + 1) * block, :] = jnp.broadcast_to(pos, (block, block))
        bound[1, par * block : (par + 1) * block, :] = jnp.broadcast_to(start, (block, block))
    low = jnp.min(starts[0]).astype(jnp.int32) >> 8
    low = low - (chip % 32 - (window - 1))
    top[...] = jnp.full(top.shape, masked_score, jnp.float32)
    total[...] = jnp.zeros(total.shape, jnp.float32)
    acc[...] = jnp.zeros(acc.shape, jnp.float32)

    @pl.loop(0, low)
    def _(m):
        dmine_ref[2 * m] = jnp.zeros((block, head), jnp.float32)
        dmine_ref[2 * m + 1] = jnp.zeros((block, head), jnp.float32)
        dother_ref[2 * m] = jnp.zeros((block, head), jnp.bfloat16)
        dother_ref[2 * m + 1] = jnp.zeros((block, head), jnp.bfloat16)

    def pair(m, half):
        return jnp.concatenate([mine_ref[2 * m + half], other_ref[2 * m + half]], axis=0)

    @pl.loop(low, window)
    def _(m):
        keys = pair(m, 0)
        bias = []
        for par in (core, 1 - core):
            kp = key_pos[pl.ds(first + 2 * m + par, 1), :]
            bias.append(jnp.where((kp <= bound[0]) & (kp >= bound[1]), 0.0, masked_score))
        bias = jnp.concatenate(bias, axis=1)
        for h in range(4):
            s = nt(qg_ref[h * 256 : (h + 1) * 256, :], keys) + bias
            scores[m, h] = s
            top[h] = jnp.maximum(top[h], jnp.maximum(s[:, :block], s[:, block:]))

    for h in range(4):
        peak = jnp.max(top[h], axis=1, keepdims=True)
        top[h] = jnp.broadcast_to(peak * to_exp2, (256, block))

    @pl.loop(low, window)
    def _(m):
        values = pair(m, 1)
        for h in range(4):
            peak = top[h]
            p = jnp.exp2(scores[m, h] * to_exp2 - jnp.concatenate([peak, peak], axis=1))
            total[h] = total[h] + (p[:, :block] + p[:, block:])
            half = p.astype(jnp.bfloat16)
            weights[m, h] = half
            acc[h] = acc[h] + jnp.dot(half, values, preferred_element_type=jnp.float32)

    for h in range(4):
        inv = 1.0 / jnp.sum(total[h], axis=1, keepdims=True)
        o = (acc[h] * inv).astype(jnp.bfloat16)
        out_ref[h * 256 : (h + 1) * 256, :] = o
        g = qg_ref[1024 + h * 256 : 1024 + (h + 1) * 256, :].astype(jnp.float32)
        q = qg_ref[h * 256 : (h + 1) * 256, :].astype(jnp.float32)
        d = jnp.sum(g * o.astype(jnp.float32), axis=1, keepdims=True)
        dot[h] = jnp.broadcast_to(d, (256, block))
        gs[h] = (g * inv).astype(jnp.bfloat16)
        qs[h] = (q * (inv * scale)).astype(jnp.bfloat16)
        total[h] = jnp.broadcast_to(inv * scale, (256, block))
        acc[h] = jnp.zeros((256, head), jnp.float32)

    @pl.loop(low, window)
    def _(m):
        keys = pair(m, 0)
        values = pair(m, 1)
        dk = jnp.zeros((256, head), jnp.float32)
        dv = jnp.zeros((256, head), jnp.float32)
        for h in range(4):
            gw = nt(qg_ref[1024 + h * 256 : 1024 + (h + 1) * 256, :], values)
            d = dot[h]
            p = weights[m, h]
            ds = (p.astype(jnp.float32) * (gw - jnp.concatenate([d, d], axis=1))).astype(jnp.bfloat16)
            acc[h] = acc[h] + jnp.dot(ds, keys, preferred_element_type=jnp.float32)
            dk = dk + tn(ds, qs[h])
            dv = dv + tn(p, gs[h])
        dmine_ref[2 * m] = dk[:block]
        dmine_ref[2 * m + 1] = dv[:block]
        dother_ref[2 * m] = dk[block:].astype(jnp.bfloat16)
        dother_ref[2 * m + 1] = dv[block:].astype(jnp.bfloat16)

    for h in range(4):
        dq_ref[h * 256 : (h + 1) * 256, :] = (acc[h] * total[h]).astype(jnp.bfloat16)


def vmem(n):
    return [pl.BlockSpec(memory_space=pltpu.VMEM)] * n


def smem():
    return pl.BlockSpec(memory_space=pltpu.SMEM)


params = pltpu.CompilerParams(vmem_limit_bytes=vmem_bytes)


def swap(x):
    return lax.ppermute(x, "dp", [(0, 1), (1, 0)])


def exchange(x):
    return lax.all_to_all(x, ("dp", "ctx"), split_axis=0, concat_axis=0, tiled=True)


def on_device(queries, keys_values, grad_out, placement, doc_lengths):
    bf16, f32 = jnp.bfloat16, jnp.float32
    place = placement.reshape(1, block)
    sent = pl.pallas_call(
        pack_kernel,
        out_shape=jax.ShapeDtypeStruct((128, send_rows, head), bf16),
        in_specs=vmem(1) + [smem()] + vmem(3),
        out_specs=vmem(1)[0],
        compiler_params=params,
        name="pack",
    )(place, doc_lengths, queries, keys_values, grad_out)
    got = exchange(sent).transpose(1, 0, 2)
    mine = got[:kv_rows]
    info = got[kv_rows:head_rows]
    qg = got[head_rows:].reshape(2, 4, 2, block, head).reshape(2048, head)
    other = swap(mine)
    where = jnp.stack([lax.axis_index("dp"), lax.axis_index("ctx")]).astype(jnp.int32)
    dmine, dother, out, dq = pl.pallas_call(
        attention_kernel,
        out_shape=(
            jax.ShapeDtypeStruct((kv_rows, block, head), f32),
            jax.ShapeDtypeStruct((kv_rows, block, head), bf16),
            jax.ShapeDtypeStruct((1024, head), bf16),
            jax.ShapeDtypeStruct((1024, head), bf16),
        ),
        in_specs=[smem()] + vmem(4),
        out_specs=tuple(vmem(4)),
        scratch_shapes=[
            pltpu.VMEM((window, 4, 256, 256), f32),
            pltpu.VMEM((window, 4, 256, 256), bf16),
            pltpu.VMEM((4, 256, block), f32),
            pltpu.VMEM((4, 256, block), f32),
            pltpu.VMEM((4, 256, head), f32),
            pltpu.VMEM((4, 256, block), f32),
            pltpu.VMEM((4, 256, head), bf16),
            pltpu.VMEM((4, 256, head), bf16),
            pltpu.VMEM((block, block), f32),
            pltpu.VMEM((2, 256, block), f32),
        ],
        compiler_params=params,
        name="attention",
    )(where, mine, other, info, qg)
    terms = (dmine + swap(dother).astype(f32)).astype(bf16)
    back = jnp.concatenate(
        [
            terms,
            jnp.zeros((head_rows - kv_rows, block, head), bf16),
            out.reshape(8, block, head),
            dq.reshape(8, block, head),
        ],
        axis=0,
    ).transpose(1, 0, 2)
    returned = exchange(back)
    r = np.arange(group * head_rows)
    i, r = r // head_rows, r % head_rows
    code = np.where(r < kv_rows, 2 * i + (r // 2) * 2 + (r % 2) * other_half, nothing)
    code = jnp.asarray(np.tile(code[None], (8, 1)).astype(np.int32))
    return pl.pallas_call(
        unpack_kernel,
        out_shape=(
            jax.ShapeDtypeStruct((block, 8 * head), bf16),
            jax.ShapeDtypeStruct((block, 8 * head), bf16),
            jax.ShapeDtypeStruct((block, 2 * head), bf16),
        ),
        in_specs=vmem(3),
        out_specs=tuple(vmem(3)),
        compiler_params=params,
        name="unpack",
    )(place, code, returned)


def solution(mesh):
    rows = P(("dp", "ctx"), None)
    return jax.shard_map(
        on_device,
        mesh=mesh,
        in_specs=(rows, rows, rows, P(("dp", "ctx")), P("dp", None)),
        out_specs=(rows, rows, rows),
        check_vma=False,
    )
```

```python
import jax
import jax.numpy as jnp
from jax import lax
from jax.experimental import pallas as pl
from jax.experimental.pallas import tpu as pltpu
from jax.sharding import PartitionSpec as P

block = 128
head = 128
entries = 36
pairs = entries // 2
kv_rows = 2 * pairs
head_rows = 40
send_rows = 56
group = 16
other_half = 1000
nothing = -100000
masked_score = -1e30
far = 1e9
vmem_bytes = 60 * 1024 * 1024


def one_hot(mask):
    return jnp.where(mask, 1.0, 0.0).astype(jnp.bfloat16)


def down(line):
    return jnp.broadcast_to(line.astype(jnp.float32), (block, block)).T


def stream_length(core, mine_ref, other_ref, stream, i):
    return jnp.where(core == stream, mine_ref[0, i], other_ref[0, i])


def make_plan(core, mine_ref, other_ref):
    lane = lax.broadcasted_iota(jnp.int32, (1, block), 1)
    pos = (lane & 63) * block
    start = jnp.zeros((1, block), jnp.int32)
    end0, end1 = jnp.int32(0), jnp.int32(0)
    for i in range(16):
        end0 = end0 + stream_length(core, mine_ref, other_ref, 0, i)
        end1 = end1 + stream_length(core, mine_ref, other_ref, 1, i)
        end = jnp.where(lane < 64, end0, end1)
        start = jnp.where(end <= pos, end, start)
    count = (lane & 63) - (start >> 7) + 1
    key = count * 64 + (lane & 63)
    row = lax.broadcasted_iota(jnp.int32, (block, block), 0)
    col = lax.broadcasted_iota(jnp.int32, (block, block), 1)
    above = (down(key) > key.astype(jnp.float32)) & ((row >> 6) == (col >> 6))
    rank = jnp.sum(jnp.where(above, 1.0, 0.0), axis=0, keepdims=True).astype(jnp.int32)
    seat = jnp.where(rank < 32, rank, 63 - rank) + 32 * (lane >> 6) + jnp.where(rank < 32, 0, 64)
    here = down(seat) == col.astype(jnp.float32)
    block_line = jnp.sum(jnp.where(here, row.astype(jnp.float32), 0.0), axis=0, keepdims=True)
    count_line = jnp.sum(jnp.where(here, down(count), 0.0), axis=0, keepdims=True)
    return block_line, count_line


def pack_kernel(core_ref, mine_ref, other_ref, place_ref, q_ref, kv_ref, g_ref, out_ref, plan_ref):
    block_line, count_line = make_plan(core_ref[0], mine_ref, other_ref)
    row8 = lax.broadcasted_iota(jnp.int32, (8, block), 0)
    plan_ref[...] = jnp.where(row8 == 0, block_line, jnp.where(row8 == 1, count_line, 0.0))
    block_down = down(block_line).astype(jnp.int32)
    count_down = down(count_line).astype(jnp.int32)
    rows = place_ref[...] >> 7
    lane = lax.broadcasted_iota(jnp.int32, (block, block), 1)
    slots_down = down(place_ref[...] & (block - 1))
    slot_line = jnp.sum(jnp.where(down(rows) == lane.astype(jnp.float32), slots_down, 0.0), axis=0, keepdims=True)
    extra = jnp.where(row8 == kv_rows % 8, slot_line, 0.0)
    kv = jnp.concatenate([kv_ref[:, :head], kv_ref[:, head:]], axis=0)
    r = lax.broadcasted_iota(jnp.int32, (group, head_rows, block), 1)
    half = (r & 1) * other_half
    for t in range(0, 128, group):
        core, chip = t // 64, t % 64

        def spread(x):
            return jnp.broadcast_to(x[:, None, :], (group, head_rows, block))

        first = block_down[chip : chip + group]
        first_count = count_down[chip : chip + group]
        second = block_down[64 + chip : 64 + chip + group]
        second_count = count_down[64 + chip : 64 + chip + group]
        entry = (r & -2) + core
        code = jnp.where(
            entry < spread(first_count),
            entry + spread(first - first_count + 1),
            jnp.where(entry >= spread(entries - second_count), entry + spread(second - (entries - 1)), nothing),
        )
        code = (jnp.where(r < kv_rows, code, nothing) + half).reshape(group * head_rows, block)
        pick = jnp.concatenate([one_hot(code == rows), one_hot(code == rows + other_half)], axis=1)
        got = jnp.dot(pick, kv, preferred_element_type=jnp.float32).reshape(group, head_rows, head)
        tail = got[:, head_rows - 8 :, :] + extra[None]
        got = jnp.concatenate([got[:, : head_rows - 8, :], tail], axis=1)
        out_ref[t : t + group, :head_rows, :] = got.astype(jnp.bfloat16)
    j = lax.broadcasted_iota(jnp.int32, (group, 8, block), 1)
    both = []
    for core in range(2):
        heads = [slice((4 * core + h) * head, (4 * core + h + 1) * head) for h in range(4)]
        both.append(jnp.concatenate([jnp.concatenate([q_ref[:, at], g_ref[:, at]], axis=1) for at in heads], axis=0))
    for c in range(0, 64, group):
        first = jnp.broadcast_to(block_down[c : c + group][:, None, :], (group, 8, block))
        second = jnp.broadcast_to(block_down[64 + c : 64 + c + group][:, None, :], (group, 8, block))
        mine = jnp.where(j < 4, first, second) == rows[None]
        pick = jnp.concatenate(
            [one_hot(mine & ((j & 3) == h)).reshape(group * 8, block) for h in range(4)], axis=1
        )
        for core in range(2):
            got = jnp.dot(pick, both[core], preferred_element_type=jnp.float32).astype(jnp.bfloat16)
            t = core * 64 + c
            out_ref[t : t + group, head_rows : head_rows + 8, :] = got[:, :head].reshape(group, 8, head)
            out_ref[t : t + group, head_rows + 8 :, :] = got[:, head:].reshape(group, 8, head)


def spread_lanes(plan, width):
    chip = lax.broadcasted_iota(jnp.int32, (block, 64 * width), 0) * width
    lane = lax.broadcasted_iota(jnp.int32, (block, 64 * width), 1)
    return jnp.dot(plan, one_hot((lane >= chip) & (lane < chip + width)), preferred_element_type=jnp.float32)


def unpack_kernel(place_ref, plan_ref, got_ref, out_ref, dq_ref, dkv_ref):
    rows_down = down(place_ref[...] >> 7)
    plan = plan_ref[...]
    lane = lax.broadcasted_iota(jnp.int32, (8, block), 1)
    lines = [plan[0:1], plan[1:2]]
    lines = lines + [pltpu.roll(plan, 64, 1)[i : i + 1] for i in range(2)]
    lines.append(lane[0:1].astype(jnp.float32))
    stacked = jnp.zeros((16, block), jnp.float32)
    row = lax.broadcasted_iota(jnp.int32, (16, block), 0)
    for i, line in enumerate(lines):
        stacked = jnp.where((row == i) & (lane[0:1] < 64), line, stacked)
    stacked = stacked.astype(jnp.bfloat16)
    wide = spread_lanes(stacked, head_rows)
    first, first_count, second, second_count, chip = [wide[i : i + 1] for i in range(5)]
    r = lax.broadcasted_iota(jnp.int32, (1, 64 * head_rows), 1) - head_rows * chip.astype(jnp.int32)
    sums = [jnp.zeros((block, head), jnp.float32), jnp.zeros((block, head), jnp.float32)]
    rows_wide = jnp.concatenate([rows_down] * (64 * head_rows // block), axis=1)
    for core in range(2):
        entry = ((r & -2) + core).astype(jnp.float32)
        code = jnp.where(
            entry < first_count,
            entry + (first - first_count + 1),
            jnp.where(entry >= entries - second_count, entry + (second - (entries - 1)), float(nothing)),
        )
        code = jnp.where(r < kv_rows, code, float(nothing))
        terms = got_ref[core * 64 : core * 64 + 64, :head_rows, :].reshape(64 * head_rows, head)
        for half in range(2):
            pick = one_hot(jnp.where((r & 1) == half, code, float(nothing)) == rows_wide)
            sums[half] = sums[half] + jnp.dot(pick, terms, preferred_element_type=jnp.float32)
    dkv_ref[...] = jnp.concatenate(sums, axis=1).astype(jnp.bfloat16)
    wide = spread_lanes(stacked, 8)
    j = lax.broadcasted_iota(jnp.int32, (1, 512), 1) & 7
    code = jnp.where(j < 4, wide[0:1], wide[2:3])
    rows_wide = jnp.concatenate([rows_down] * 4, axis=1)
    picks = [one_hot(jnp.where((j & 3) == h, code, float(nothing)) == rows_wide) for h in range(4)]
    for core in range(2):
        both = jnp.concatenate(
            [
                got_ref[core * 64 : core * 64 + 64, head_rows : head_rows + 8, :].reshape(512, head),
                got_ref[core * 64 : core * 64 + 64, head_rows + 8 :, :].reshape(512, head),
            ],
            axis=1,
        )
        for h in range(4):
            got = jnp.dot(picks[h], both, preferred_element_type=jnp.float32).astype(jnp.bfloat16)
            at = (4 * core + h) * head
            out_ref[:, at : at + head] = got[:, :head]
            dq_ref[:, at : at + head] = got[:, head:]


def nt(a, b):
    return lax.dot_general(a, b, (((1,), (1,)), ((), ())), preferred_element_type=jnp.float32)


def tn(a, b):
    return lax.dot_general(a, b, (((0,), (0,)), ((), ())), preferred_element_type=jnp.float32)


def attention_kernel(
    where_ref, mine_len, other_len, plan_ref, mine_ref, other_ref, info_ref, qg_ref,
    dmine_ref, dother_ref, out_ref, dq_ref,
    scores, weights, top, total, acc, dot, qs, gs, key_pos, bound,
):
    core = where_ref[0]
    chip = where_ref[1]
    stream = chip // 32
    scale = head ** (-0.5)
    to_exp2 = scale * 1.4426950408889634
    slots = info_ref[0].astype(jnp.float32)
    stream_base = (64 * stream).astype(jnp.float32)
    block_row = lax.broadcasted_iota(jnp.int32, (block, block), 0).astype(jnp.float32)
    key_pos[...] = slots.T + 128.0 * (block_row - stream_base)
    lane = lax.broadcasted_iota(jnp.int32, (block, block), 1)
    lane8 = lax.broadcasted_iota(jnp.int32, (8, block), 1)
    row8 = lax.broadcasted_iota(jnp.int32, (8, block), 0)
    plan = plan_ref[...]
    dmine_ref[...] = jnp.zeros(dmine_ref.shape, jnp.float32)
    dother_ref[...] = jnp.zeros(dother_ref.shape, jnp.float32)

    def planned(row, x):
        seat = (row8 == row) & (lane8 == chip + 64 * x)
        return jnp.sum(jnp.where(seat, plan, 0.0)).astype(jnp.int32)

    def pair(m, half):
        return jnp.concatenate([mine_ref[2 * m + half], other_ref[2 * m + half]], axis=0)

    for x in range(2):
        mine_block = planned(0, x)
        count = planned(1, x)
        if x == 0:
            begin, end = jnp.int32(0), (count + 1) >> 1
            entry_low, entry_high = jnp.int32(0), count
            base = mine_block - count + 1
        else:
            begin, end = (entries - count) >> 1, jnp.int32(pairs)
            entry_low, entry_high = entries - count, jnp.int32(entries)
            base = mine_block - (entries - 1)
        slot = jnp.sum(jnp.where(lane == mine_block, slots, 0.0), axis=1, keepdims=True)
        pos = jnp.broadcast_to(slot + 128.0 * (mine_block.astype(jnp.float32) - stream_base), (block, block))
        start = jnp.zeros((block, block), jnp.float32)
        doc_end = jnp.int32(0)
        for i in range(16):
            doc_end = doc_end + stream_length(core, mine_len, other_len, stream, i)
            f = doc_end.astype(jnp.float32)
            start = jnp.where(f <= pos, f, start)
        bound[0] = pos
        bound[1] = start
        top[...] = jnp.full(top.shape, masked_score, jnp.float32)
        total[...] = jnp.zeros(total.shape, jnp.float32)
        acc[...] = jnp.zeros(acc.shape, jnp.float32)
        q_at, g_at = x * 512, 1024 + x * 512

        @pl.loop(begin, end)
        def _(m):
            keys = pair(m, 0)
            bias = []
            for par in (core, 1 - core):
                entry = 2 * m + par
                valid = (entry >= entry_low) & (entry < entry_high)
                kp = key_pos[pl.ds(jnp.where(valid, base + entry, 0), 1), :]
                kp = jnp.where(valid, kp, far)
                bias.append(jnp.where((kp <= bound[0]) & (kp >= bound[1]), 0.0, masked_score))
            bias = jnp.concatenate(bias, axis=1)
            bias = jnp.concatenate([bias, bias], axis=0)
            for h in range(2):
                s = nt(qg_ref[q_at + h * 256 : q_at + (h + 1) * 256, :], keys) + bias
                scores[m, h] = s
                top[h] = jnp.maximum(top[h], jnp.maximum(s[:, :block], s[:, block:]))

        for h in range(2):
            peak = jnp.max(top[h], axis=1, keepdims=True)
            top[h] = jnp.broadcast_to(peak * to_exp2, (256, block))

        @pl.loop(begin, end)
        def _(m):
            values = pair(m, 1)
            for h in range(2):
                peak = top[h]
                p = jnp.exp2(scores[m, h] * to_exp2 - jnp.concatenate([peak, peak], axis=1))
                total[h] = total[h] + (p[:, :block] + p[:, block:])
                half = p.astype(jnp.bfloat16)
                weights[m, h] = half
                acc[h] = acc[h] + jnp.dot(half, values, preferred_element_type=jnp.float32)

        for h in range(2):
            inv = 1.0 / jnp.sum(total[h], axis=1, keepdims=True)
            o = (acc[h] * inv).astype(jnp.bfloat16)
            out_ref[q_at + h * 256 : q_at + (h + 1) * 256, :] = o
            g = qg_ref[g_at + h * 256 : g_at + (h + 1) * 256, :].astype(jnp.float32)
            q = qg_ref[q_at + h * 256 : q_at + (h + 1) * 256, :].astype(jnp.float32)
            d = jnp.sum(g * o.astype(jnp.float32), axis=1, keepdims=True)
            dot[h] = jnp.broadcast_to(d, (256, block))
            gs[h] = (g * inv).astype(jnp.bfloat16)
            qs[h] = (q * (inv * scale)).astype(jnp.bfloat16)
            total[h] = jnp.broadcast_to(inv * scale, (256, block))
            acc[h] = jnp.zeros((256, head), jnp.float32)

        @pl.loop(begin, end)
        def _(m):
            keys = pair(m, 0)
            values = pair(m, 1)
            dk = jnp.zeros((256, head), jnp.float32)
            dv = jnp.zeros((256, head), jnp.float32)
            for h in range(2):
                gw = nt(qg_ref[g_at + h * 256 : g_at + (h + 1) * 256, :], values)
                d = dot[h]
                p = weights[m, h]
                ds = (p.astype(jnp.float32) * (gw - jnp.concatenate([d, d], axis=1))).astype(jnp.bfloat16)
                acc[h] = acc[h] + jnp.dot(ds, keys, preferred_element_type=jnp.float32)
                dk = dk + tn(ds, qs[h])
                dv = dv + tn(p, gs[h])
            dmine_ref[2 * m] = dmine_ref[2 * m] + dk[:block]
            dmine_ref[2 * m + 1] = dmine_ref[2 * m + 1] + dv[:block]
            dother_ref[2 * m] = dother_ref[2 * m] + dk[block:]
            dother_ref[2 * m + 1] = dother_ref[2 * m + 1] + dv[block:]

        for h in range(2):
            dq_ref[q_at + h * 256 : q_at + (h + 1) * 256, :] = (acc[h] * total[h]).astype(jnp.bfloat16)


def vmem(n):
    return [pl.BlockSpec(memory_space=pltpu.VMEM)] * n


def smem():
    return pl.BlockSpec(memory_space=pltpu.SMEM)


params = pltpu.CompilerParams(vmem_limit_bytes=vmem_bytes)


def swap(x):
    return lax.ppermute(x, "dp", [(0, 1), (1, 0)])


def exchange(x):
    return lax.all_to_all(x, ("dp", "ctx"), split_axis=0, concat_axis=0, tiled=True)


def on_device(queries, keys_values, grad_out, placement, doc_lengths):
    bf16, f32 = jnp.bfloat16, jnp.float32
    place = placement.reshape(1, block)
    where = jnp.stack([lax.axis_index("dp"), lax.axis_index("ctx")]).astype(jnp.int32)
    other_lengths = swap(doc_lengths)
    sent, plan = pl.pallas_call(
        pack_kernel,
        out_shape=(
            jax.ShapeDtypeStruct((128, send_rows, head), bf16),
            jax.ShapeDtypeStruct((8, block), f32),
        ),
        in_specs=[smem()] * 3 + vmem(4),
        out_specs=tuple(vmem(2)),
        compiler_params=params,
        name="pack",
    )(where, doc_lengths, other_lengths, place, queries, keys_values, grad_out)
    got = exchange(sent).transpose(1, 0, 2)
    mine = got[:kv_rows]
    info = got[kv_rows:head_rows]
    qg = got[head_rows:].reshape(2048, head)
    other = swap(mine)
    dmine, dother, out, dq = pl.pallas_call(
        attention_kernel,
        out_shape=(
            jax.ShapeDtypeStruct((kv_rows, block, head), f32),
            jax.ShapeDtypeStruct((kv_rows, block, head), f32),
            jax.ShapeDtypeStruct((1024, head), bf16),
            jax.ShapeDtypeStruct((1024, head), bf16),
        ),
        in_specs=[smem()] * 3 + vmem(5),
        out_specs=tuple(vmem(4)),
        scratch_shapes=[
            pltpu.VMEM((pairs, 2, 256, 256), f32),
            pltpu.VMEM((pairs, 2, 256, 256), bf16),
            pltpu.VMEM((2, 256, block), f32),
            pltpu.VMEM((2, 256, block), f32),
            pltpu.VMEM((2, 256, head), f32),
            pltpu.VMEM((2, 256, block), f32),
            pltpu.VMEM((2, 256, head), bf16),
            pltpu.VMEM((2, 256, head), bf16),
            pltpu.VMEM((block, block), f32),
            pltpu.VMEM((2, block, block), f32),
        ],
        compiler_params=params,
        name="attention",
    )(where, doc_lengths, other_lengths, plan, mine, other, info, qg)
    terms = (dmine + swap(dother.astype(bf16)).astype(f32)).astype(bf16)
    back = jnp.concatenate(
        [
            terms,
            jnp.zeros((head_rows - kv_rows, block, head), bf16),
            out.reshape(8, block, head),
            dq.reshape(8, block, head),
        ],
        axis=0,
    ).transpose(1, 0, 2)
    returned = exchange(back)
    return pl.pallas_call(
        unpack_kernel,
        out_shape=(
            jax.ShapeDtypeStruct((block, 8 * head), bf16),
            jax.ShapeDtypeStruct((block, 8 * head), bf16),
            jax.ShapeDtypeStruct((block, 2 * head), bf16),
        ),
        in_specs=vmem(3),
        out_specs=tuple(vmem(3)),
        compiler_params=params,
        name="unpack",
    )(place, plan, returned)


def solution(mesh):
    rows = P(("dp", "ctx"), None)
    return jax.shard_map(
        on_device,
        mesh=mesh,
        in_specs=(rows, rows, rows, P(("dp", "ctx")), P("dp", None)),
        out_specs=(rows, rows, rows),
        check_vma=False,
    )
```

```python
import jax
import jax.numpy as jnp
from jax import lax
from jax.experimental import pallas as pl
from jax.experimental.pallas import tpu as pltpu
from jax.sharding import PartitionSpec as P

block = 128
head = 128
entries = 36
pairs = entries // 2
kv_rows = 2 * pairs
head_rows = 40
send_rows = 56
group = 16
other_half = 1000
nothing = -100000
masked_score = -1e30
far = 1e9
step = 3
mib = 1024 * 1024


def one_hot(mask):
    return jnp.where(mask, 1.0, 0.0).astype(jnp.bfloat16)


def down(line):
    return jnp.broadcast_to(line.astype(jnp.float32), (block, block)).T


def stream_length(core, mine_ref, other_ref, stream, i):
    return jnp.where(core == stream, mine_ref[0, i], other_ref[0, i])


def make_plan(core, mine_ref, other_ref):
    lane = lax.broadcasted_iota(jnp.int32, (1, block), 1)
    pos = (lane & 63) * block
    start = jnp.zeros((1, block), jnp.int32)
    end0, end1 = jnp.int32(0), jnp.int32(0)
    for i in range(16):
        end0 = end0 + stream_length(core, mine_ref, other_ref, 0, i)
        end1 = end1 + stream_length(core, mine_ref, other_ref, 1, i)
        end = jnp.where(lane < 64, end0, end1)
        start = jnp.where(end <= pos, end, start)
    count = (lane & 63) - (start >> 7) + 1
    key = count * 64 + (lane & 63)
    row = lax.broadcasted_iota(jnp.int32, (block, block), 0)
    col = lax.broadcasted_iota(jnp.int32, (block, block), 1)
    above = (down(key) > key.astype(jnp.float32)) & ((row >> 6) == (col >> 6))
    rank = jnp.sum(jnp.where(above, 1.0, 0.0), axis=0, keepdims=True).astype(jnp.int32)
    seat = jnp.where(rank < 32, rank, 63 - rank) + 32 * (lane >> 6) + jnp.where(rank < 32, 0, 64)
    here = down(seat) == col.astype(jnp.float32)
    block_line = jnp.sum(jnp.where(here, row.astype(jnp.float32), 0.0), axis=0, keepdims=True)
    count_line = jnp.sum(jnp.where(here, down(count), 0.0), axis=0, keepdims=True)
    return block_line, count_line


def pack_kernel(mine_ref, other_ref, place_ref, q_ref, kv_ref, g_ref, out_ref, plan_ref):
    block_line, count_line = make_plan(lax.axis_index("dp"), mine_ref, other_ref)
    row8 = lax.broadcasted_iota(jnp.int32, (8, block), 0)
    plan_ref[...] = jnp.where(row8 == 0, block_line, jnp.where(row8 == 1, count_line, 0.0))
    block_down = down(block_line).astype(jnp.int32)
    count_down = down(count_line).astype(jnp.int32)
    rows = place_ref[...] >> 7
    lane = lax.broadcasted_iota(jnp.int32, (block, block), 1)
    slots_down = down(place_ref[...] & (block - 1))
    slot_line = jnp.sum(jnp.where(down(rows) == lane.astype(jnp.float32), slots_down, 0.0), axis=0, keepdims=True)
    extra = jnp.where(row8 == kv_rows % 8, slot_line, 0.0)
    kv = jnp.concatenate([kv_ref[:, :head], kv_ref[:, head:]], axis=0)
    r = lax.broadcasted_iota(jnp.int32, (group, head_rows, block), 1)
    half = (r & 1) * other_half
    for t in range(0, 128, group):
        core, chip = t // 64, t % 64

        def spread(x):
            return jnp.broadcast_to(x[:, None, :], (group, head_rows, block))

        first = block_down[chip : chip + group]
        first_count = count_down[chip : chip + group]
        second = block_down[64 + chip : 64 + chip + group]
        second_count = count_down[64 + chip : 64 + chip + group]
        entry = (r & -2) + core
        code = jnp.where(
            entry < spread(first_count),
            entry + spread(first - first_count + 1),
            jnp.where(entry >= spread(entries - second_count), entry + spread(second - (entries - 1)), nothing),
        )
        code = (jnp.where(r < kv_rows, code, nothing) + half).reshape(group * head_rows, block)
        pick = jnp.concatenate([one_hot(code == rows), one_hot(code == rows + other_half)], axis=1)
        got = jnp.dot(pick, kv, preferred_element_type=jnp.float32).reshape(group, head_rows, head)
        tail = got[:, head_rows - 8 :, :] + extra[None]
        got = jnp.concatenate([got[:, : head_rows - 8, :], tail], axis=1)
        out_ref[t : t + group, :head_rows, :] = got.astype(jnp.bfloat16)
    j = lax.broadcasted_iota(jnp.int32, (group, 8, block), 1)
    both = []
    for core in range(2):
        heads = [slice((4 * core + h) * head, (4 * core + h + 1) * head) for h in range(4)]
        both.append(jnp.concatenate([jnp.concatenate([q_ref[:, at], g_ref[:, at]], axis=1) for at in heads], axis=0))
    for c in range(0, 64, group):
        first = jnp.broadcast_to(block_down[c : c + group][:, None, :], (group, 8, block))
        second = jnp.broadcast_to(block_down[64 + c : 64 + c + group][:, None, :], (group, 8, block))
        mine = jnp.where(j < 4, first, second) == rows[None]
        pick = jnp.concatenate(
            [one_hot(mine & ((j & 3) == h)).reshape(group * 8, block) for h in range(4)], axis=1
        )
        for core in range(2):
            got = jnp.dot(pick, both[core], preferred_element_type=jnp.float32).astype(jnp.bfloat16)
            t = core * 64 + c
            out_ref[t : t + group, head_rows : head_rows + 8, :] = got[:, :head].reshape(group, 8, head)
            out_ref[t : t + group, head_rows + 8 :, :] = got[:, head:].reshape(group, 8, head)


def spread_lanes(plan, width):
    chip = lax.broadcasted_iota(jnp.int32, (block, 64 * width), 0) * width
    lane = lax.broadcasted_iota(jnp.int32, (block, 64 * width), 1)
    return jnp.dot(plan, one_hot((lane >= chip) & (lane < chip + width)), preferred_element_type=jnp.float32)


def unpack_kernel(place_ref, plan_ref, got_ref, out_ref, dq_ref, dkv_ref):
    rows_down = down(place_ref[...] >> 7)
    plan = plan_ref[...]
    lane = lax.broadcasted_iota(jnp.int32, (8, block), 1)
    lines = [plan[0:1], plan[1:2]]
    lines = lines + [pltpu.roll(plan, 64, 1)[i : i + 1] for i in range(2)]
    lines.append(lane[0:1].astype(jnp.float32))
    stacked = jnp.zeros((16, block), jnp.float32)
    row = lax.broadcasted_iota(jnp.int32, (16, block), 0)
    for i, line in enumerate(lines):
        stacked = jnp.where((row == i) & (lane[0:1] < 64), line, stacked)
    stacked = stacked.astype(jnp.bfloat16)
    wide = spread_lanes(stacked, head_rows)
    first, first_count, second, second_count, chip = [wide[i : i + 1] for i in range(5)]
    r = lax.broadcasted_iota(jnp.int32, (1, 64 * head_rows), 1) - head_rows * chip.astype(jnp.int32)
    sums = [jnp.zeros((block, head), jnp.float32), jnp.zeros((block, head), jnp.float32)]
    rows_wide = jnp.concatenate([rows_down] * (64 * head_rows // block), axis=1)
    for core in range(2):
        entry = ((r & -2) + core).astype(jnp.float32)
        code = jnp.where(
            entry < first_count,
            entry + (first - first_count + 1),
            jnp.where(entry >= entries - second_count, entry + (second - (entries - 1)), float(nothing)),
        )
        code = jnp.where(r < kv_rows, code, float(nothing))
        terms = got_ref[core * 64 : core * 64 + 64, :head_rows, :].reshape(64 * head_rows, head)
        for half in range(2):
            pick = one_hot(jnp.where((r & 1) == half, code, float(nothing)) == rows_wide)
            sums[half] = sums[half] + jnp.dot(pick, terms, preferred_element_type=jnp.float32)
    dkv_ref[...] = jnp.concatenate(sums, axis=1).astype(jnp.bfloat16)
    wide = spread_lanes(stacked, 8)
    j = lax.broadcasted_iota(jnp.int32, (1, 512), 1) & 7
    code = jnp.where(j < 4, wide[0:1], wide[2:3])
    rows_wide = jnp.concatenate([rows_down] * 4, axis=1)
    picks = [one_hot(jnp.where((j & 3) == h, code, float(nothing)) == rows_wide) for h in range(4)]
    for core in range(2):
        both = jnp.concatenate(
            [
                got_ref[core * 64 : core * 64 + 64, head_rows : head_rows + 8, :].reshape(512, head),
                got_ref[core * 64 : core * 64 + 64, head_rows + 8 :, :].reshape(512, head),
            ],
            axis=1,
        )
        for h in range(4):
            got = jnp.dot(picks[h], both, preferred_element_type=jnp.float32).astype(jnp.bfloat16)
            at = (4 * core + h) * head
            out_ref[:, at : at + head] = got[:, :head]
            dq_ref[:, at : at + head] = got[:, head:]


def nt(a, b):
    return lax.dot_general(a, b, (((1,), (1,)), ((), ())), preferred_element_type=jnp.float32)


def tn(a, b):
    return lax.dot_general(a, b, (((0,), (0,)), ((), ())), preferred_element_type=jnp.float32)


def nn(a, b):
    return jnp.dot(a, b, preferred_element_type=jnp.float32)


def attention_kernel(
    mine_len, other_len, plan_ref, mine_ref, other_ref,
    dmine_ref, dother_ref, out_ref, dq_ref,
    kv, qg, scores, weights, top, total, acc, dot, qs, gs, key_pos, bound,
):
    core = lax.axis_index("dp")
    chip = lax.axis_index("ctx")
    stream = chip // 32
    scale = head ** (-0.5)
    to_exp2 = scale * 1.4426950408889634
    stream_base = (64 * stream).astype(jnp.float32)
    block_row = lax.broadcasted_iota(jnp.int32, (block, block), 0).astype(jnp.float32)
    lane8 = lax.broadcasted_iota(jnp.int32, (8, block), 1)
    row8 = lax.broadcasted_iota(jnp.int32, (8, block), 0)
    for side, ref in enumerate((mine_ref, other_ref)):
        for r in range(0, send_rows if side == 0 else head_rows, 8):
            rows = jnp.transpose(ref[:, r : r + 8, :], (1, 0, 2))
            if r >= head_rows:
                at = (r - head_rows) * block
                qg[at : at + 8 * block, :] = rows.reshape(8 * block, head)
                continue
            for i in range(0, min(8, kv_rows - r), 2):
                at = (r + i + side) * block
                kv[0, at : at + block, :] = rows[i]
                kv[1, at : at + block, :] = rows[i + 1]
            if side == 0 and r + 8 == head_rows:
                slots = rows[kv_rows - r].astype(jnp.float32)
                key_pos[...] = slots.T + 128.0 * (block_row - stream_base)
    plan = plan_ref[...]
    dmine_ref[...] = jnp.zeros(dmine_ref.shape, jnp.bfloat16)
    dother_ref[...] = jnp.zeros(dother_ref.shape, jnp.bfloat16)
    span = 256 * step

    def planned(row, x):
        seat = (row8 == row) & (lane8 == chip + 64 * x)
        return jnp.sum(jnp.where(seat, plan, 0.0)).astype(jnp.int32)

    def some(half, m):
        return kv[half, pl.ds(pl.multiple_of(m * span, span), span), :]

    def add(ref, i, x):
        ref[i] = (ref[i].astype(jnp.float32) + x).astype(jnp.bfloat16)

    for x in range(2):
        mine_block = planned(0, x)
        count = planned(1, x)
        if x == 0:
            begin, end = jnp.int32(0), (count + 2 * step - 1) // (2 * step)
            entry_low, entry_high = jnp.int32(0), count
            base = mine_block - count + 1
        else:
            begin, end = (entries - count) // (2 * step), jnp.int32(pairs // step)
            entry_low, entry_high = entries - count, jnp.int32(entries)
            base = mine_block - (entries - 1)
        pos = key_pos[pl.ds(mine_block, 1), :]
        start = jnp.zeros((1, block), jnp.float32)
        doc_end = jnp.int32(0)
        for i in range(16):
            doc_end = doc_end + stream_length(core, mine_len, other_len, stream, i)
            f = doc_end.astype(jnp.float32)
            start = jnp.where(f <= pos, f, start)
        bound[0:1] = pos
        bound[1:2] = start
        top[...] = jnp.full(top.shape, masked_score, jnp.float32)
        total[...] = jnp.zeros(total.shape, jnp.float32)
        acc[...] = jnp.zeros(acc.shape, jnp.float32)
        q_at, g_at = x * 512, 1024 + x * 512

        @pl.loop(begin, end)
        def _(m):
            keys = some(0, m)
            bias = []
            for u, par in [(u, par) for u in range(step) for par in (core, 1 - core)]:
                entry = 2 * (m * step + u) + par
                valid = (entry >= entry_low) & (entry < entry_high)
                kp = key_pos[pl.ds(jnp.where(valid, base + entry, 0), 1), :]
                kp = jnp.broadcast_to(jnp.where(valid, kp, far), (block, block)).T
                bias.append(jnp.where((kp <= bound[0:1]) & (kp >= bound[1:2]), 0.0, masked_score))
            bias = jnp.concatenate(bias, axis=0)
            bias = jnp.concatenate([bias] * 4, axis=1)
            s = nt(keys, qg[q_at : q_at + 512, :]) + bias
            scores[m] = s
            top[...] = jnp.maximum(top[...], jnp.max(s.reshape(span // 8, 8, 512), axis=0))

        top[...] = jnp.broadcast_to(jnp.max(top[...], axis=0, keepdims=True) * to_exp2, top.shape)

        @pl.loop(begin, end)
        def _(m):
            p = jnp.exp2(scores[m] * to_exp2 - top[0:1])
            total[...] = total[...] + jnp.sum(p.reshape(span // 8, 8, 512), axis=0)
            half = p.astype(jnp.bfloat16)
            weights[m] = half
            acc[...] = acc[...] + tn(some(1, m), half)

        inv = 1.0 / jnp.sum(total[...], axis=0, keepdims=True)
        for h in range(4):
            at = slice(h * block, (h + 1) * block)
            q_rows = slice(q_at + h * block, q_at + (h + 1) * block)
            inv_down = jnp.broadcast_to(inv[:, at], (block, block)).T
            o = (acc[:, at].T * inv_down).astype(jnp.bfloat16)
            out_ref[q_rows, :] = o
            g = qg[g_at + h * block : g_at + (h + 1) * block, :].astype(jnp.float32)
            q = qg[q_rows, :].astype(jnp.float32)
            d = jnp.sum(g * o.astype(jnp.float32), axis=1, keepdims=True)
            dot[:, at] = jnp.broadcast_to(d, (block, block)).T[:8]
            gs[at] = (g * inv_down).astype(jnp.bfloat16)
            qs[at] = (q * (inv_down * scale)).astype(jnp.bfloat16)
        total[...] = jnp.broadcast_to(inv * scale, total.shape)
        acc[...] = jnp.zeros(acc.shape, jnp.float32)

        @pl.loop(begin, end)
        def _(m):
            gw = nt(some(1, m), qg[g_at : g_at + 512, :])
            p = weights[m]
            ds = (p.astype(jnp.float32) * (gw - dot[0:1])).astype(jnp.bfloat16)
            acc[...] = acc[...] + tn(some(0, m), ds)
            dk = nn(ds, qs[...])
            dv = nn(p, gs[...])
            for u in range(step):
                i = 2 * (m * step + u)
                add(dmine_ref, i, dk[u * 256 : u * 256 + block])
                add(dmine_ref, i + 1, dv[u * 256 : u * 256 + block])
                add(dother_ref, i, dk[u * 256 + block : (u + 1) * 256])
                add(dother_ref, i + 1, dv[u * 256 + block : (u + 1) * 256])

        for h in range(4):
            at = slice(h * block, (h + 1) * block)
            dq_ref[q_at + h * block : q_at + (h + 1) * block, :] = (acc[:, at] * total[0:1, at]).T.astype(jnp.bfloat16)


def join_kernel(mine_ref, other_ref, out_ref, dq_ref, back_ref):
    def put(r, rows):
        back_ref[:, r : r + 8, :] = jnp.transpose(rows, (1, 0, 2))

    for r in range(0, head_rows, 8):
        n = min(8, kv_rows - r)
        rows = mine_ref[r : r + n].astype(jnp.float32) + other_ref[r : r + n].astype(jnp.float32)
        rows = rows.astype(jnp.bfloat16)
        if n < 8:
            rows = jnp.concatenate([rows, jnp.zeros((8 - n, block, head), jnp.bfloat16)], axis=0)
        put(r, rows)
    put(head_rows, out_ref[...].reshape(8, block, head))
    put(head_rows + 8, dq_ref[...].reshape(8, block, head))


def vmem(n):
    return [pl.BlockSpec(memory_space=pltpu.VMEM)] * n


def smem():
    return pl.BlockSpec(memory_space=pltpu.SMEM)


def params(size):
    return pltpu.CompilerParams(vmem_limit_bytes=size * mib)


def swap(x):
    return lax.ppermute(x, "dp", [(0, 1), (1, 0)])


def exchange(x):
    return lax.all_to_all(x, ("dp", "ctx"), split_axis=0, concat_axis=0, tiled=True)


def on_device(queries, keys_values, grad_out, placement, doc_lengths):
    bf16, f32 = jnp.bfloat16, jnp.float32
    place = placement.reshape(1, block)
    other_lengths = swap(doc_lengths)
    sent, plan = pl.pallas_call(
        pack_kernel,
        out_shape=(
            jax.ShapeDtypeStruct((128, send_rows, head), bf16),
            jax.ShapeDtypeStruct((8, block), f32),
        ),
        in_specs=[smem()] * 2 + vmem(4),
        out_specs=tuple(vmem(2)),
        compiler_params=params(24),
        name="pack",
    )(doc_lengths, other_lengths, place, queries, keys_values, grad_out)
    got = exchange(sent)
    dmine, dother, out, dq = pl.pallas_call(
        attention_kernel,
        out_shape=(
            jax.ShapeDtypeStruct((kv_rows, block, head), bf16),
            jax.ShapeDtypeStruct((kv_rows, block, head), bf16),
            jax.ShapeDtypeStruct((1024, head), bf16),
            jax.ShapeDtypeStruct((1024, head), bf16),
        ),
        in_specs=[smem()] * 2 + vmem(3),
        out_specs=tuple(vmem(4)),
        scratch_shapes=[
            pltpu.VMEM((2, entries * block, head), bf16),
            pltpu.VMEM((2048, head), bf16),
            pltpu.VMEM((pairs // step, 256 * step, 512), f32),
            pltpu.VMEM((pairs // step, 256 * step, 512), bf16),
            pltpu.VMEM((8, 512), f32),
            pltpu.VMEM((8, 512), f32),
            pltpu.VMEM((head, 512), f32),
            pltpu.VMEM((8, 512), f32),
            pltpu.VMEM((512, head), bf16),
            pltpu.VMEM((512, head), bf16),
            pltpu.VMEM((block, block), f32),
            pltpu.VMEM((8, block), f32),
        ],
        compiler_params=params(48),
        name="attention",
    )(doc_lengths, other_lengths, plan, got, swap(got))
    back = pl.pallas_call(
        join_kernel,
        out_shape=jax.ShapeDtypeStruct((128, send_rows, head), bf16),
        in_specs=vmem(4),
        out_specs=vmem(1)[0],
        compiler_params=params(24),
        name="join",
    )(dmine, swap(dother), out, dq)
    returned = exchange(back)
    return pl.pallas_call(
        unpack_kernel,
        out_shape=(
            jax.ShapeDtypeStruct((block, 8 * head), bf16),
            jax.ShapeDtypeStruct((block, 8 * head), bf16),
            jax.ShapeDtypeStruct((block, 2 * head), bf16),
        ),
        in_specs=vmem(3),
        out_specs=tuple(vmem(3)),
        compiler_params=params(24),
        name="unpack",
    )(place, plan, returned)


def solution(mesh):
    rows = P(("dp", "ctx"), None)
    return jax.shard_map(
        on_device,
        mesh=mesh,
        in_specs=(rows, rows, rows, P(("dp", "ctx")), P("dp", None)),
        out_specs=(rows, rows, rows),
        check_vma=False,
    )
```

```python
import jax
import jax.numpy as jnp
from jax import lax
from jax.experimental import pallas as pl
from jax.experimental.pallas import tpu as pltpu
from jax.sharding import PartitionSpec as P

block = 128
head = 128
entries = 36
pairs = entries // 2
kv_rows = 2 * pairs
head_rows = 40
send_rows = 56
group = 16
other_half = 1000
nothing = -100000
masked_score = -1e30
far = 1e9
step = 3
mib = 1024 * 1024


def one_hot(mask):
    return jnp.where(mask, 1.0, 0.0).astype(jnp.bfloat16)


def down(line):
    return jnp.broadcast_to(line.astype(jnp.float32), (block, block)).T


def stream_length(core, mine_ref, other_ref, stream, i):
    return jnp.where(core == stream, mine_ref[0, i], other_ref[0, i])


def make_plan(core, mine_ref, other_ref):
    lane = lax.broadcasted_iota(jnp.int32, (1, block), 1)
    pos = (lane & 63) * block
    start = jnp.zeros((1, block), jnp.int32)
    end0, end1 = jnp.int32(0), jnp.int32(0)
    for i in range(16):
        end0 = end0 + stream_length(core, mine_ref, other_ref, 0, i)
        end1 = end1 + stream_length(core, mine_ref, other_ref, 1, i)
        end = jnp.where(lane < 64, end0, end1)
        start = jnp.where(end <= pos, end, start)
    count = (lane & 63) - (start >> 7) + 1
    key = count * 64 + (lane & 63)
    row = lax.broadcasted_iota(jnp.int32, (block, block), 0)
    col = lax.broadcasted_iota(jnp.int32, (block, block), 1)
    above = (down(key) > key.astype(jnp.float32)) & ((row >> 6) == (col >> 6))
    rank = jnp.sum(jnp.where(above, 1.0, 0.0), axis=0, keepdims=True).astype(jnp.int32)
    seat = jnp.where(rank < 32, rank, 63 - rank) + 32 * (lane >> 6) + jnp.where(rank < 32, 0, 64)
    here = down(seat) == col.astype(jnp.float32)
    block_line = jnp.sum(jnp.where(here, row.astype(jnp.float32), 0.0), axis=0, keepdims=True)
    count_line = jnp.sum(jnp.where(here, down(count), 0.0), axis=0, keepdims=True)
    return block_line, count_line


def pack_kernel(
    mine_hbm, other_hbm, place_hbm, q_hbm, kv_hbm, g_hbm, out_hbm, plan_ref,
    mine_ref, other_ref, place_ref, q_ref, kv_ref, g_ref, out_ref, sems,
):
    moves = [
        pltpu.make_async_copy(src, dst, sems.at[i])
        for i, (src, dst) in enumerate(
            [
                (mine_hbm, mine_ref),
                (other_hbm, other_ref),
                (place_hbm, place_ref),
                (kv_hbm, kv_ref),
                (q_hbm, q_ref),
                (g_hbm, g_ref),
            ]
        )
    ]
    for move in moves:
        move.start()
    for move in moves[:3]:
        move.wait()
    block_line, count_line = make_plan(lax.axis_index("dp"), mine_ref, other_ref)
    row8 = lax.broadcasted_iota(jnp.int32, (8, block), 0)
    plan_ref[...] = jnp.where(row8 == 0, block_line, jnp.where(row8 == 1, count_line, 0.0))
    block_down = down(block_line).astype(jnp.int32)
    count_down = down(count_line).astype(jnp.int32)
    rows = place_ref[...] >> 7
    lane = lax.broadcasted_iota(jnp.int32, (block, block), 1)
    slots_down = down(place_ref[...] & (block - 1))
    slot_line = jnp.sum(jnp.where(down(rows) == lane.astype(jnp.float32), slots_down, 0.0), axis=0, keepdims=True)
    extra = jnp.where(row8 == kv_rows % 8, slot_line, 0.0)
    moves[3].wait()
    kv = jnp.concatenate([kv_ref[:, :head], kv_ref[:, head:]], axis=0)
    r = lax.broadcasted_iota(jnp.int32, (group, head_rows, block), 1)
    half = (r & 1) * other_half
    j = lax.broadcasted_iota(jnp.int32, (group, 8, block), 1)
    moves[4].wait()
    moves[5].wait()
    both = []
    for core in range(2):
        heads = [slice((4 * core + h) * head, (4 * core + h + 1) * head) for h in range(4)]
        both.append(jnp.concatenate([jnp.concatenate([q_ref[:, at], g_ref[:, at]], axis=1) for at in heads], axis=0))

    def spread(x, n):
        return jnp.broadcast_to(x[:, None, :], (group, n, block))

    sends = []
    for chip in range(0, 64, group):
        first = block_down[chip : chip + group]
        first_count = count_down[chip : chip + group]
        second = block_down[64 + chip : 64 + chip + group]
        second_count = count_down[64 + chip : 64 + chip + group]
        wanted = jnp.where(j < 4, spread(first, 8), spread(second, 8)) == rows[None]
        heads = jnp.concatenate(
            [one_hot(wanted & ((j & 3) == h)).reshape(group * 8, block) for h in range(4)], axis=1
        )
        for core in range(2):
            t = core * 64 + chip
            entry = (r & -2) + core
            code = jnp.where(
                entry < spread(first_count, head_rows),
                entry + spread(first - first_count + 1, head_rows),
                jnp.where(
                    entry >= spread(entries - second_count, head_rows),
                    entry + spread(second - (entries - 1), head_rows),
                    nothing,
                ),
            )
            code = (jnp.where(r < kv_rows, code, nothing) + half).reshape(group * head_rows, block)
            pick = jnp.concatenate([one_hot(code == rows), one_hot(code == rows + other_half)], axis=1)
            got = jnp.dot(pick, kv, preferred_element_type=jnp.float32).reshape(group, head_rows, head)
            tail = got[:, head_rows - 8 :, :] + extra[None]
            got = jnp.concatenate([got[:, : head_rows - 8, :], tail], axis=1)
            out_ref[t : t + group, :head_rows, :] = got.astype(jnp.bfloat16)
            got = jnp.dot(heads, both[core], preferred_element_type=jnp.float32).astype(jnp.bfloat16)
            out_ref[t : t + group, head_rows : head_rows + 8, :] = got[:, :head].reshape(group, 8, head)
            out_ref[t : t + group, head_rows + 8 :, :] = got[:, head:].reshape(group, 8, head)
            at = pl.ds(t, group)
            sends.append(pltpu.make_async_copy(out_ref.at[at], out_hbm.at[at], sems.at[6 + len(sends)]))
            sends[-1].start()
    for send in sends:
        send.wait()


def spread_lanes(plan, width):
    chip = lax.broadcasted_iota(jnp.int32, (block, 64 * width), 0) * width
    lane = lax.broadcasted_iota(jnp.int32, (block, 64 * width), 1)
    return jnp.dot(plan, one_hot((lane >= chip) & (lane < chip + width)), preferred_element_type=jnp.float32)


def unpack_kernel(
    place_ref, plan_ref, got_ref, out_hbm, dq_hbm, dkv_hbm, out_ref, dq_ref, dkv_ref, sems
):
    moves = [
        pltpu.make_async_copy(src, dst, sems.at[i])
        for i, (src, dst) in enumerate([(out_ref, out_hbm), (dq_ref, dq_hbm), (dkv_ref, dkv_hbm)])
    ]
    rows_down = down(place_ref[...] >> 7)
    plan = plan_ref[...]
    lane = lax.broadcasted_iota(jnp.int32, (8, block), 1)
    lines = [plan[0:1], plan[1:2]]
    lines = lines + [pltpu.roll(plan, 64, 1)[i : i + 1] for i in range(2)]
    lines.append(lane[0:1].astype(jnp.float32))
    stacked = jnp.zeros((16, block), jnp.float32)
    row = lax.broadcasted_iota(jnp.int32, (16, block), 0)
    for i, line in enumerate(lines):
        stacked = jnp.where((row == i) & (lane[0:1] < 64), line, stacked)
    stacked = stacked.astype(jnp.bfloat16)
    wide = spread_lanes(stacked, 8)
    j = lax.broadcasted_iota(jnp.int32, (1, 512), 1) & 7
    code = jnp.where(j < 4, wide[0:1], wide[2:3])
    rows_wide = jnp.concatenate([rows_down] * 4, axis=1)
    picks = [one_hot(jnp.where((j & 3) == h, code, float(nothing)) == rows_wide) for h in range(4)]
    for core in range(2):
        both = jnp.concatenate(
            [
                got_ref[core * 64 : core * 64 + 64, head_rows : head_rows + 8, :].reshape(512, head),
                got_ref[core * 64 : core * 64 + 64, head_rows + 8 :, :].reshape(512, head),
            ],
            axis=1,
        )
        for h in range(4):
            got = jnp.dot(picks[h], both, preferred_element_type=jnp.float32).astype(jnp.bfloat16)
            at = (4 * core + h) * head
            out_ref[:, at : at + head] = got[:, :head]
            dq_ref[:, at : at + head] = got[:, head:]
    moves[0].start()
    moves[1].start()
    wide = spread_lanes(stacked, head_rows)
    first, first_count, second, second_count, chip = [wide[i : i + 1] for i in range(5)]
    r = lax.broadcasted_iota(jnp.int32, (1, 64 * head_rows), 1) - head_rows * chip.astype(jnp.int32)
    sums = [jnp.zeros((block, head), jnp.float32), jnp.zeros((block, head), jnp.float32)]
    rows_wide = jnp.concatenate([rows_down] * (64 * head_rows // block), axis=1)
    for core in range(2):
        entry = ((r & -2) + core).astype(jnp.float32)
        code = jnp.where(
            entry < first_count,
            entry + (first - first_count + 1),
            jnp.where(entry >= entries - second_count, entry + (second - (entries - 1)), float(nothing)),
        )
        code = jnp.where(r < kv_rows, code, float(nothing))
        terms = got_ref[core * 64 : core * 64 + 64, :head_rows, :].reshape(64 * head_rows, head)
        for half in range(2):
            pick = one_hot(jnp.where((r & 1) == half, code, float(nothing)) == rows_wide)
            sums[half] = sums[half] + jnp.dot(pick, terms, preferred_element_type=jnp.float32)
    dkv_ref[...] = jnp.concatenate(sums, axis=1).astype(jnp.bfloat16)
    moves[2].start()
    for move in moves:
        move.wait()


def nt(a, b):
    return lax.dot_general(a, b, (((1,), (1,)), ((), ())), preferred_element_type=jnp.float32)


def tn(a, b):
    return lax.dot_general(a, b, (((0,), (0,)), ((), ())), preferred_element_type=jnp.float32)


def nn(a, b):
    return jnp.dot(a, b, preferred_element_type=jnp.float32)


def split_kernel(got_ref, kv_ref, info_ref, qg_ref):
    for r in range(0, send_rows, 8):
        rows = jnp.transpose(got_ref[:, r : r + 8, :], (1, 0, 2))
        if r < kv_rows:
            n = min(8, kv_rows - r)
            kv_ref[r : r + n] = rows[:n]
            if n < 8:
                info_ref[...] = rows[n]
        else:
            at = (r - head_rows) * block
            qg_ref[at : at + 8 * block, :] = rows.reshape(8 * block, head)


def attention_kernel(
    mine_len, other_len, plan_ref, mine_ref, other_ref, info_ref, qg,
    dmine_ref, dother_ref, out_ref, dq_ref,
    kv, scores, weights, top, total, acc, dot, qs, gs, key_pos, bound,
):
    core = lax.axis_index("dp")
    chip = lax.axis_index("ctx")
    stream = chip // 32
    scale = head ** (-0.5)
    to_exp2 = scale * 1.4426950408889634
    stream_base = (64 * stream).astype(jnp.float32)
    block_row = lax.broadcasted_iota(jnp.int32, (block, block), 0).astype(jnp.float32)
    lane8 = lax.broadcasted_iota(jnp.int32, (8, block), 1)
    row8 = lax.broadcasted_iota(jnp.int32, (8, block), 0)
    slots = info_ref[...].astype(jnp.float32)
    key_pos[...] = slots.T + 128.0 * (block_row - stream_base)
    for i in range(pairs):
        for half in range(2):
            kv[half, 2 * i * block : (2 * i + 1) * block, :] = mine_ref[2 * i + half]
            kv[half, (2 * i + 1) * block : (2 * i + 2) * block, :] = other_ref[2 * i + half]
    plan = plan_ref[...]
    dmine_ref[...] = jnp.zeros(dmine_ref.shape, jnp.bfloat16)
    dother_ref[...] = jnp.zeros(dother_ref.shape, jnp.bfloat16)
    span = 256 * step

    def planned(row, x):
        seat = (row8 == row) & (lane8 == chip + 64 * x)
        return jnp.sum(jnp.where(seat, plan, 0.0)).astype(jnp.int32)

    def some(half, m):
        return kv[half, pl.ds(pl.multiple_of(m * span, span), span), :]

    def add(ref, i, x):
        ref[i] = (ref[i].astype(jnp.float32) + x).astype(jnp.bfloat16)

    for x in range(2):
        mine_block = planned(0, x)
        count = planned(1, x)
        if x == 0:
            begin, end = jnp.int32(0), (count + 2 * step - 1) // (2 * step)
            entry_low, entry_high = jnp.int32(0), count
            base = mine_block - count + 1
        else:
            begin, end = (entries - count) // (2 * step), jnp.int32(pairs // step)
            entry_low, entry_high = entries - count, jnp.int32(entries)
            base = mine_block - (entries - 1)
        pos = key_pos[pl.ds(mine_block, 1), :]
        start = jnp.zeros((1, block), jnp.float32)
        doc_end = jnp.int32(0)
        for i in range(16):
            doc_end = doc_end + stream_length(core, mine_len, other_len, stream, i)
            f = doc_end.astype(jnp.float32)
            start = jnp.where(f <= pos, f, start)
        bound[0:1] = pos
        bound[1:2] = start
        top[...] = jnp.full(top.shape, masked_score, jnp.float32)
        total[...] = jnp.zeros(total.shape, jnp.float32)
        acc[...] = jnp.zeros(acc.shape, jnp.float32)
        q_at, g_at = x * 512, 1024 + x * 512

        @pl.loop(begin, end)
        def _(m):
            keys = some(0, m)
            bias = []
            for u, par in [(u, par) for u in range(step) for par in (core, 1 - core)]:
                entry = 2 * (m * step + u) + par
                valid = (entry >= entry_low) & (entry < entry_high)
                kp = key_pos[pl.ds(jnp.where(valid, base + entry, 0), 1), :]
                kp = jnp.broadcast_to(jnp.where(valid, kp, far), (block, block)).T
                bias.append(jnp.where((kp <= bound[0:1]) & (kp >= bound[1:2]), 0.0, masked_score))
            bias = jnp.concatenate(bias, axis=0)
            bias = jnp.concatenate([bias] * 4, axis=1)
            s = nt(keys, qg[q_at : q_at + 512, :]) + bias
            scores[m] = s
            top[...] = jnp.maximum(top[...], jnp.max(s.reshape(span // 8, 8, 512), axis=0))

        top[...] = jnp.broadcast_to(jnp.max(top[...], axis=0, keepdims=True) * to_exp2, top.shape)

        @pl.loop(begin, end)
        def _(m):
            p = jnp.exp2(scores[m] * to_exp2 - top[0:1])
            total[...] = total[...] + jnp.sum(p.reshape(span // 8, 8, 512), axis=0)
            half = p.astype(jnp.bfloat16)
            weights[m] = half
            acc[...] = acc[...] + tn(some(1, m), half)

        inv = 1.0 / jnp.sum(total[...], axis=0, keepdims=True)
        for h in range(4):
            at = slice(h * block, (h + 1) * block)
            q_rows = slice(q_at + h * block, q_at + (h + 1) * block)
            inv_down = jnp.broadcast_to(inv[:, at], (block, block)).T
            o = (acc[:, at].T * inv_down).astype(jnp.bfloat16)
            out_ref[q_rows, :] = o
            g = qg[g_at + h * block : g_at + (h + 1) * block, :].astype(jnp.float32)
            q = qg[q_rows, :].astype(jnp.float32)
            d = jnp.sum(g * o.astype(jnp.float32), axis=1, keepdims=True)
            dot[:, at] = jnp.broadcast_to(d, (block, block)).T[:8]
            gs[at] = (g * inv_down).astype(jnp.bfloat16)
            qs[at] = (q * (inv_down * scale)).astype(jnp.bfloat16)
        total[...] = jnp.broadcast_to(inv * scale, total.shape)
        acc[...] = jnp.zeros(acc.shape, jnp.float32)

        @pl.loop(begin, end)
        def _(m):
            gw = nt(some(1, m), qg[g_at : g_at + 512, :])
            p = weights[m]
            ds = (p.astype(jnp.float32) * (gw - dot[0:1])).astype(jnp.bfloat16)
            acc[...] = acc[...] + tn(some(0, m), ds)
            dk = nn(ds, qs[...])
            dv = nn(p, gs[...])
            for u in range(step):
                i = 2 * (m * step + u)
                add(dmine_ref, i, dk[u * 256 : u * 256 + block])
                add(dmine_ref, i + 1, dv[u * 256 : u * 256 + block])
                add(dother_ref, i, dk[u * 256 + block : (u + 1) * 256])
                add(dother_ref, i + 1, dv[u * 256 + block : (u + 1) * 256])

        for h in range(4):
            at = slice(h * block, (h + 1) * block)
            dq_ref[q_at + h * block : q_at + (h + 1) * block, :] = (acc[:, at] * total[0:1, at]).T.astype(jnp.bfloat16)


def join_kernel(mine_ref, other_ref, out_ref, dq_ref, back_ref):
    def put(r, rows):
        back_ref[:, r : r + 8, :] = jnp.transpose(rows, (1, 0, 2))

    for r in range(0, head_rows, 8):
        n = min(8, kv_rows - r)
        rows = mine_ref[r : r + n].astype(jnp.float32) + other_ref[r : r + n].astype(jnp.float32)
        rows = rows.astype(jnp.bfloat16)
        if n < 8:
            rows = jnp.concatenate([rows, jnp.zeros((8 - n, block, head), jnp.bfloat16)], axis=0)
        put(r, rows)
    put(head_rows, out_ref[...].reshape(8, block, head))
    put(head_rows + 8, dq_ref[...].reshape(8, block, head))


def vmem(n):
    return [pl.BlockSpec(memory_space=pltpu.VMEM)] * n


def smem():
    return pl.BlockSpec(memory_space=pltpu.SMEM)


def params(size):
    return pltpu.CompilerParams(vmem_limit_bytes=size * mib)


def swap(x):
    return lax.ppermute(x, "dp", [(0, 1), (1, 0)])


def exchange(x):
    return lax.all_to_all(x, ("dp", "ctx"), split_axis=0, concat_axis=0, tiled=True)


def on_device(queries, keys_values, grad_out, placement, doc_lengths):
    bf16, f32 = jnp.bfloat16, jnp.float32
    place = placement.reshape(1, block)
    other_lengths = swap(doc_lengths)
    sent, plan = pl.pallas_call(
        pack_kernel,
        out_shape=(
            jax.ShapeDtypeStruct((128, send_rows, head), bf16),
            jax.ShapeDtypeStruct((8, block), f32),
        ),
        in_specs=[pl.BlockSpec(memory_space=pl.ANY)] * 6,
        out_specs=(pl.BlockSpec(memory_space=pl.ANY), vmem(1)[0]),
        scratch_shapes=[
            pltpu.SMEM((1, 16), jnp.int32),
            pltpu.SMEM((1, 16), jnp.int32),
            pltpu.VMEM((1, block), jnp.int32),
            pltpu.VMEM((block, 8 * head), bf16),
            pltpu.VMEM((block, 2 * head), bf16),
            pltpu.VMEM((block, 8 * head), bf16),
            pltpu.VMEM((128, send_rows, head), bf16),
            pltpu.SemaphoreType.DMA((6 + 128 // group,)),
        ],
        compiler_params=pltpu.CompilerParams(vmem_limit_bytes=58 * mib),
        name="pack",
    )(doc_lengths, other_lengths, place, queries, keys_values, grad_out)
    mine, info, qg = pl.pallas_call(
        split_kernel,
        out_shape=(
            jax.ShapeDtypeStruct((kv_rows, block, head), bf16),
            jax.ShapeDtypeStruct((block, head), bf16),
            jax.ShapeDtypeStruct((2048, head), bf16),
        ),
        in_specs=vmem(1),
        out_specs=tuple(vmem(3)),
        compiler_params=params(24),
        name="split",
    )(exchange(sent))
    dmine, dother, out, dq = pl.pallas_call(
        attention_kernel,
        out_shape=(
            jax.ShapeDtypeStruct((kv_rows, block, head), bf16),
            jax.ShapeDtypeStruct((kv_rows, block, head), bf16),
            jax.ShapeDtypeStruct((1024, head), bf16),
            jax.ShapeDtypeStruct((1024, head), bf16),
        ),
        in_specs=[smem()] * 2 + vmem(5),
        out_specs=tuple(vmem(4)),
        scratch_shapes=[
            pltpu.VMEM((2, entries * block, head), bf16),
            pltpu.VMEM((pairs // step, 256 * step, 512), f32),
            pltpu.VMEM((pairs // step, 256 * step, 512), bf16),
            pltpu.VMEM((8, 512), f32),
            pltpu.VMEM((8, 512), f32),
            pltpu.VMEM((head, 512), f32),
            pltpu.VMEM((8, 512), f32),
            pltpu.VMEM((512, head), bf16),
            pltpu.VMEM((512, head), bf16),
            pltpu.VMEM((block, block), f32),
            pltpu.VMEM((8, block), f32),
        ],
        compiler_params=params(32),
        name="attention",
    )(doc_lengths, other_lengths, plan, mine, swap(mine), info, qg)
    back = pl.pallas_call(
        join_kernel,
        out_shape=jax.ShapeDtypeStruct((128, send_rows, head), bf16),
        in_specs=vmem(4),
        out_specs=vmem(1)[0],
        compiler_params=params(24),
        name="join",
    )(dmine, swap(dother), out, dq)
    returned = exchange(back)
    return pl.pallas_call(
        unpack_kernel,
        out_shape=(
            jax.ShapeDtypeStruct((block, 8 * head), bf16),
            jax.ShapeDtypeStruct((block, 8 * head), bf16),
            jax.ShapeDtypeStruct((block, 2 * head), bf16),
        ),
        in_specs=vmem(3),
        out_specs=tuple([pl.BlockSpec(memory_space=pl.ANY)] * 3),
        scratch_shapes=[
            pltpu.VMEM((block, 8 * head), bf16),
            pltpu.VMEM((block, 8 * head), bf16),
            pltpu.VMEM((block, 2 * head), bf16),
            pltpu.SemaphoreType.DMA((3,)),
        ],
        compiler_params=params(24),
        name="unpack",
    )(place, plan, returned)


def solution(mesh):
    rows = P(("dp", "ctx"), None)
    return jax.shard_map(
        on_device,
        mesh=mesh,
        in_specs=(rows, rows, rows, P(("dp", "ctx")), P("dp", None)),
        out_specs=(rows, rows, rows),
        check_vma=False,
    )
```

```python
import jax
import jax.numpy as jnp
from jax import lax
from jax.experimental import pallas as pl
from jax.experimental.pallas import tpu as pltpu
from jax.sharding import PartitionSpec as P

block = 128
head = 128
entries = 36
pairs = entries // 2
kv_rows = 2 * pairs
head_rows = 40
send_rows = 56
group = 16
other_half = 1000
nothing = -100000
masked_score = -1e30
far = 1e9
mib = 1024 * 1024


def one_hot(mask):
    return jnp.where(mask, 1.0, 0.0).astype(jnp.bfloat16)


def down(line):
    return jnp.broadcast_to(line.astype(jnp.float32), (block, block)).T


def stream_length(core, mine_ref, other_ref, stream, i):
    return jnp.where(core == stream, mine_ref[0, i], other_ref[0, i])


def make_plan(core, mine_ref, other_ref):
    lane = lax.broadcasted_iota(jnp.int32, (1, block), 1)
    pos = (lane & 63) * block
    start = jnp.zeros((1, block), jnp.int32)
    end0, end1 = jnp.int32(0), jnp.int32(0)
    for i in range(16):
        end0 = end0 + stream_length(core, mine_ref, other_ref, 0, i)
        end1 = end1 + stream_length(core, mine_ref, other_ref, 1, i)
        end = jnp.where(lane < 64, end0, end1)
        start = jnp.where(end <= pos, end, start)
    count = (lane & 63) - (start >> 7) + 1
    key = count * 64 + (lane & 63)
    row = lax.broadcasted_iota(jnp.int32, (block, block), 0)
    col = lax.broadcasted_iota(jnp.int32, (block, block), 1)
    above = (down(key) > key.astype(jnp.float32)) & ((row >> 6) == (col >> 6))
    rank = jnp.sum(jnp.where(above, 1.0, 0.0), axis=0, keepdims=True).astype(jnp.int32)
    seat = jnp.where(rank < 32, rank, 63 - rank) + 32 * (lane >> 6) + jnp.where(rank < 32, 0, 64)
    here = down(seat) == col.astype(jnp.float32)
    block_line = jnp.sum(jnp.where(here, row.astype(jnp.float32), 0.0), axis=0, keepdims=True)
    count_line = jnp.sum(jnp.where(here, down(count), 0.0), axis=0, keepdims=True)
    return block_line, count_line


def pack_kernel(
    mine_hbm, other_hbm, place_hbm, q_hbm, kv_hbm, g_hbm, out_hbm, plan_ref,
    mine_ref, other_ref, place_ref, q_ref, kv_ref, g_ref, out_ref, sems,
):
    moves = [
        pltpu.make_async_copy(src, dst, sems.at[i])
        for i, (src, dst) in enumerate(
            [
                (mine_hbm, mine_ref),
                (other_hbm, other_ref),
                (place_hbm, place_ref),
                (kv_hbm, kv_ref),
                (q_hbm, q_ref),
                (g_hbm, g_ref),
            ]
        )
    ]
    for move in moves:
        move.start()
    for move in moves[:3]:
        move.wait()
    block_line, count_line = make_plan(lax.axis_index("dp"), mine_ref, other_ref)
    row8 = lax.broadcasted_iota(jnp.int32, (8, block), 0)
    plan_ref[...] = jnp.where(row8 == 0, block_line, jnp.where(row8 == 1, count_line, 0.0)).astype(jnp.int32)
    block_down = down(block_line).astype(jnp.int32)
    count_down = down(count_line).astype(jnp.int32)
    rows = place_ref[...] >> 7
    lane = lax.broadcasted_iota(jnp.int32, (block, block), 1)
    slots_down = down(place_ref[...] & (block - 1))
    slot_line = jnp.sum(jnp.where(down(rows) == lane.astype(jnp.float32), slots_down, 0.0), axis=0, keepdims=True)
    extra = jnp.where(row8 == kv_rows % 8, slot_line, 0.0)
    moves[3].wait()
    kv = jnp.concatenate([kv_ref[:, :head], kv_ref[:, head:]], axis=0)
    r = lax.broadcasted_iota(jnp.int32, (group, head_rows, block), 1)
    half = (r & 1) * other_half
    j = lax.broadcasted_iota(jnp.int32, (group, 8, block), 1)
    moves[4].wait()
    moves[5].wait()
    both = []
    for core in range(2):
        heads = [slice((4 * core + h) * head, (4 * core + h + 1) * head) for h in range(4)]
        both.append(jnp.concatenate([jnp.concatenate([q_ref[:, at], g_ref[:, at]], axis=1) for at in heads], axis=0))

    def spread(x, n):
        return jnp.broadcast_to(x[:, None, :], (group, n, block))

    sends = []
    for chip in range(0, 64, group):
        first = block_down[chip : chip + group]
        first_count = count_down[chip : chip + group]
        second = block_down[64 + chip : 64 + chip + group]
        second_count = count_down[64 + chip : 64 + chip + group]
        wanted = jnp.where(j < 4, spread(first, 8), spread(second, 8)) == rows[None]
        heads = jnp.concatenate(
            [one_hot(wanted & ((j & 3) == h)).reshape(group * 8, block) for h in range(4)], axis=1
        )
        for core in range(2):
            t = core * 64 + chip
            entry = (r & -2) + core
            code = jnp.where(
                entry < spread(first_count, head_rows),
                entry + spread(first - first_count + 1, head_rows),
                jnp.where(
                    entry >= spread(entries - second_count, head_rows),
                    entry + spread(second - (entries - 1), head_rows),
                    nothing,
                ),
            )
            code = (jnp.where(r < kv_rows, code, nothing) + half).reshape(group * head_rows, block)
            pick = jnp.concatenate([one_hot(code == rows), one_hot(code == rows + other_half)], axis=1)
            got = jnp.dot(pick, kv, preferred_element_type=jnp.float32).reshape(group, head_rows, head)
            tail = got[:, head_rows - 8 :, :] + extra[None]
            got = jnp.concatenate([got[:, : head_rows - 8, :], tail], axis=1)
            out_ref[t : t + group, :head_rows, :] = got.astype(jnp.bfloat16)
            got = jnp.dot(heads, both[core], preferred_element_type=jnp.float32).astype(jnp.bfloat16)
            out_ref[t : t + group, head_rows : head_rows + 8, :] = got[:, :head].reshape(group, 8, head)
            out_ref[t : t + group, head_rows + 8 :, :] = got[:, head:].reshape(group, 8, head)
            at = pl.ds(t, group)
            sends.append(pltpu.make_async_copy(out_ref.at[at], out_hbm.at[at], sems.at[6 + len(sends)]))
            sends[-1].start()
    for send in sends:
        send.wait()


def spread_lanes(plan, width):
    chip = lax.broadcasted_iota(jnp.int32, (block, 64 * width), 0) * width
    lane = lax.broadcasted_iota(jnp.int32, (block, 64 * width), 1)
    return jnp.dot(plan, one_hot((lane >= chip) & (lane < chip + width)), preferred_element_type=jnp.float32)


def unpack_kernel(
    place_ref, plan_ref, got_ref, out_hbm, dq_hbm, dkv_hbm, out_ref, dq_ref, dkv_ref, sems
):
    moves = [
        pltpu.make_async_copy(src, dst, sems.at[i])
        for i, (src, dst) in enumerate([(out_ref, out_hbm), (dq_ref, dq_hbm), (dkv_ref, dkv_hbm)])
    ]
    rows_down = down(place_ref[...] >> 7)
    plan = plan_ref[...].astype(jnp.float32)
    lane = lax.broadcasted_iota(jnp.int32, (8, block), 1)
    lines = [plan[0:1], plan[1:2]]
    lines = lines + [pltpu.roll(plan, 64, 1)[i : i + 1] for i in range(2)]
    lines.append(lane[0:1].astype(jnp.float32))
    stacked = jnp.zeros((16, block), jnp.float32)
    row = lax.broadcasted_iota(jnp.int32, (16, block), 0)
    for i, line in enumerate(lines):
        stacked = jnp.where((row == i) & (lane[0:1] < 64), line, stacked)
    stacked = stacked.astype(jnp.bfloat16)
    wide = spread_lanes(stacked, 8)
    j = lax.broadcasted_iota(jnp.int32, (1, 512), 1) & 7
    code = jnp.where(j < 4, wide[0:1], wide[2:3])
    rows_wide = jnp.concatenate([rows_down] * 4, axis=1)
    picks = [one_hot(jnp.where((j & 3) == h, code, float(nothing)) == rows_wide) for h in range(4)]
    for core in range(2):
        both = jnp.concatenate(
            [
                got_ref[core * 64 : core * 64 + 64, head_rows : head_rows + 8, :].reshape(512, head),
                got_ref[core * 64 : core * 64 + 64, head_rows + 8 :, :].reshape(512, head),
            ],
            axis=1,
        )
        for h in range(4):
            got = jnp.dot(picks[h], both, preferred_element_type=jnp.float32).astype(jnp.bfloat16)
            at = (4 * core + h) * head
            out_ref[:, at : at + head] = got[:, :head]
            dq_ref[:, at : at + head] = got[:, head:]
    moves[0].start()
    moves[1].start()
    wide = spread_lanes(stacked, head_rows)
    first, first_count, second, second_count, chip = [wide[i : i + 1] for i in range(5)]
    r = lax.broadcasted_iota(jnp.int32, (1, 64 * head_rows), 1) - head_rows * chip.astype(jnp.int32)
    sums = [jnp.zeros((block, head), jnp.float32), jnp.zeros((block, head), jnp.float32)]
    rows_wide = jnp.concatenate([rows_down] * (64 * head_rows // block), axis=1)
    for core in range(2):
        entry = ((r & -2) + core).astype(jnp.float32)
        code = jnp.where(
            entry < first_count,
            entry + (first - first_count + 1),
            jnp.where(entry >= entries - second_count, entry + (second - (entries - 1)), float(nothing)),
        )
        code = jnp.where(r < kv_rows, code, float(nothing))
        terms = got_ref[core * 64 : core * 64 + 64, :head_rows, :].reshape(64 * head_rows, head)
        for half in range(2):
            pick = one_hot(jnp.where((r & 1) == half, code, float(nothing)) == rows_wide)
            sums[half] = sums[half] + jnp.dot(pick, terms, preferred_element_type=jnp.float32)
    dkv_ref[...] = jnp.concatenate(sums, axis=1).astype(jnp.bfloat16)
    moves[2].start()
    for move in moves:
        move.wait()


def nt(a, b):
    return lax.dot_general(a, b, (((1,), (1,)), ((), ())), preferred_element_type=jnp.float32)


def tn(a, b):
    return lax.dot_general(a, b, (((0,), (0,)), ((), ())), preferred_element_type=jnp.float32)


def nn(a, b):
    return jnp.dot(a, b, preferred_element_type=jnp.float32)


def split_kernel(got_ref, kv_ref, info_ref, qg_ref):
    for r in range(0, send_rows, 8):
        rows = jnp.transpose(got_ref[:, r : r + 8, :], (1, 0, 2))
        if r < kv_rows:
            n = min(8, kv_rows - r)
            kv_ref[r : r + n] = rows[:n]
            if n < 8:
                info_ref[...] = rows[n]
        else:
            at = (r - head_rows) * block
            qg_ref[at : at + 8 * block, :] = rows.reshape(8 * block, head)


to_exp2 = head ** (-0.5) * 1.4426950408889634


def span_of(x, plan_ref, chip):
    count = plan_ref[1, chip + 64 * x]
    if x == 0:
        return 3, 0, jnp.int32(0), count, jnp.int32(0), (count + 5) // 6
    return 1, 3, entries - count, jnp.int32(entries), (entries - count) // 2, jnp.int32(pairs)


def rows_of(x):
    return slice(x * 512, (x + 1) * 512), slice(1024 + x * 512, 1536 + x * 512)


def blocks(ref, half, m, n):
    return jnp.concatenate([ref[2 * (m * n + u) + half] for u in range(n)], axis=0)


def slot(m, n, shift):
    return pl.ds(m * n + shift, n)


def flat(x):
    return x.reshape(x.shape[0] * block, 512)


def find_positions(core, chip, mine_len, other_len, plan_ref, info_ref, key_pos, bound):
    stream = chip // 32
    stream_base = (64 * stream).astype(jnp.float32)
    block_row = lax.broadcasted_iota(jnp.int32, (block, block), 0)
    key_pos[...] = info_ref[...].astype(jnp.float32).T + 128.0 * (block_row.astype(jnp.float32) - stream_base)
    for x in range(2):
        pos = key_pos[pl.ds(plan_ref[0, chip + 64 * x], 1), :]
        start = jnp.zeros((1, block), jnp.float32)
        doc_end = jnp.int32(0)
        for i in range(16):
            doc_end = doc_end + stream_length(core, mine_len, other_len, stream, i)
            f = doc_end.astype(jnp.float32)
            start = jnp.where(f <= pos, f, start)
        bound[2 * x : 2 * x + 1] = pos
        bound[2 * x + 1 : 2 * x + 2] = start


def score(x, m, n, low, high, parity, plan_ref, chip, kv_ref, qg, key_pos, bound):
    base = plan_ref[0, chip + 64 * x] - plan_ref[1, chip + 64 * x] + 1 - low
    bias = []
    for u in range(n):
        entry = 2 * (m * n + u) + parity
        valid = (entry >= low) & (entry < high)
        kp = key_pos[pl.ds(jnp.where(valid, base + entry, 0), 1), :]
        kp = jnp.broadcast_to(jnp.where(valid, kp, far), (block, block)).T
        seen = (kp <= bound[2 * x : 2 * x + 1]) & (kp >= bound[2 * x + 1 : 2 * x + 2])
        bias.append(jnp.where(seen, 0.0, masked_score))
    bias = jnp.concatenate(bias, axis=0)
    bias = jnp.concatenate([bias] * 4, axis=1)
    return nt(blocks(kv_ref, 0, m, n), qg[rows_of(x)[0], :]) + bias


def peak_of(s):
    return jnp.max(s.reshape(s.shape[0] // 8, 8, 512), axis=0)


def sum_of(p):
    return jnp.sum(p.reshape(p.shape[0] // 8, 8, 512), axis=0)


def scores_kernel(
    mine_len, other_len, plan_ref, mine_ref, info_ref, qg,
    s_ref, gw_ref, top_ref,
    key_pos, bound,
):
    core = lax.axis_index("dp")
    chip = lax.axis_index("ctx")
    find_positions(core, chip, mine_len, other_len, plan_ref, info_ref, key_pos, bound)
    for x in range(2):
        n, shift, low, high, begin, end = span_of(x, plan_ref, chip)
        top_ref[x] = jnp.full((8, 512), masked_score, jnp.float32)

        @pl.loop(begin, end)
        def _(m):
            s = score(x, m, n, low, high, core, plan_ref, chip, mine_ref, qg, key_pos, bound)
            gw = nt(blocks(mine_ref, 1, m, n), qg[rows_of(x)[1], :])
            s_ref[slot(m, n, shift)] = s.reshape(n, block, 512)
            top_ref[x] = jnp.maximum(top_ref[x], peak_of(s))
            gw_ref[slot(m, n, shift)] = gw.reshape(n, block, 512)


def backward(n, at, p_ref, gw_ref, kv_ref, dot, qs, gs, acc, out_ref, first, m):
    p = flat(p_ref[at])
    ds = (p.astype(jnp.float32) * (flat(gw_ref[at]) - dot)).astype(jnp.bfloat16)
    dk = nn(ds, qs)
    acc[...] = acc[...] + tn(blocks(kv_ref, 0, m, n), ds)
    dv = nn(p, gs)
    for u in range(n):
        for half, value in enumerate((dk, dv)):
            value = value[u * block : (u + 1) * block]
            i = 2 * (m * n + u) + half
            if not first:
                value = value + out_ref[i].astype(jnp.float32)
            out_ref[i] = value.astype(jnp.bfloat16)


def clear_rest(out_ref, end):
    @pl.loop(6 * end, kv_rows)
    def _(i):
        out_ref[i] = jnp.zeros((block, head), jnp.bfloat16)


def turned(x):
    row = lax.broadcasted_iota(jnp.int32, (block, block), 0)
    eye = one_hot(row == lax.broadcasted_iota(jnp.int32, (block, block), 1))
    return jnp.concatenate([nt(eye, x[:, h * block : (h + 1) * block]) for h in range(4)], axis=0)


def weights_kernel(
    mine_len, other_len, plan_ref, mine_ref, other_ref, info_ref, qg, s_ref, found_ref,
    dother_ref, out_ref, p_ref, dot_ref, qs_ref, gs_ref, acc_ref, inv_ref,
    scores, gws, ps, top, total, acc, key_pos, bound,
):
    core = lax.axis_index("dp")
    chip = lax.axis_index("ctx")
    scale = head ** (-0.5)
    ones = jnp.full((16, block), 1.0, jnp.bfloat16)
    row16 = lax.broadcasted_iota(jnp.int32, (16, 512), 0)
    find_positions(core, chip, mine_len, other_len, plan_ref, info_ref, key_pos, bound)
    for x in range(2):
        n, shift, low, high, begin, end = span_of(x, plan_ref, chip)
        q_rows, g_rows = rows_of(x)
        if x == 0:
            clear_rest(dother_ref, end)
        top[...] = found_ref[x]

        @pl.loop(begin, end)
        def _(m):
            s = score(x, m, n, low, high, 1 - core, plan_ref, chip, other_ref, qg, key_pos, bound)
            scores[slot(m, n, shift)] = s.reshape(n, block, 512)
            top[...] = jnp.maximum(top[...], peak_of(s))

        top[...] = jnp.broadcast_to(jnp.max(top[...], axis=0, keepdims=True) * to_exp2, (8, 512))
        total[...] = jnp.zeros(total.shape, jnp.float32)
        acc[...] = jnp.zeros(acc.shape, jnp.float32)

        @pl.loop(begin, end)
        def _(m):
            at = slot(m, n, shift)
            gws[at] = nt(blocks(other_ref, 1, m, n), qg[g_rows, :]).reshape(n, block, 512)
            p = jnp.exp2(flat(s_ref[at]) * to_exp2 - top[0:1])
            p_other = jnp.exp2(flat(scores[at]) * to_exp2 - top[0:1])
            total[...] = total[...] + (sum_of(p) + sum_of(p_other))
            p, p_other = p.astype(jnp.bfloat16), p_other.astype(jnp.bfloat16)
            p_ref[at] = p.reshape(n, block, 512)
            ps[at] = p_other.reshape(n, block, 512)
            values = jnp.concatenate([blocks(mine_ref, 1, m, n), blocks(other_ref, 1, m, n)], axis=0)
            acc[...] = acc[...] + tn(values, jnp.concatenate([p, p_other], axis=0))

        inv = 1.0 / jnp.sum(total[...], axis=0, keepdims=True)
        part = inv.astype(jnp.bfloat16).astype(jnp.float32)
        rest = inv - part
        middle = rest.astype(jnp.bfloat16).astype(jnp.float32)
        parts = jnp.where(row16 == 0, part, jnp.where(row16 == 1, middle, jnp.where(row16 == 2, rest - middle, 0.0)))
        inv_down = tn(parts.astype(jnp.bfloat16), ones)
        o = turned((acc[...] * inv).astype(jnp.bfloat16))
        out_ref[q_rows, :] = o.astype(jnp.bfloat16)
        g = qg[g_rows, :].astype(jnp.float32)
        terms = g * o
        part = terms.astype(jnp.bfloat16)
        d = nt(ones, part) + nt(ones, (terms - part.astype(jnp.float32)).astype(jnp.bfloat16))
        dot_ref[x] = d[:8]
        gs_ref[q_rows, :] = (g * inv_down).astype(jnp.bfloat16)
        qs_ref[q_rows, :] = (qg[q_rows, :].astype(jnp.float32) * (inv_down * scale)).astype(jnp.bfloat16)
        inv_ref[x] = jnp.broadcast_to(inv * scale, (8, 512))
        acc[...] = jnp.zeros(acc.shape, jnp.float32)

        @pl.loop(begin, end)
        def _(m):
            backward(
                n, slot(m, n, shift), ps, gws, other_ref, dot_ref[x][0:1], qs_ref[q_rows, :], gs_ref[q_rows, :],
                acc, dother_ref, x == 0, m,
            )

        acc_ref[x] = acc[...]


def grads_kernel(
    plan_ref, mine_ref, gw_ref, p_ref, dot_ref, qs_ref, gs_ref, acc_ref, inv_ref,
    dmine_ref, dq_ref,
    acc,
):
    chip = lax.axis_index("ctx")
    for x in range(2):
        n, shift, _, _, begin, end = span_of(x, plan_ref, chip)
        q_rows = rows_of(x)[0]
        if x == 0:
            clear_rest(dmine_ref, end)
        acc[...] = acc_ref[x]

        @pl.loop(begin, end)
        def _(m):
            backward(
                n, slot(m, n, shift), p_ref, gw_ref, mine_ref, dot_ref[x][0:1], qs_ref[q_rows, :], gs_ref[q_rows, :],
                acc, dmine_ref, x == 0, m,
            )

        dq_ref[q_rows, :] = turned((acc[...] * inv_ref[x][0:1]).astype(jnp.bfloat16)).astype(jnp.bfloat16)


def join_kernel(mine_ref, other_ref, out_ref, dq_ref, back_ref):
    def put(r, rows):
        back_ref[:, r : r + 8, :] = jnp.transpose(rows, (1, 0, 2))

    for r in range(0, head_rows, 8):
        n = min(8, kv_rows - r)
        rows = mine_ref[r : r + n].astype(jnp.float32) + other_ref[r : r + n].astype(jnp.float32)
        rows = rows.astype(jnp.bfloat16)
        if n < 8:
            rows = jnp.concatenate([rows, jnp.zeros((8 - n, block, head), jnp.bfloat16)], axis=0)
        put(r, rows)
    put(head_rows, out_ref[...].reshape(8, block, head))
    put(head_rows + 8, dq_ref[...].reshape(8, block, head))


def vmem(n):
    return [pl.BlockSpec(memory_space=pltpu.VMEM)] * n


def smem():
    return pl.BlockSpec(memory_space=pltpu.SMEM)


def params(size):
    return pltpu.CompilerParams(vmem_limit_bytes=size * mib)


def swap(x):
    return lax.ppermute(x, "dp", [(0, 1), (1, 0)])


def exchange(x):
    return lax.all_to_all(x, ("dp", "ctx"), split_axis=0, concat_axis=0, tiled=True)


def kernel(name, body, ins, scalars, outs, scratch, size):
    return pl.pallas_call(
        body,
        out_shape=tuple(jax.ShapeDtypeStruct(shape, dtype) for shape, dtype in outs),
        in_specs=[smem()] * scalars + vmem(len(ins) - scalars),
        out_specs=tuple(vmem(len(outs))),
        scratch_shapes=[pltpu.VMEM(shape, dtype) for shape, dtype in scratch],
        compiler_params=params(size),
        name=name,
    )(*ins)


def attention(lengths, other_lengths, plan, mine, other, info, qg):
    bf16, f32 = jnp.bfloat16, jnp.float32
    slots = (pairs + 3, block, 512)
    rows = ((2, 8, 512), f32)
    acc = ((2, head, 512), f32)
    heads = ((1024, head), bf16)
    places = [((block, block), f32), ((8, block), f32)]
    s, gw, top = kernel(
        "scores", scores_kernel, (lengths, other_lengths, plan, mine, info, qg), 3,
        [(slots, f32), (slots, f32), rows], places, 12,
    )
    dother, out, p, dot, qs, gs, partial, inv = kernel(
        "weights", weights_kernel, (lengths, other_lengths, plan, mine, other, info, qg, s, top), 3,
        [((kv_rows, block, head), bf16), heads, (slots, bf16), rows, heads, heads, acc, rows],
        [(slots, f32), (slots, f32), (slots, bf16), ((8, 512), f32), ((8, 512), f32), ((head, 512), f32)] + places, 24,
    )
    other_terms = swap(dother)
    dmine, dq = kernel(
        "grads", grads_kernel, (plan, mine, gw, p, dot, qs, gs, partial, inv), 1,
        [((kv_rows, block, head), bf16), heads], [((head, 512), f32)], 12,
    )
    return dmine, other_terms, out, dq


def on_device(queries, keys_values, grad_out, placement, doc_lengths):
    bf16, f32 = jnp.bfloat16, jnp.float32
    place = placement.reshape(1, block)
    other_lengths = swap(doc_lengths)
    sent, plan = pl.pallas_call(
        pack_kernel,
        out_shape=(
            jax.ShapeDtypeStruct((128, send_rows, head), bf16),
            jax.ShapeDtypeStruct((8, block), jnp.int32),
        ),
        in_specs=[pl.BlockSpec(memory_space=pl.ANY)] * 6,
        out_specs=(pl.BlockSpec(memory_space=pl.ANY), vmem(1)[0]),
        scratch_shapes=[
            pltpu.SMEM((1, 16), jnp.int32),
            pltpu.SMEM((1, 16), jnp.int32),
            pltpu.VMEM((1, block), jnp.int32),
            pltpu.VMEM((block, 8 * head), bf16),
            pltpu.VMEM((block, 2 * head), bf16),
            pltpu.VMEM((block, 8 * head), bf16),
            pltpu.VMEM((128, send_rows, head), bf16),
            pltpu.SemaphoreType.DMA((6 + 128 // group,)),
        ],
        compiler_params=pltpu.CompilerParams(vmem_limit_bytes=58 * mib),
        name="pack",
    )(doc_lengths, other_lengths, place, queries, keys_values, grad_out)
    mine, info, qg = pl.pallas_call(
        split_kernel,
        out_shape=(
            jax.ShapeDtypeStruct((kv_rows, block, head), bf16),
            jax.ShapeDtypeStruct((block, head), bf16),
            jax.ShapeDtypeStruct((2048, head), bf16),
        ),
        in_specs=vmem(1),
        out_specs=tuple(vmem(3)),
        compiler_params=params(24),
        name="split",
    )(exchange(sent))
    dmine, dother, out, dq = attention(doc_lengths, other_lengths, plan, mine, swap(mine), info, qg)
    back = pl.pallas_call(
        join_kernel,
        out_shape=jax.ShapeDtypeStruct((128, send_rows, head), bf16),
        in_specs=vmem(4),
        out_specs=vmem(1)[0],
        compiler_params=params(24),
        name="join",
    )(dmine, dother, out, dq)
    returned = exchange(back)
    return pl.pallas_call(
        unpack_kernel,
        out_shape=(
            jax.ShapeDtypeStruct((block, 8 * head), bf16),
            jax.ShapeDtypeStruct((block, 8 * head), bf16),
            jax.ShapeDtypeStruct((block, 2 * head), bf16),
        ),
        in_specs=vmem(3),
        out_specs=tuple([pl.BlockSpec(memory_space=pl.ANY)] * 3),
        scratch_shapes=[
            pltpu.VMEM((block, 8 * head), bf16),
            pltpu.VMEM((block, 8 * head), bf16),
            pltpu.VMEM((block, 2 * head), bf16),
            pltpu.SemaphoreType.DMA((3,)),
        ],
        compiler_params=params(24),
        name="unpack",
    )(place, plan, returned)


def solution(mesh):
    rows = P(("dp", "ctx"), None)
    return jax.shard_map(
        on_device,
        mesh=mesh,
        in_specs=(rows, rows, rows, P(("dp", "ctx")), P("dp", None)),
        out_specs=(rows, rows, rows),
        check_vma=False,
    )
```

```python
import jax
import jax.numpy as jnp
from jax import lax
from jax.experimental import pallas as pl
from jax.experimental.pallas import tpu as pltpu
from jax.sharding import PartitionSpec as P

block = 128
head = 128
entries = 36
pairs = entries // 2
kv_rows = 2 * pairs
head_rows = 40
send_rows = 56
group = 16
other_half = 1000
nothing = -100000
masked_score = -1e30
far = 1e9
mib = 1024 * 1024


def one_hot(mask):
    return jnp.where(mask, 1.0, 0.0).astype(jnp.bfloat16)


def down(line):
    return jnp.broadcast_to(line.astype(jnp.float32), (block, block)).T


def stream_length(core, mine_ref, other_ref, stream, i):
    return jnp.where(core == stream, mine_ref[0, i], other_ref[0, i])


def make_plan(core, mine_ref, other_ref):
    lane = lax.broadcasted_iota(jnp.int32, (1, block), 1)
    pos = (lane & 63) * block
    start = jnp.zeros((1, block), jnp.int32)
    end0, end1 = jnp.int32(0), jnp.int32(0)
    for i in range(16):
        end0 = end0 + stream_length(core, mine_ref, other_ref, 0, i)
        end1 = end1 + stream_length(core, mine_ref, other_ref, 1, i)
        end = jnp.where(lane < 64, end0, end1)
        start = jnp.where(end <= pos, end, start)
    count = (lane & 63) - (start >> 7) + 1
    key = count * 64 + (lane & 63)
    row = lax.broadcasted_iota(jnp.int32, (block, block), 0)
    col = lax.broadcasted_iota(jnp.int32, (block, block), 1)
    above = (down(key) > key.astype(jnp.float32)) & ((row >> 6) == (col >> 6))
    rank = jnp.sum(jnp.where(above, 1.0, 0.0), axis=0, keepdims=True).astype(jnp.int32)
    seat = jnp.where(rank < 32, rank, 63 - rank) + 32 * (lane >> 6) + jnp.where(rank < 32, 0, 64)
    here = down(seat) == col.astype(jnp.float32)
    block_line = jnp.sum(jnp.where(here, row.astype(jnp.float32), 0.0), axis=0, keepdims=True)
    count_line = jnp.sum(jnp.where(here, down(count), 0.0), axis=0, keepdims=True)
    return block_line, count_line


def pack_kernel(
    mine_hbm, other_hbm, place_hbm, q_hbm, kv_hbm, g_hbm, out_hbm, plan_ref,
    mine_ref, other_ref, place_ref, q_ref, kv_ref, g_ref, out_ref, sems,
):
    moves = [
        pltpu.make_async_copy(src, dst, sems.at[i])
        for i, (src, dst) in enumerate(
            [
                (mine_hbm, mine_ref),
                (other_hbm, other_ref),
                (place_hbm, place_ref),
                (kv_hbm, kv_ref),
                (q_hbm, q_ref),
                (g_hbm, g_ref),
            ]
        )
    ]
    for move in moves:
        move.start()
    for move in moves[:3]:
        move.wait()
    block_line, count_line = make_plan(lax.axis_index("dp"), mine_ref, other_ref)
    row8 = lax.broadcasted_iota(jnp.int32, (8, block), 0)
    plan_ref[...] = jnp.where(row8 == 0, block_line, jnp.where(row8 == 1, count_line, 0.0)).astype(jnp.int32)
    block_down = down(block_line).astype(jnp.int32)
    count_down = down(count_line).astype(jnp.int32)
    rows = place_ref[...] >> 7
    lane = lax.broadcasted_iota(jnp.int32, (block, block), 1)
    slots_down = down(place_ref[...] & (block - 1))
    slot_line = jnp.sum(jnp.where(down(rows) == lane.astype(jnp.float32), slots_down, 0.0), axis=0, keepdims=True)
    extra = jnp.where(row8 == kv_rows % 8, slot_line, 0.0)
    moves[3].wait()
    kv = jnp.concatenate([kv_ref[:, :head], kv_ref[:, head:]], axis=0)
    r = lax.broadcasted_iota(jnp.int32, (group, head_rows, block), 1)
    half = (r & 1) * other_half
    j = lax.broadcasted_iota(jnp.int32, (group, 8, block), 1)
    moves[4].wait()
    moves[5].wait()
    both = []
    for core in range(2):
        heads = [slice((4 * core + h) * head, (4 * core + h + 1) * head) for h in range(4)]
        both.append(jnp.concatenate([jnp.concatenate([q_ref[:, at], g_ref[:, at]], axis=1) for at in heads], axis=0))

    def spread(x, n):
        return jnp.broadcast_to(x[:, None, :], (group, n, block))

    sends = []
    for chip in range(0, 64, group):
        first = block_down[chip : chip + group]
        first_count = count_down[chip : chip + group]
        second = block_down[64 + chip : 64 + chip + group]
        second_count = count_down[64 + chip : 64 + chip + group]
        wanted = jnp.where(j < 4, spread(first, 8), spread(second, 8)) == rows[None]
        heads = jnp.concatenate(
            [one_hot(wanted & ((j & 3) == h)).reshape(group * 8, block) for h in range(4)], axis=1
        )
        for core in range(2):
            t = core * 64 + chip
            entry = (r & -2) + core
            code = jnp.where(
                entry < spread(first_count, head_rows),
                entry + spread(first - first_count + 1, head_rows),
                jnp.where(
                    entry >= spread(entries - second_count, head_rows),
                    entry + spread(second - (entries - 1), head_rows),
                    nothing,
                ),
            )
            code = (jnp.where(r < kv_rows, code, nothing) + half).reshape(group * head_rows, block)
            pick = jnp.concatenate([one_hot(code == rows), one_hot(code == rows + other_half)], axis=1)
            got = jnp.dot(pick, kv, preferred_element_type=jnp.float32).reshape(group, head_rows, head)
            tail = got[:, head_rows - 8 :, :] + extra[None]
            got = jnp.concatenate([got[:, : head_rows - 8, :], tail], axis=1)
            out_ref[t : t + group, :head_rows, :] = got.astype(jnp.bfloat16)
            got = jnp.dot(heads, both[core], preferred_element_type=jnp.float32).astype(jnp.bfloat16)
            out_ref[t : t + group, head_rows : head_rows + 8, :] = got[:, :head].reshape(group, 8, head)
            out_ref[t : t + group, head_rows + 8 :, :] = got[:, head:].reshape(group, 8, head)
            at = pl.ds(t, group)
            sends.append(pltpu.make_async_copy(out_ref.at[at], out_hbm.at[at], sems.at[6 + len(sends)]))
            sends[-1].start()
    for send in sends:
        send.wait()


def spread_lanes(plan, width):
    chip = lax.broadcasted_iota(jnp.int32, (block, 64 * width), 0) * width
    lane = lax.broadcasted_iota(jnp.int32, (block, 64 * width), 1)
    return jnp.dot(plan, one_hot((lane >= chip) & (lane < chip + width)), preferred_element_type=jnp.float32)


def unpack_kernel(
    place_ref, plan_ref, got_ref, out_hbm, dq_hbm, dkv_hbm, out_ref, dq_ref, dkv_ref, sems
):
    moves = [
        pltpu.make_async_copy(src, dst, sems.at[i])
        for i, (src, dst) in enumerate([(out_ref, out_hbm), (dq_ref, dq_hbm), (dkv_ref, dkv_hbm)])
    ]
    rows_down = down(place_ref[...] >> 7)
    plan = plan_ref[...].astype(jnp.float32)
    lane = lax.broadcasted_iota(jnp.int32, (8, block), 1)
    lines = [plan[0:1], plan[1:2]]
    lines = lines + [pltpu.roll(plan, 64, 1)[i : i + 1] for i in range(2)]
    lines.append(lane[0:1].astype(jnp.float32))
    stacked = jnp.zeros((16, block), jnp.float32)
    row = lax.broadcasted_iota(jnp.int32, (16, block), 0)
    for i, line in enumerate(lines):
        stacked = jnp.where((row == i) & (lane[0:1] < 64), line, stacked)
    stacked = stacked.astype(jnp.bfloat16)
    wide = spread_lanes(stacked, 8)
    j = lax.broadcasted_iota(jnp.int32, (1, 512), 1) & 7
    code = jnp.where(j < 4, wide[0:1], wide[2:3])
    rows_wide = jnp.concatenate([rows_down] * 4, axis=1)
    picks = [one_hot(jnp.where((j & 3) == h, code, float(nothing)) == rows_wide) for h in range(4)]
    for core in range(2):
        both = jnp.concatenate(
            [
                got_ref[core * 64 : core * 64 + 64, head_rows : head_rows + 8, :].reshape(512, head),
                got_ref[core * 64 : core * 64 + 64, head_rows + 8 :, :].reshape(512, head),
            ],
            axis=1,
        )
        for h in range(4):
            got = jnp.dot(picks[h], both, preferred_element_type=jnp.float32).astype(jnp.bfloat16)
            at = (4 * core + h) * head
            out_ref[:, at : at + head] = got[:, :head]
            dq_ref[:, at : at + head] = got[:, head:]
    moves[0].start()
    moves[1].start()
    wide = spread_lanes(stacked, head_rows)
    first, first_count, second, second_count, chip = [wide[i : i + 1] for i in range(5)]
    r = lax.broadcasted_iota(jnp.int32, (1, 64 * head_rows), 1) - head_rows * chip.astype(jnp.int32)
    sums = [jnp.zeros((block, head), jnp.float32), jnp.zeros((block, head), jnp.float32)]
    rows_wide = jnp.concatenate([rows_down] * (64 * head_rows // block), axis=1)
    for core in range(2):
        entry = ((r & -2) + core).astype(jnp.float32)
        code = jnp.where(
            entry < first_count,
            entry + (first - first_count + 1),
            jnp.where(entry >= entries - second_count, entry + (second - (entries - 1)), float(nothing)),
        )
        code = jnp.where(r < kv_rows, code, float(nothing))
        terms = got_ref[core * 64 : core * 64 + 64, :head_rows, :].reshape(64 * head_rows, head)
        for half in range(2):
            pick = one_hot(jnp.where((r & 1) == half, code, float(nothing)) == rows_wide)
            sums[half] = sums[half] + jnp.dot(pick, terms, preferred_element_type=jnp.float32)
    dkv_ref[...] = jnp.concatenate(sums, axis=1).astype(jnp.bfloat16)
    moves[2].start()
    for move in moves:
        move.wait()


def nt(a, b):
    return lax.dot_general(a, b, (((1,), (1,)), ((), ())), preferred_element_type=jnp.float32)


def tn(a, b):
    return lax.dot_general(a, b, (((0,), (0,)), ((), ())), preferred_element_type=jnp.float32)


def nn(a, b):
    return jnp.dot(a, b, preferred_element_type=jnp.float32)


def split_kernel(got_ref, kv_ref, info_ref, qg_ref):
    for r in range(0, send_rows, 8):
        rows = jnp.transpose(got_ref[:, r : r + 8, :], (1, 0, 2))
        if r < kv_rows:
            n = min(8, kv_rows - r)
            kv_ref[r : r + n] = rows[:n]
            if n < 8:
                info_ref[...] = rows[n]
        else:
            at = (r - head_rows) * block
            qg_ref[at : at + 8 * block, :] = rows.reshape(8 * block, head)


to_exp2 = head ** (-0.5) * 1.4426950408889634


def spans_of(plan_ref, chip):
    first, second = plan_ref[1, chip], plan_ref[1, chip + 64]
    begin = entries - second
    few = second <= 2
    whole = jnp.int32(entries)
    return [
        (0, 6, 0, jnp.int32(0), first, jnp.int32(0), (first + 11) // 12),
        (1, 1, 6, begin, whole, jnp.where(few, begin // 2, pairs), jnp.int32(pairs)),
        (1, 3, 6, begin, whole, jnp.where(few, pairs // 3, begin // 6), jnp.int32(pairs // 3)),
    ]


def rows_of(x):
    return slice(x * 512, (x + 1) * 512), slice(1024 + x * 512, 1536 + x * 512)


def blocks(ref, half, m, n):
    return jnp.concatenate([ref[2 * (m * n + u) + half] for u in range(n)], axis=0)


def slot(m, n, shift):
    return pl.ds(m * n + shift, n)


def flat(x):
    return x.reshape(x.shape[0] * block, 512)


def find_positions(core, chip, mine_len, other_len, plan_ref, info_ref, key_pos, bound):
    stream = chip // 32
    stream_base = (64 * stream).astype(jnp.float32)
    block_row = lax.broadcasted_iota(jnp.int32, (block, block), 0)
    key_pos[...] = info_ref[...].astype(jnp.float32).T + 128.0 * (block_row.astype(jnp.float32) - stream_base)
    for x in range(2):
        pos = key_pos[pl.ds(plan_ref[0, chip + 64 * x], 1), :]
        start = jnp.zeros((1, block), jnp.float32)
        doc_end = jnp.int32(0)
        for i in range(16):
            doc_end = doc_end + stream_length(core, mine_len, other_len, stream, i)
            f = doc_end.astype(jnp.float32)
            start = jnp.where(f <= pos, f, start)
        bound[2 * x : 2 * x + 1] = pos
        bound[2 * x + 1 : 2 * x + 2] = start


def score(x, m, n, low, high, parity, plan_ref, chip, kv_ref, qg, key_pos, bound):
    base = plan_ref[0, chip + 64 * x] - plan_ref[1, chip + 64 * x] + 1 - low
    bias = []
    for u in range(n):
        entry = 2 * (m * n + u) + parity
        valid = (entry >= low) & (entry < high)
        kp = key_pos[pl.ds(jnp.where(valid, base + entry, 0), 1), :]
        kp = jnp.broadcast_to(jnp.where(valid, kp, far), (block, block)).T
        seen = (kp <= bound[2 * x : 2 * x + 1]) & (kp >= bound[2 * x + 1 : 2 * x + 2])
        bias.append(jnp.where(seen, 0.0, masked_score))
    bias = jnp.concatenate(bias, axis=0)
    bias = jnp.concatenate([bias] * 4, axis=1)
    return nt(blocks(kv_ref, 0, m, n), qg[rows_of(x)[0], :]) + bias


def peak_of(s):
    return jnp.max(s.reshape(s.shape[0] // 8, 8, 512), axis=0)


def sum_of(p):
    return jnp.sum(p.reshape(p.shape[0] // 8, 8, 512), axis=0)


def scores_kernel(
    mine_len, other_len, plan_ref, mine_ref, info_ref, qg,
    s_ref, gw_ref, top_ref, key_pos, bound,
):
    core = lax.axis_index("dp")
    chip = lax.axis_index("ctx")
    find_positions(core, chip, mine_len, other_len, plan_ref, info_ref, key_pos, bound)
    top_ref[...] = jnp.full(top_ref.shape, masked_score, jnp.float32)
    for x, n, shift, low, high, begin, end in spans_of(plan_ref, chip):
        cols = slice(x * 512, (x + 1) * 512)

        @pl.loop(begin, end)
        def _(m):
            s = score(x, m, n, low, high, core, plan_ref, chip, mine_ref, qg, key_pos, bound)
            gw = nt(blocks(mine_ref, 1, m, n), qg[rows_of(x)[1], :])
            s_ref[slot(m, n, shift)] = s.reshape(n, block, 512)
            top_ref[:, cols] = jnp.maximum(top_ref[:, cols], peak_of(s))
            gw_ref[slot(m, n, shift)] = gw.reshape(n, block, 512)


def backward(span, p_ref, gw_ref, kv_ref, dot_ref, qs_ref, gs_ref, acc, out_ref):
    x, n, shift, _, _, begin, end = span
    cols = slice(x * 512, (x + 1) * 512)

    @pl.loop(begin, end)
    def _(m):
        at = slot(m, n, shift)
        p = flat(p_ref[at])
        ds = (p.astype(jnp.float32) * (flat(gw_ref[at]) - dot_ref[0:1, cols])).astype(jnp.bfloat16)
        dk = nn(ds, qs_ref[cols, :])
        acc[:, cols] = acc[:, cols] + tn(blocks(kv_ref, 0, m, n), ds)
        dv = nn(p, gs_ref[cols, :])
        for u in range(n):
            for half, value in enumerate((dk, dv)):
                value = value[u * block : (u + 1) * block]
                i = 2 * (m * n + u) + half
                if x == 1:
                    value = value + out_ref[i].astype(jnp.float32)
                out_ref[i] = value.astype(jnp.bfloat16)


def clear_rest(out_ref, end):
    @pl.loop(12 * end, kv_rows)
    def _(i):
        out_ref[i] = jnp.zeros((block, head), jnp.bfloat16)


def turned(x):
    row = lax.broadcasted_iota(jnp.int32, (block, block), 0)
    eye = one_hot(row == lax.broadcasted_iota(jnp.int32, (block, block), 1))
    return jnp.concatenate([nt(eye, x[:, h * block : (h + 1) * block]) for h in range(8)], axis=0)


def weights_kernel(
    plan_ref, mine_ref, other_ref, qg, s_ref, found_ref, key_pos, bound,
    dother_ref, out_ref, p_ref, dot_ref, qs_ref, gs_ref, acc_ref, inv_ref,
    scores, gws, ps, top, total, acc,
):
    core = lax.axis_index("dp")
    chip = lax.axis_index("ctx")
    scale = head ** (-0.5)
    ones = jnp.full((16, block), 1.0, jnp.bfloat16)
    row16 = lax.broadcasted_iota(jnp.int32, (16, 1024), 0)
    spans = spans_of(plan_ref, chip)
    clear_rest(dother_ref, spans[0][-1])
    top[...] = found_ref[...]
    total[...] = jnp.zeros(total.shape, jnp.float32)
    acc[...] = jnp.zeros(acc.shape, jnp.float32)
    for x, n, shift, low, high, begin, end in spans:
        cols = slice(x * 512, (x + 1) * 512)

        @pl.loop(begin, end)
        def _(m):
            s = score(x, m, n, low, high, 1 - core, plan_ref, chip, other_ref, qg, key_pos, bound)
            scores[slot(m, n, shift)] = s.reshape(n, block, 512)
            top[:, cols] = jnp.maximum(top[:, cols], peak_of(s))

    top[...] = jnp.broadcast_to(jnp.max(top[...], axis=0, keepdims=True) * to_exp2, top.shape)
    for x, n, shift, low, high, begin, end in spans:
        cols = slice(x * 512, (x + 1) * 512)

        @pl.loop(begin, end)
        def _(m):
            at = slot(m, n, shift)
            gws[at] = nt(blocks(other_ref, 1, m, n), qg[rows_of(x)[1], :]).reshape(n, block, 512)
            p = jnp.exp2(flat(s_ref[at]) * to_exp2 - top[0:1, cols])
            p_other = jnp.exp2(flat(scores[at]) * to_exp2 - top[0:1, cols])
            total[:, cols] = total[:, cols] + (sum_of(p) + sum_of(p_other))
            p, p_other = p.astype(jnp.bfloat16), p_other.astype(jnp.bfloat16)
            p_ref[at] = p.reshape(n, block, 512)
            ps[at] = p_other.reshape(n, block, 512)
            values = jnp.concatenate([blocks(mine_ref, 1, m, n), blocks(other_ref, 1, m, n)], axis=0)
            acc[:, cols] = acc[:, cols] + tn(values, jnp.concatenate([p, p_other], axis=0))

    inv = 1.0 / jnp.sum(total[...], axis=0, keepdims=True)
    part = inv.astype(jnp.bfloat16).astype(jnp.float32)
    rest = inv - part
    middle = rest.astype(jnp.bfloat16).astype(jnp.float32)
    parts = jnp.where(row16 == 0, part, jnp.where(row16 == 1, middle, jnp.where(row16 == 2, rest - middle, 0.0)))
    inv_down = tn(parts.astype(jnp.bfloat16), ones)
    o = turned((acc[...] * inv).astype(jnp.bfloat16))
    out_ref[...] = o.astype(jnp.bfloat16)
    g = qg[1024:, :].astype(jnp.float32)
    terms = g * o
    part = terms.astype(jnp.bfloat16)
    d = nt(ones, part) + nt(ones, (terms - part.astype(jnp.float32)).astype(jnp.bfloat16))
    dot_ref[...] = d[:8]
    gs_ref[...] = (g * inv_down).astype(jnp.bfloat16)
    qs_ref[...] = (qg[:1024, :].astype(jnp.float32) * (inv_down * scale)).astype(jnp.bfloat16)
    inv_ref[...] = jnp.broadcast_to(inv * scale, inv_ref.shape)
    acc_ref[...] = jnp.zeros(acc_ref.shape, jnp.float32)
    for span in spans:
        backward(span, ps, gws, other_ref, dot_ref, qs_ref, gs_ref, acc_ref, dother_ref)


def grads_kernel(
    plan_ref, mine_ref, gw_ref, p_ref, dot_ref, qs_ref, gs_ref, part_ref, inv_ref,
    dmine_ref, dq_ref,
    acc,
):
    chip = lax.axis_index("ctx")
    spans = spans_of(plan_ref, chip)
    clear_rest(dmine_ref, spans[0][-1])
    acc[...] = part_ref[...]
    for span in spans:
        backward(span, p_ref, gw_ref, mine_ref, dot_ref, qs_ref, gs_ref, acc, dmine_ref)
    dq_ref[...] = turned((acc[...] * inv_ref[0:1]).astype(jnp.bfloat16)).astype(jnp.bfloat16)


def join_kernel(mine_ref, other_ref, out_ref, dq_ref, back_ref):
    def put(r, rows):
        back_ref[:, r : r + 8, :] = jnp.transpose(rows, (1, 0, 2))

    for r in range(0, head_rows, 8):
        n = min(8, kv_rows - r)
        rows = mine_ref[r : r + n].astype(jnp.float32) + other_ref[r : r + n].astype(jnp.float32)
        rows = rows.astype(jnp.bfloat16)
        if n < 8:
            rows = jnp.concatenate([rows, jnp.zeros((8 - n, block, head), jnp.bfloat16)], axis=0)
        put(r, rows)
    put(head_rows, out_ref[...].reshape(8, block, head))
    put(head_rows + 8, dq_ref[...].reshape(8, block, head))


def vmem(n):
    return [pl.BlockSpec(memory_space=pltpu.VMEM)] * n


def smem():
    return pl.BlockSpec(memory_space=pltpu.SMEM)


def params(size):
    return pltpu.CompilerParams(vmem_limit_bytes=size * mib)


def swap(x):
    return lax.ppermute(x, "dp", [(0, 1), (1, 0)])


def exchange(x):
    return lax.all_to_all(x, ("dp", "ctx"), split_axis=0, concat_axis=0, tiled=True)


def kernel(name, body, ins, scalars, outs, scratch, size):
    return pl.pallas_call(
        body,
        out_shape=tuple(jax.ShapeDtypeStruct(shape, dtype) for shape, dtype in outs),
        in_specs=[smem()] * scalars + vmem(len(ins) - scalars),
        out_specs=tuple(vmem(len(outs))),
        scratch_shapes=[pltpu.VMEM(shape, dtype) for shape, dtype in scratch],
        compiler_params=params(size),
        name=name,
    )(*ins)


def attention(lengths, other_lengths, plan, mine, other, info, qg):
    bf16, f32 = jnp.bfloat16, jnp.float32
    slots = (pairs + 6, block, 512)
    rows = ((8, 1024), f32)
    acc = ((head, 1024), f32)
    heads = ((1024, head), bf16)
    places = [((block, block), f32), ((8, block), f32)]
    s, gw, top, key_pos, bound = kernel(
        "scores", scores_kernel, (lengths, other_lengths, plan, mine, info, qg), 3,
        [(slots, f32), (slots, f32), ((8, 1024), f32)] + places, [], 12,
    )
    dother, out, p, dot, qs, gs, partial, inv = kernel(
        "weights", weights_kernel, (plan, mine, other, qg, s, top, key_pos, bound), 1,
        [((kv_rows, block, head), bf16), heads, (slots, bf16), rows, heads, heads, acc, rows],
        [(slots, f32), (slots, f32), (slots, bf16), rows, rows, acc], 24,
    )
    other_terms = swap(dother)
    dmine, dq = kernel(
        "grads", grads_kernel, (plan, mine, gw, p, dot, qs, gs, partial, inv), 1,
        [((kv_rows, block, head), bf16), heads], [acc], 12,
    )
    return dmine, other_terms, out, dq


def on_device(queries, keys_values, grad_out, placement, doc_lengths):
    bf16, f32 = jnp.bfloat16, jnp.float32
    place = placement.reshape(1, block)
    other_lengths = swap(doc_lengths)
    sent, plan = pl.pallas_call(
        pack_kernel,
        out_shape=(
            jax.ShapeDtypeStruct((128, send_rows, head), bf16),
            jax.ShapeDtypeStruct((8, block), jnp.int32),
        ),
        in_specs=[pl.BlockSpec(memory_space=pl.ANY)] * 6,
        out_specs=(pl.BlockSpec(memory_space=pl.ANY), vmem(1)[0]),
        scratch_shapes=[
            pltpu.SMEM((1, 16), jnp.int32),
            pltpu.SMEM((1, 16), jnp.int32),
            pltpu.VMEM((1, block), jnp.int32),
            pltpu.VMEM((block, 8 * head), bf16),
            pltpu.VMEM((block, 2 * head), bf16),
            pltpu.VMEM((block, 8 * head), bf16),
            pltpu.VMEM((128, send_rows, head), bf16),
            pltpu.SemaphoreType.DMA((6 + 128 // group,)),
        ],
        compiler_params=pltpu.CompilerParams(vmem_limit_bytes=58 * mib),
        name="pack",
    )(doc_lengths, other_lengths, place, queries, keys_values, grad_out)
    mine, info, qg = pl.pallas_call(
        split_kernel,
        out_shape=(
            jax.ShapeDtypeStruct((kv_rows, block, head), bf16),
            jax.ShapeDtypeStruct((block, head), bf16),
            jax.ShapeDtypeStruct((2048, head), bf16),
        ),
        in_specs=vmem(1),
        out_specs=tuple(vmem(3)),
        compiler_params=params(24),
        name="split",
    )(exchange(sent))
    dmine, dother, out, dq = attention(doc_lengths, other_lengths, plan, mine, swap(mine), info, qg)
    back = pl.pallas_call(
        join_kernel,
        out_shape=jax.ShapeDtypeStruct((128, send_rows, head), bf16),
        in_specs=vmem(4),
        out_specs=vmem(1)[0],
        compiler_params=params(24),
        name="join",
    )(dmine, dother, out, dq)
    returned = exchange(back)
    return pl.pallas_call(
        unpack_kernel,
        out_shape=(
            jax.ShapeDtypeStruct((block, 8 * head), bf16),
            jax.ShapeDtypeStruct((block, 8 * head), bf16),
            jax.ShapeDtypeStruct((block, 2 * head), bf16),
        ),
        in_specs=vmem(3),
        out_specs=tuple([pl.BlockSpec(memory_space=pl.ANY)] * 3),
        scratch_shapes=[
            pltpu.VMEM((block, 8 * head), bf16),
            pltpu.VMEM((block, 8 * head), bf16),
            pltpu.VMEM((block, 2 * head), bf16),
            pltpu.SemaphoreType.DMA((3,)),
        ],
        compiler_params=params(24),
        name="unpack",
    )(place, plan, returned)


def solution(mesh):
    rows = P(("dp", "ctx"), None)
    return jax.shard_map(
        on_device,
        mesh=mesh,
        in_specs=(rows, rows, rows, P(("dp", "ctx")), P("dp", None)),
        out_specs=(rows, rows, rows),
        check_vma=False,
    )
```

```python
import jax
import jax.numpy as jnp
from jax import lax
from jax.experimental import pallas as pl
from jax.experimental.pallas import tpu as pltpu
from jax.sharding import PartitionSpec as P

block = 128
head = 128
entries = 36
pairs = entries // 2
kv_rows = 2 * pairs
head_rows = 40
send_rows = 56
group = 16
other_half = 1000
nothing = -100000
masked_score = -1e30
far = 1e9
mib = 1024 * 1024


def one_hot(mask):
    return jnp.where(mask, 1.0, 0.0).astype(jnp.bfloat16)


def down(line):
    return jnp.broadcast_to(line.astype(jnp.float32), (block, block)).T


def stream_length(core, mine_ref, other_ref, stream, i):
    return jnp.where(core == stream, mine_ref[0, i], other_ref[0, i])


def make_plan(core, mine_ref, other_ref):
    lane = lax.broadcasted_iota(jnp.int32, (1, block), 1)
    pos = (lane & 63) * block
    start = jnp.zeros((1, block), jnp.int32)
    end0, end1 = jnp.int32(0), jnp.int32(0)
    for i in range(16):
        end0 = end0 + stream_length(core, mine_ref, other_ref, 0, i)
        end1 = end1 + stream_length(core, mine_ref, other_ref, 1, i)
        end = jnp.where(lane < 64, end0, end1)
        start = jnp.where(end <= pos, end, start)
    count = (lane & 63) - (start >> 7) + 1
    key = count * 64 + (lane & 63)
    row = lax.broadcasted_iota(jnp.int32, (block, block), 0)
    col = lax.broadcasted_iota(jnp.int32, (block, block), 1)
    above = (down(key) > key.astype(jnp.float32)) & ((row >> 6) == (col >> 6))
    rank = jnp.sum(jnp.where(above, 1.0, 0.0), axis=0, keepdims=True).astype(jnp.int32)
    seat = jnp.where(rank < 32, rank, 63 - rank) + 32 * (lane >> 6) + jnp.where(rank < 32, 0, 64)
    here = down(seat) == col.astype(jnp.float32)
    block_line = jnp.sum(jnp.where(here, row.astype(jnp.float32), 0.0), axis=0, keepdims=True)
    count_line = jnp.sum(jnp.where(here, down(count), 0.0), axis=0, keepdims=True)
    return block_line, count_line


def slots_kernel(place_ref, line_ref):
    lane = lax.broadcasted_iota(jnp.int32, (block, block), 1).astype(jnp.float32)
    slots_down = down(place_ref[...] & (block - 1))
    line = jnp.sum(jnp.where(down(place_ref[...] >> 7) == lane, slots_down, 0.0), axis=0, keepdims=True)
    line_ref[...] = jnp.broadcast_to(line, (8, block))


def pack_kernel(mine_ref, other_ref, place_ref, line_ref, q_ref, kv_ref, g_ref, out_ref, plan_ref):
    block_line, count_line = make_plan(lax.axis_index("dp"), mine_ref, other_ref)
    row8 = lax.broadcasted_iota(jnp.int32, (8, block), 0)
    plan_ref[...] = jnp.where(row8 == 0, block_line, jnp.where(row8 == 1, count_line, 0.0)).astype(jnp.int32)
    block_down = down(block_line).astype(jnp.int32)
    count_down = down(count_line).astype(jnp.int32)
    rows = place_ref[...] >> 7
    slot_line = line_ref[0:1]
    extra = jnp.where(row8 == kv_rows % 8, slot_line, 0.0)
    kv = jnp.concatenate([kv_ref[:, :head], kv_ref[:, head:]], axis=0)
    r = lax.broadcasted_iota(jnp.int32, (group, head_rows, block), 1)
    half = (r & 1) * other_half
    j = lax.broadcasted_iota(jnp.int32, (group, 8, block), 1)
    both = []
    for core in range(2):
        heads = [slice((4 * core + h) * head, (4 * core + h + 1) * head) for h in range(4)]
        both.append(jnp.concatenate([jnp.concatenate([q_ref[:, at], g_ref[:, at]], axis=1) for at in heads], axis=0))

    def spread(x, n):
        return jnp.broadcast_to(x[:, None, :], (group, n, block))

    for chip in range(0, 64, group):
        first = block_down[chip : chip + group]
        first_count = count_down[chip : chip + group]
        second = block_down[64 + chip : 64 + chip + group]
        second_count = count_down[64 + chip : 64 + chip + group]
        wanted = jnp.where(j < 4, spread(first, 8), spread(second, 8)) == rows[None]
        heads = jnp.concatenate(
            [one_hot(wanted & ((j & 3) == h)).reshape(group * 8, block) for h in range(4)], axis=1
        )
        for core in range(2):
            t = core * 64 + chip
            entry = (r & -2) + core
            code = jnp.where(
                entry < spread(first_count, head_rows),
                entry + spread(first - first_count + 1, head_rows),
                jnp.where(
                    entry >= spread(entries - second_count, head_rows),
                    entry + spread(second - (entries - 1), head_rows),
                    nothing,
                ),
            )
            code = (jnp.where(r < kv_rows, code, nothing) + half).reshape(group * head_rows, block)
            pick = jnp.concatenate([one_hot(code == rows), one_hot(code == rows + other_half)], axis=1)
            got = jnp.dot(pick, kv, preferred_element_type=jnp.float32).reshape(group, head_rows, head)
            tail = got[:, head_rows - 8 :, :] + extra[None]
            got = jnp.concatenate([got[:, : head_rows - 8, :], tail], axis=1)
            out_ref[t : t + group, :head_rows, :] = got.astype(jnp.bfloat16)
            got = jnp.dot(heads, both[core], preferred_element_type=jnp.float32).astype(jnp.bfloat16)
            out_ref[t : t + group, head_rows : head_rows + 8, :] = got[:, :head].reshape(group, 8, head)
            out_ref[t : t + group, head_rows + 8 :, :] = got[:, head:].reshape(group, 8, head)


def spread_lanes(plan, width):
    chip = lax.broadcasted_iota(jnp.int32, (block, 64 * width), 0) * width
    lane = lax.broadcasted_iota(jnp.int32, (block, 64 * width), 1)
    return jnp.dot(plan, one_hot((lane >= chip) & (lane < chip + width)), preferred_element_type=jnp.float32)


def unpack_kernel(
    place_ref, plan_ref, got_ref, out_hbm, dq_hbm, dkv_hbm, out_ref, dq_ref, dkv_ref, sems
):
    moves = [
        pltpu.make_async_copy(src, dst, sems.at[i])
        for i, (src, dst) in enumerate([(out_ref, out_hbm), (dq_ref, dq_hbm), (dkv_ref, dkv_hbm)])
    ]
    rows_down = down(place_ref[...] >> 7)
    plan = plan_ref[...].astype(jnp.float32)
    lane = lax.broadcasted_iota(jnp.int32, (8, block), 1)
    lines = [plan[0:1], plan[1:2]]
    lines = lines + [pltpu.roll(plan, 64, 1)[i : i + 1] for i in range(2)]
    lines.append(lane[0:1].astype(jnp.float32))
    stacked = jnp.zeros((16, block), jnp.float32)
    row = lax.broadcasted_iota(jnp.int32, (16, block), 0)
    for i, line in enumerate(lines):
        stacked = jnp.where((row == i) & (lane[0:1] < 64), line, stacked)
    stacked = stacked.astype(jnp.bfloat16)
    wide = spread_lanes(stacked, 8)
    j = lax.broadcasted_iota(jnp.int32, (1, 512), 1) & 7
    code = jnp.where(j < 4, wide[0:1], wide[2:3])
    rows_wide = jnp.concatenate([rows_down] * 4, axis=1)
    picks = [one_hot(jnp.where((j & 3) == h, code, float(nothing)) == rows_wide) for h in range(4)]
    for core in range(2):
        both = jnp.concatenate(
            [
                got_ref[core * 64 : core * 64 + 64, head_rows : head_rows + 8, :].reshape(512, head),
                got_ref[core * 64 : core * 64 + 64, head_rows + 8 :, :].reshape(512, head),
            ],
            axis=1,
        )
        for h in range(4):
            got = jnp.dot(picks[h], both, preferred_element_type=jnp.float32).astype(jnp.bfloat16)
            at = (4 * core + h) * head
            out_ref[:, at : at + head] = got[:, :head]
            dq_ref[:, at : at + head] = got[:, head:]
    moves[0].start()
    moves[1].start()
    wide = spread_lanes(stacked, head_rows)
    first, first_count, second, second_count, chip = [wide[i : i + 1] for i in range(5)]
    r = lax.broadcasted_iota(jnp.int32, (1, 64 * head_rows), 1) - head_rows * chip.astype(jnp.int32)
    sums = [jnp.zeros((block, head), jnp.float32), jnp.zeros((block, head), jnp.float32)]
    rows_wide = jnp.concatenate([rows_down] * (64 * head_rows // block), axis=1)
    for core in range(2):
        entry = ((r & -2) + core).astype(jnp.float32)
        code = jnp.where(
            entry < first_count,
            entry + (first - first_count + 1),
            jnp.where(entry >= entries - second_count, entry + (second - (entries - 1)), float(nothing)),
        )
        code = jnp.where(r < kv_rows, code, float(nothing))
        terms = got_ref[core * 64 : core * 64 + 64, :head_rows, :].reshape(64 * head_rows, head)
        for half in range(2):
            pick = one_hot(jnp.where((r & 1) == half, code, float(nothing)) == rows_wide)
            sums[half] = sums[half] + jnp.dot(pick, terms, preferred_element_type=jnp.float32)
    dkv_ref[...] = jnp.concatenate(sums, axis=1).astype(jnp.bfloat16)
    moves[2].start()
    for move in moves:
        move.wait()


def nt(a, b):
    return lax.dot_general(a, b, (((1,), (1,)), ((), ())), preferred_element_type=jnp.float32)


def tn(a, b):
    return lax.dot_general(a, b, (((0,), (0,)), ((), ())), preferred_element_type=jnp.float32)


def nn(a, b):
    return jnp.dot(a, b, preferred_element_type=jnp.float32)


def split_kernel(got_ref, kv_ref, info_ref, qg_ref):
    for r in range(0, send_rows, 8):
        rows = jnp.transpose(got_ref[:, r : r + 8, :], (1, 0, 2))
        if r < kv_rows:
            n = min(8, kv_rows - r)
            kv_ref[r : r + n] = rows[:n]
            if n < 8:
                info_ref[...] = rows[n]
        else:
            at = (r - head_rows) * block
            qg_ref[at : at + 8 * block, :] = rows.reshape(8 * block, head)


to_exp2 = head ** (-0.5) * 1.4426950408889634


def spans_of(plan_ref, chip):
    first, second = plan_ref[1, chip], plan_ref[1, chip + 64]
    begin = entries - second
    few = second <= 2
    whole = jnp.int32(entries)
    return [
        (0, 6, 0, jnp.int32(0), first, jnp.int32(0), (first + 11) // 12),
        (1, 1, 6, begin, whole, jnp.where(few, begin // 2, pairs), jnp.int32(pairs)),
        (1, 3, 6, begin, whole, jnp.where(few, pairs // 3, begin // 6), jnp.int32(pairs // 3)),
    ]


def rows_of(x):
    return slice(x * 512, (x + 1) * 512), slice(1024 + x * 512, 1536 + x * 512)


def blocks(ref, half, m, n):
    return jnp.concatenate([ref[2 * (m * n + u) + half] for u in range(n)], axis=0)


def slot(m, n, shift):
    return pl.ds(m * n + shift, n)


def flat(x):
    return x.reshape(x.shape[0] * block, 512)


def find_positions(core, chip, mine_len, other_len, plan_ref, info_ref, key_pos, bound):
    stream = chip // 32
    stream_base = (64 * stream).astype(jnp.float32)
    block_row = lax.broadcasted_iota(jnp.int32, (block, block), 0)
    key_pos[...] = info_ref[...].astype(jnp.float32).T + 128.0 * (block_row.astype(jnp.float32) - stream_base)
    for x in range(2):
        pos = key_pos[pl.ds(plan_ref[0, chip + 64 * x], 1), :]
        start = jnp.zeros((1, block), jnp.float32)
        doc_end = jnp.int32(0)
        for i in range(16):
            doc_end = doc_end + stream_length(core, mine_len, other_len, stream, i)
            f = doc_end.astype(jnp.float32)
            start = jnp.where(f <= pos, f, start)
        bound[2 * x : 2 * x + 1] = pos
        bound[2 * x + 1 : 2 * x + 2] = start


def score(x, m, n, low, high, parity, plan_ref, chip, kv_ref, qg, key_pos, bound):
    base = plan_ref[0, chip + 64 * x] - plan_ref[1, chip + 64 * x] + 1 - low
    bias = []
    for u in range(n):
        entry = 2 * (m * n + u) + parity
        valid = (entry >= low) & (entry < high)
        kp = key_pos[pl.ds(jnp.where(valid, base + entry, 0), 1), :]
        kp = jnp.broadcast_to(jnp.where(valid, kp, far), (block, block)).T
        seen = (kp <= bound[2 * x : 2 * x + 1]) & (kp >= bound[2 * x + 1 : 2 * x + 2])
        bias.append(jnp.where(seen, 0.0, masked_score))
    bias = jnp.concatenate(bias, axis=0)
    bias = jnp.concatenate([bias] * 4, axis=1)
    return nt(blocks(kv_ref, 0, m, n), qg[rows_of(x)[0], :]) + bias


def peak_of(s):
    return jnp.max(s.reshape(s.shape[0] // 8, 8, 512), axis=0)


def sum_of(p):
    return jnp.sum(p.reshape(p.shape[0] // 8, 8, 512), axis=0)


def scores_kernel(
    mine_len, other_len, plan_ref, mine_ref, info_ref, qg,
    s_ref, gw_ref, top_ref, key_pos, bound,
):
    core = lax.axis_index("dp")
    chip = lax.axis_index("ctx")
    find_positions(core, chip, mine_len, other_len, plan_ref, info_ref, key_pos, bound)
    top_ref[...] = jnp.full(top_ref.shape, masked_score, jnp.float32)
    for x, n, shift, low, high, begin, end in spans_of(plan_ref, chip):
        cols = slice(x * 512, (x + 1) * 512)

        @pl.loop(begin, end)
        def _(m):
            s = score(x, m, n, low, high, core, plan_ref, chip, mine_ref, qg, key_pos, bound)
            gw = nt(blocks(mine_ref, 1, m, n), qg[rows_of(x)[1], :])
            s_ref[slot(m, n, shift)] = s.reshape(n, block, 512)
            top_ref[:, cols] = jnp.maximum(top_ref[:, cols], peak_of(s))
            gw_ref[slot(m, n, shift)] = gw.reshape(n, block, 512)


def backward(span, p_ref, gw_ref, kv_ref, dot_ref, qs_ref, gs_ref, acc, out_ref):
    x, n, shift, _, _, begin, end = span
    cols = slice(x * 512, (x + 1) * 512)

    @pl.loop(begin, end)
    def _(m):
        at = slot(m, n, shift)
        p = flat(p_ref[at])
        ds = (p.astype(jnp.float32) * (flat(gw_ref[at]) - dot_ref[0:1, cols])).astype(jnp.bfloat16)
        dk = nn(ds, qs_ref[cols, :])
        acc[:, cols] = acc[:, cols] + tn(blocks(kv_ref, 0, m, n), ds)
        dv = nn(p, gs_ref[cols, :])
        for u in range(n):
            for half, value in enumerate((dk, dv)):
                value = value[u * block : (u + 1) * block]
                i = 2 * (m * n + u) + half
                if x == 1:
                    value = value + out_ref[i].astype(jnp.float32)
                out_ref[i] = value.astype(jnp.bfloat16)


def clear_rest(out_ref, end):
    @pl.loop(12 * end, kv_rows)
    def _(i):
        out_ref[i] = jnp.zeros((block, head), jnp.bfloat16)


def turned(x):
    row = lax.broadcasted_iota(jnp.int32, (block, block), 0)
    eye = one_hot(row == lax.broadcasted_iota(jnp.int32, (block, block), 1))
    return jnp.concatenate([nt(eye, x[:, h * block : (h + 1) * block]) for h in range(8)], axis=0)


def weights_kernel(
    plan_ref, mine_ref, other_ref, qg, s_ref, found_ref, key_pos, bound,
    dother_ref, out_ref, p_ref, dot_ref, qs_ref, gs_ref, acc_ref, inv_ref,
    scores, gws, ps, top, total, acc,
):
    core = lax.axis_index("dp")
    chip = lax.axis_index("ctx")
    scale = head ** (-0.5)
    ones = jnp.full((16, block), 1.0, jnp.bfloat16)
    row16 = lax.broadcasted_iota(jnp.int32, (16, 1024), 0)
    spans = spans_of(plan_ref, chip)
    clear_rest(dother_ref, spans[0][-1])
    top[...] = found_ref[...]
    total[...] = jnp.zeros(total.shape, jnp.float32)
    acc[...] = jnp.zeros(acc.shape, jnp.float32)
    for x, n, shift, low, high, begin, end in spans:
        cols = slice(x * 512, (x + 1) * 512)

        @pl.loop(begin, end)
        def _(m):
            s = score(x, m, n, low, high, 1 - core, plan_ref, chip, other_ref, qg, key_pos, bound)
            scores[slot(m, n, shift)] = s.reshape(n, block, 512)
            top[:, cols] = jnp.maximum(top[:, cols], peak_of(s))

    top[...] = jnp.broadcast_to(jnp.max(top[...], axis=0, keepdims=True) * to_exp2, top.shape)
    for x, n, shift, low, high, begin, end in spans:
        cols = slice(x * 512, (x + 1) * 512)

        @pl.loop(begin, end)
        def _(m):
            at = slot(m, n, shift)
            gws[at] = nt(blocks(other_ref, 1, m, n), qg[rows_of(x)[1], :]).reshape(n, block, 512)
            p = jnp.exp2(flat(s_ref[at]) * to_exp2 - top[0:1, cols])
            p_other = jnp.exp2(flat(scores[at]) * to_exp2 - top[0:1, cols])
            total[:, cols] = total[:, cols] + (sum_of(p) + sum_of(p_other))
            p, p_other = p.astype(jnp.bfloat16), p_other.astype(jnp.bfloat16)
            p_ref[at] = p.reshape(n, block, 512)
            ps[at] = p_other.reshape(n, block, 512)
            values = jnp.concatenate([blocks(mine_ref, 1, m, n), blocks(other_ref, 1, m, n)], axis=0)
            acc[:, cols] = acc[:, cols] + tn(values, jnp.concatenate([p, p_other], axis=0))

    inv = 1.0 / jnp.sum(total[...], axis=0, keepdims=True)
    part = inv.astype(jnp.bfloat16).astype(jnp.float32)
    rest = inv - part
    middle = rest.astype(jnp.bfloat16).astype(jnp.float32)
    parts = jnp.where(row16 == 0, part, jnp.where(row16 == 1, middle, jnp.where(row16 == 2, rest - middle, 0.0)))
    inv_down = tn(parts.astype(jnp.bfloat16), ones)
    o = turned((acc[...] * inv).astype(jnp.bfloat16))
    out_ref[...] = o.astype(jnp.bfloat16)
    g = qg[1024:, :].astype(jnp.float32)
    terms = g * o
    part = terms.astype(jnp.bfloat16)
    d = nt(ones, part) + nt(ones, (terms - part.astype(jnp.float32)).astype(jnp.bfloat16))
    dot_ref[...] = d[:8]
    gs_ref[...] = (g * inv_down).astype(jnp.bfloat16)
    qs_ref[...] = (qg[:1024, :].astype(jnp.float32) * (inv_down * scale)).astype(jnp.bfloat16)
    inv_ref[...] = jnp.broadcast_to(inv * scale, inv_ref.shape)
    acc_ref[...] = jnp.zeros(acc_ref.shape, jnp.float32)
    for span in spans:
        backward(span, ps, gws, other_ref, dot_ref, qs_ref, gs_ref, acc_ref, dother_ref)


def grads_kernel(
    plan_ref, mine_ref, gw_ref, p_ref, dot_ref, qs_ref, gs_ref, part_ref, inv_ref,
    dmine_ref, dq_ref,
    acc,
):
    chip = lax.axis_index("ctx")
    spans = spans_of(plan_ref, chip)
    clear_rest(dmine_ref, spans[0][-1])
    acc[...] = part_ref[...]
    for span in spans:
        backward(span, p_ref, gw_ref, mine_ref, dot_ref, qs_ref, gs_ref, acc, dmine_ref)
    dq_ref[...] = turned((acc[...] * inv_ref[0:1]).astype(jnp.bfloat16)).astype(jnp.bfloat16)


def join_kernel(mine_ref, other_ref, out_ref, dq_ref, back_ref):
    def put(r, rows):
        back_ref[:, r : r + 8, :] = jnp.transpose(rows, (1, 0, 2))

    for r in range(0, head_rows, 8):
        n = min(8, kv_rows - r)
        rows = mine_ref[r : r + n].astype(jnp.float32) + other_ref[r : r + n].astype(jnp.float32)
        rows = rows.astype(jnp.bfloat16)
        if n < 8:
            rows = jnp.concatenate([rows, jnp.zeros((8 - n, block, head), jnp.bfloat16)], axis=0)
        put(r, rows)
    put(head_rows, out_ref[...].reshape(8, block, head))
    put(head_rows + 8, dq_ref[...].reshape(8, block, head))


def vmem(n):
    return [pl.BlockSpec(memory_space=pltpu.VMEM)] * n


def smem():
    return pl.BlockSpec(memory_space=pltpu.SMEM)


def params(size):
    return pltpu.CompilerParams(vmem_limit_bytes=size * mib)


def swap(x):
    return lax.ppermute(x, "dp", [(0, 1), (1, 0)])


def exchange(x):
    return lax.all_to_all(x, ("dp", "ctx"), split_axis=0, concat_axis=0, tiled=True)


def kernel(name, body, ins, scalars, outs, scratch, size):
    return pl.pallas_call(
        body,
        out_shape=tuple(jax.ShapeDtypeStruct(shape, dtype) for shape, dtype in outs),
        in_specs=[smem()] * scalars + vmem(len(ins) - scalars),
        out_specs=tuple(vmem(len(outs))),
        scratch_shapes=[pltpu.VMEM(shape, dtype) for shape, dtype in scratch],
        compiler_params=params(size),
        name=name,
    )(*ins)


def attention(lengths, other_lengths, plan, mine, other, info, qg):
    bf16, f32 = jnp.bfloat16, jnp.float32
    slots = (pairs + 6, block, 512)
    rows = ((8, 1024), f32)
    acc = ((head, 1024), f32)
    heads = ((1024, head), bf16)
    places = [((block, block), f32), ((8, block), f32)]
    s, gw, top, key_pos, bound = kernel(
        "scores", scores_kernel, (lengths, other_lengths, plan, mine, info, qg), 3,
        [(slots, f32), (slots, f32), ((8, 1024), f32)] + places, [], 12,
    )
    dother, out, p, dot, qs, gs, partial, inv = kernel(
        "weights", weights_kernel, (plan, mine, other, qg, s, top, key_pos, bound), 1,
        [((kv_rows, block, head), bf16), heads, (slots, bf16), rows, heads, heads, acc, rows],
        [(slots, f32), (slots, f32), (slots, bf16), rows, rows, acc], 24,
    )
    other_terms = swap(dother)
    dmine, dq = kernel(
        "grads", grads_kernel, (plan, mine, gw, p, dot, qs, gs, partial, inv), 1,
        [((kv_rows, block, head), bf16), heads], [acc], 12,
    )
    return dmine, other_terms, out, dq


def on_device(queries, keys_values, grad_out, placement, doc_lengths):
    bf16, f32 = jnp.bfloat16, jnp.float32
    place = placement.reshape(1, block)
    other_lengths = swap(doc_lengths)
    line = pl.pallas_call(
        slots_kernel,
        out_shape=jax.ShapeDtypeStruct((8, block), f32),
        in_specs=vmem(1),
        out_specs=vmem(1)[0],
        compiler_params=params(8),
        cost_estimate=pl.CostEstimate(flops=4 * 10**9, bytes_accessed=0, transcendentals=0),
        name="slots",
    )(place)
    sent, plan = pl.pallas_call(
        pack_kernel,
        out_shape=(
            jax.ShapeDtypeStruct((128, send_rows, head), bf16),
            jax.ShapeDtypeStruct((8, block), jnp.int32),
        ),
        in_specs=[smem()] * 2 + vmem(5),
        out_specs=tuple(vmem(2)),
        compiler_params=params(24),
        name="pack",
    )(doc_lengths, other_lengths, place, line, queries, keys_values, grad_out)
    mine, info, qg = pl.pallas_call(
        split_kernel,
        out_shape=(
            jax.ShapeDtypeStruct((kv_rows, block, head), bf16),
            jax.ShapeDtypeStruct((block, head), bf16),
            jax.ShapeDtypeStruct((2048, head), bf16),
        ),
        in_specs=vmem(1),
        out_specs=tuple(vmem(3)),
        compiler_params=params(24),
        name="split",
    )(exchange(sent))
    dmine, dother, out, dq = attention(doc_lengths, other_lengths, plan, mine, swap(mine), info, qg)
    back = pl.pallas_call(
        join_kernel,
        out_shape=jax.ShapeDtypeStruct((128, send_rows, head), bf16),
        in_specs=vmem(4),
        out_specs=vmem(1)[0],
        compiler_params=params(24),
        name="join",
    )(dmine, dother, out, dq)
    returned = exchange(back)
    return pl.pallas_call(
        unpack_kernel,
        out_shape=(
            jax.ShapeDtypeStruct((block, 8 * head), bf16),
            jax.ShapeDtypeStruct((block, 8 * head), bf16),
            jax.ShapeDtypeStruct((block, 2 * head), bf16),
        ),
        in_specs=vmem(3),
        out_specs=tuple([pl.BlockSpec(memory_space=pl.ANY)] * 3),
        scratch_shapes=[
            pltpu.VMEM((block, 8 * head), bf16),
            pltpu.VMEM((block, 8 * head), bf16),
            pltpu.VMEM((block, 2 * head), bf16),
            pltpu.SemaphoreType.DMA((3,)),
        ],
        compiler_params=params(24),
        name="unpack",
    )(place, plan, returned)


def solution(mesh):
    rows = P(("dp", "ctx"), None)
    return jax.shard_map(
        on_device,
        mesh=mesh,
        in_specs=(rows, rows, rows, P(("dp", "ctx")), P("dp", None)),
        out_specs=(rows, rows, rows),
        check_vma=False,
    )
```

```python
import jax
import jax.numpy as jnp
from jax import lax
from jax.experimental import pallas as pl
from jax.experimental.pallas import tpu as pltpu
from jax.sharding import PartitionSpec as P

block = 128
head = 128
entries = 35
pairs = 18
tiles = 2 * pairs
kv_rows = 4 * pairs
out_rows = kv_rows + 16
send_rows = kv_rows + 32
group = 16
other_half = 1000
nothing = -100000
masked_score = -1e30
far = 1e9
mib = 1024 * 1024


def one_hot(mask):
    return jnp.where(mask, 1.0, 0.0).astype(jnp.bfloat16)


def down(line):
    return jnp.broadcast_to(line.astype(jnp.float32), (block, block)).T


def stream_length(core, mine_ref, other_ref, stream, i):
    return jnp.where(core == stream, mine_ref[0, i], other_ref[0, i])


def make_plan(core, mine_ref, other_ref):
    lane = lax.broadcasted_iota(jnp.int32, (1, block), 1)
    pos = (lane & 63) * block
    start = jnp.zeros((1, block), jnp.int32)
    end0, end1 = jnp.int32(0), jnp.int32(0)
    for i in range(16):
        end0 = end0 + stream_length(core, mine_ref, other_ref, 0, i)
        end1 = end1 + stream_length(core, mine_ref, other_ref, 1, i)
        end = jnp.where(lane < 64, end0, end1)
        start = jnp.where(end <= pos, end, start)
    count = (lane & 63) - (start >> 7) + 1
    key = count * 64 + (lane & 63)
    row = lax.broadcasted_iota(jnp.int32, (block, block), 0)
    col = lax.broadcasted_iota(jnp.int32, (block, block), 1)
    above = (down(key) > key.astype(jnp.float32)) & ((row >> 6) == (col >> 6))
    rank = jnp.sum(jnp.where(above, 1.0, 0.0), axis=0, keepdims=True).astype(jnp.int32)
    seat = jnp.where(rank < 32, rank, 63 - rank) + 32 * (lane >> 6) + jnp.where(rank < 32, 0, 64)
    here = down(seat) == col.astype(jnp.float32)
    block_line = jnp.sum(jnp.where(here, row.astype(jnp.float32), 0.0), axis=0, keepdims=True)
    count_line = jnp.sum(jnp.where(here, down(count), 0.0), axis=0, keepdims=True)
    return block_line, count_line


def slots_kernel(place_ref, line_ref):
    lane = lax.broadcasted_iota(jnp.int32, (block, block), 1).astype(jnp.float32)
    slots_down = down(place_ref[...] & (block - 1))
    line = jnp.sum(jnp.where(down(place_ref[...] >> 7) == lane, slots_down, 0.0), axis=0, keepdims=True)
    line_ref[...] = jnp.broadcast_to(line, (8, block))


def pack_kernel(mine_ref, other_ref, place_ref, line_ref, q_ref, kv_ref, g_ref, out_ref, plan_ref):
    block_line, count_line = make_plan(lax.axis_index("dp"), mine_ref, other_ref)
    row8 = lax.broadcasted_iota(jnp.int32, (8, block), 0)
    plan_ref[...] = jnp.where(row8 == 0, block_line, jnp.where(row8 == 1, count_line, 0.0)).astype(jnp.int32)
    block_down = down(block_line).astype(jnp.int32)
    count_down = down(count_line).astype(jnp.int32)
    rows = place_ref[...] >> 7
    slot_line = line_ref[0:1]
    extra = jnp.where(row8 == 7, slot_line, 0.0)
    kv = jnp.concatenate([kv_ref[:, :head], kv_ref[:, head:]], axis=0)
    r = lax.broadcasted_iota(jnp.int32, (group, kv_rows, block), 1)
    entry = ((r >> 2) << 1) + (r & 1)
    half = ((r >> 1) & 1) * other_half
    j = lax.broadcasted_iota(jnp.int32, (group, 8, block), 1)
    both = []
    for part in range(2):
        heads = [slice((4 * part + h) * head, (4 * part + h + 1) * head) for h in range(4)]
        both.append(jnp.concatenate([jnp.concatenate([q_ref[:, at], g_ref[:, at]], axis=1) for at in heads], axis=0))

    def spread(x, n):
        return jnp.broadcast_to(x[:, None, :], (group, n, block))

    for chip in range(0, 64, group):
        at = slice(chip, chip + group)
        first = block_down[at]
        first_count = count_down[at]
        second = block_down[64 + chip : 64 + chip + group]
        second_count = count_down[64 + chip : 64 + chip + group]
        code = jnp.where(
            entry < spread(first_count, kv_rows),
            entry + spread(first - first_count + 1, kv_rows),
            jnp.where(
                (entry >= spread(entries - second_count, kv_rows)) & (entry < entries),
                entry + spread(second - (entries - 1), kv_rows),
                nothing,
            ),
        )
        code = (code + half).reshape(group * kv_rows, block)
        pick = jnp.concatenate([one_hot(code == rows), one_hot(code == rows + other_half)], axis=1)
        got = jnp.dot(pick, kv, preferred_element_type=jnp.float32).reshape(group, kv_rows, head)
        tail = got[:, kv_rows - 8 :, :] + extra[None]
        got = jnp.concatenate([got[:, : kv_rows - 8, :], tail], axis=1)
        out_ref[at, :kv_rows, :] = got.astype(jnp.bfloat16)
        wanted = jnp.where(j < 4, spread(first, 8), spread(second, 8)) == rows[None]
        heads = jnp.concatenate(
            [one_hot(wanted & ((j & 3) == h)).reshape(group * 8, block) for h in range(4)], axis=1
        )
        for part in range(2):
            got = jnp.dot(heads, both[part], preferred_element_type=jnp.float32).astype(jnp.bfloat16)
            to = kv_rows + 8 * part
            out_ref[at, to : to + 8, :] = got[:, :head].reshape(group, 8, head)
            out_ref[at, to + 16 : to + 24, :] = got[:, head:].reshape(group, 8, head)


def spread_lanes(plan, width):
    chip = lax.broadcasted_iota(jnp.int32, (64, 64 * width), 0) * width
    lane = lax.broadcasted_iota(jnp.int32, (64, 64 * width), 1)
    return jnp.dot(plan, one_hot((lane >= chip) & (lane < chip + width)), preferred_element_type=jnp.float32)


def unpack_kernel(
    place_ref, plan_ref, got_ref, out_hbm, dq_hbm, dkv_hbm, out_ref, dq_ref, dkv_ref, sems
):
    moves = [
        pltpu.make_async_copy(src, dst, sems.at[i])
        for i, (src, dst) in enumerate([(out_ref, out_hbm), (dq_ref, dq_hbm), (dkv_ref, dkv_hbm)])
    ]
    rows_down = down(place_ref[...] >> 7)
    plan = plan_ref[...].astype(jnp.float32)
    lane = lax.broadcasted_iota(jnp.int32, (8, block), 1)
    lines = [plan[0:1], plan[1:2]]
    lines = lines + [pltpu.roll(plan, 64, 1)[i : i + 1] for i in range(2)]
    lines.append(lane[0:1].astype(jnp.float32))
    stacked = jnp.zeros((16, block), jnp.float32)
    row = lax.broadcasted_iota(jnp.int32, (16, block), 0)
    for i, line in enumerate(lines):
        stacked = jnp.where((row == i) & (lane[0:1] < 64), line, stacked)
    stacked = stacked.astype(jnp.bfloat16)[:, :64]
    wide = spread_lanes(stacked, 8)
    j = lax.broadcasted_iota(jnp.int32, (1, 512), 1) & 7
    code = jnp.where(j < 4, wide[0:1], wide[2:3])
    rows_wide = jnp.concatenate([rows_down] * 4, axis=1)
    picks = [one_hot(jnp.where((j & 3) == h, code, float(nothing)) == rows_wide) for h in range(4)]
    for part in range(2):
        to = kv_rows + 8 * part
        both = jnp.concatenate(
            [got_ref[:, to : to + 8, :].reshape(512, head), got_ref[:, to + 16 : to + 24, :].reshape(512, head)],
            axis=1,
        )
        for h in range(4):
            got = jnp.dot(picks[h], both, preferred_element_type=jnp.float32).astype(jnp.bfloat16)
            at = (4 * part + h) * head
            out_ref[:, at : at + head] = got[:, :head]
            dq_ref[:, at : at + head] = got[:, head:]
    moves[0].start()
    moves[1].start()
    wide = spread_lanes(stacked, kv_rows)
    first, first_count, second, second_count, chip = [wide[i : i + 1] for i in range(5)]
    r = lax.broadcasted_iota(jnp.int32, (1, 64 * kv_rows), 1) - kv_rows * chip.astype(jnp.int32)
    rows_wide = jnp.concatenate([rows_down] * (64 * kv_rows // block), axis=1)
    entry = (((r >> 2) << 1) + (r & 1)).astype(jnp.float32)
    code = jnp.where(
        entry < first_count,
        entry + (first - first_count + 1),
        jnp.where(
            (entry >= entries - second_count) & (entry < entries), entry + (second - (entries - 1)), float(nothing)
        ),
    )
    terms = got_ref[:, :kv_rows, :].reshape(64 * kv_rows, head)
    sums = []
    for half in range(2):
        pick = one_hot(jnp.where(((r >> 1) & 1) == half, code, float(nothing)) == rows_wide)
        sums.append(jnp.dot(pick, terms, preferred_element_type=jnp.float32))
    dkv_ref[...] = jnp.concatenate(sums, axis=1).astype(jnp.bfloat16)
    moves[2].start()
    for move in moves:
        move.wait()


def nt(a, b):
    return lax.dot_general(a, b, (((1,), (1,)), ((), ())), preferred_element_type=jnp.float32)


def tn(a, b):
    return lax.dot_general(a, b, (((0,), (0,)), ((), ())), preferred_element_type=jnp.float32)


def nn(a, b):
    return jnp.dot(a, b, preferred_element_type=jnp.float32)


def split_kernel(got_ref, kv_ref, qg_ref):
    for i in range(send_rows // 8):
        rows = jnp.transpose(got_ref[:, 8 * i : 8 * i + 8, :], (1, 0, 2))
        if i < tiles // 4:
            kv_ref[4 * i : 4 * i + 4] = rows.reshape(4, block, head)
        else:
            kind, part = divmod(i - tiles // 4, 2)
            for x in range(2):
                at = 1024 * kind + 512 * x + 256 * part
                qg_ref[at : at + 256, :] = rows[4 * x : 4 * x + 4].reshape(256, head)


to_exp2 = head ** (-0.5) * 1.4426950408889634


def spans_of(plan_ref, chip):
    first, second = plan_ref[1, chip], plan_ref[1, chip + 64]
    begin = entries - second
    few = second <= 3
    whole = jnp.int32(entries)
    return [
        (0, 6, 0, jnp.int32(0), first, jnp.int32(0), (first + 11) // 12),
        (1, 2, 6, begin, whole, jnp.where(few, begin // 4, pairs // 2), jnp.int32(pairs // 2)),
        (1, 3, 6, begin, whole, jnp.where(few, pairs // 3, begin // 6), jnp.int32(pairs // 3)),
    ]


def rows_of(x):
    return slice(x * 512, (x + 1) * 512), slice(1024 + x * 512, 1536 + x * 512)


def blocks(ref, half, m, n):
    return jnp.concatenate([ref[2 * (m * n + u) + half] for u in range(n)], axis=0)


def slot(m, n, shift):
    return pl.ds(m * n + shift, n)


def flat(x):
    return x.reshape(x.shape[0] * block, 512)


def find_positions(chip, kv_ref, key_pos):
    stream_base = (64 * (chip // 32)).astype(jnp.float32)
    block_row = lax.broadcasted_iota(jnp.int32, (block, block), 0)
    slots = kv_ref[tiles - 1][block // 2 :, :].astype(jnp.float32)
    key_pos[...] = jnp.concatenate([slots, slots], axis=0).T + 128.0 * (block_row.astype(jnp.float32) - stream_base)


def find_bounds(core, chip, mine_len, other_len, plan_ref, key_pos, bound):
    for x in range(2):
        pos = key_pos[pl.ds(plan_ref[0, chip + 64 * x], 1), :]
        start = jnp.zeros((1, block), jnp.float32)
        doc_end = jnp.int32(0)
        for i in range(16):
            doc_end = doc_end + stream_length(core, mine_len, other_len, chip // 32, i)
            f = doc_end.astype(jnp.float32)
            start = jnp.where(f <= pos, f, start)
        bound[2 * x : 2 * x + 1] = pos
        bound[2 * x + 1 : 2 * x + 2] = start


def score(x, m, n, low, high, plan_ref, chip, kv_ref, qg, key_pos, bound):
    base = plan_ref[0, chip + 64 * x] - plan_ref[1, chip + 64 * x] + 1 - low
    lane = lax.broadcasted_iota(jnp.int32, (1, block), 1)
    bias = []
    for u in range(n):
        found = []
        for i in range(2):
            entry = 2 * (m * n + u) + i
            valid = (entry >= low) & (entry < high)
            kp = key_pos[pl.ds(jnp.where(valid, base + entry, 0), 1), :]
            found.append(jnp.where(valid, kp, far))
        kp = jnp.broadcast_to(jnp.where(lane < block // 2, found[0], found[1]), (block, block)).T
        seen = (kp <= bound[2 * x : 2 * x + 1]) & (kp >= bound[2 * x + 1 : 2 * x + 2])
        bias.append(jnp.where(seen, 0.0, masked_score))
    bias = jnp.concatenate(bias, axis=0)
    bias = jnp.concatenate([bias] * 4, axis=1)
    return nt(blocks(kv_ref, 0, m, n), qg[rows_of(x)[0], :]) + bias


def peak_of(s):
    return jnp.max(s.reshape(s.shape[0] // 8, 8, 512), axis=0)


def sum_of(p):
    return jnp.sum(p.reshape(p.shape[0] // 8, 8, 512), axis=0)


def scores_kernel(
    mine_len, other_len, plan_ref, mine_ref, qg,
    s_ref, gw_ref, top_ref, key_pos, bound,
):
    core = lax.axis_index("dp")
    chip = lax.axis_index("ctx")
    find_positions(chip, mine_ref, key_pos)
    find_bounds(core, chip, mine_len, other_len, plan_ref, key_pos, bound)
    top_ref[...] = jnp.full(top_ref.shape, masked_score, jnp.float32)
    for x, n, shift, low, high, begin, end in spans_of(plan_ref, chip):
        cols = slice(x * 512, (x + 1) * 512)

        @pl.loop(begin, end)
        def _(m):
            s = score(x, m, n, low, high, plan_ref, chip, mine_ref, qg, key_pos, bound)
            gw = nt(blocks(mine_ref, 1, m, n), qg[rows_of(x)[1], :])
            s_ref[slot(m, n, shift)] = s.reshape(n, block, 512)
            top_ref[:, cols] = jnp.maximum(top_ref[:, cols], peak_of(s))
            gw_ref[slot(m, n, shift)] = gw.reshape(n, block, 512)


def backward(span, p_ref, gw_ref, kv_ref, dot_ref, qs_ref, gs_ref, acc, out_ref):
    x, n, shift, _, _, begin, end = span
    cols = slice(x * 512, (x + 1) * 512)

    @pl.loop(begin, end)
    def _(m):
        at = slot(m, n, shift)
        p = flat(p_ref[at])
        ds = (p.astype(jnp.float32) * (flat(gw_ref[at]) - dot_ref[0:1, cols])).astype(jnp.bfloat16)
        dk = nn(ds, qs_ref[cols, :])
        acc[:, cols] = acc[:, cols] + tn(blocks(kv_ref, 0, m, n), ds)
        dv = nn(p, gs_ref[cols, :])
        for u in range(n):
            for half, value in enumerate((dk, dv)):
                value = value[u * block : (u + 1) * block]
                i = 2 * (m * n + u) + half
                if x == 1:
                    value = value + out_ref[i].astype(jnp.float32)
                out_ref[i] = value.astype(jnp.bfloat16)


def clear_rest(out_ref, end):
    @pl.loop(12 * end, tiles)
    def _(i):
        out_ref[i] = jnp.zeros((block, head), jnp.bfloat16)


def turned(x):
    row = lax.broadcasted_iota(jnp.int32, (block, block), 0)
    eye = one_hot(row == lax.broadcasted_iota(jnp.int32, (block, block), 1))
    return jnp.concatenate([nt(eye, x[:, h * block : (h + 1) * block]) for h in range(8)], axis=0)


def weights_kernel(
    plan_ref, mine_ref, other_ref, qg, s_ref, found_ref, bound,
    dother_ref, out_ref, p_ref, dot_ref, qs_ref, gs_ref, acc_ref, inv_ref,
    scores, gws, ps, top, total, acc, key_pos,
):
    chip = lax.axis_index("ctx")
    find_positions(chip, other_ref, key_pos)
    scale = head ** (-0.5)
    ones = jnp.full((16, block), 1.0, jnp.bfloat16)
    row16 = lax.broadcasted_iota(jnp.int32, (16, 1024), 0)
    spans = spans_of(plan_ref, chip)
    clear_rest(dother_ref, spans[0][-1])
    top[...] = found_ref[...]
    total[...] = jnp.zeros(total.shape, jnp.float32)
    acc[...] = jnp.zeros(acc.shape, jnp.float32)
    for x, n, shift, low, high, begin, end in spans:
        cols = slice(x * 512, (x + 1) * 512)

        @pl.loop(begin, end)
        def _(m):
            s = score(x, m, n, low, high, plan_ref, chip, other_ref, qg, key_pos, bound)
            scores[slot(m, n, shift)] = s.reshape(n, block, 512)
            top[:, cols] = jnp.maximum(top[:, cols], peak_of(s))

    top[...] = jnp.broadcast_to(jnp.max(top[...], axis=0, keepdims=True) * to_exp2, top.shape)
    for x, n, shift, low, high, begin, end in spans:
        cols = slice(x * 512, (x + 1) * 512)

        @pl.loop(begin, end)
        def _(m):
            at = slot(m, n, shift)
            gws[at] = nt(blocks(other_ref, 1, m, n), qg[rows_of(x)[1], :]).reshape(n, block, 512)
            p = jnp.exp2(flat(s_ref[at]) * to_exp2 - top[0:1, cols])
            p_other = jnp.exp2(flat(scores[at]) * to_exp2 - top[0:1, cols])
            total[:, cols] = total[:, cols] + (sum_of(p) + sum_of(p_other))
            p, p_other = p.astype(jnp.bfloat16), p_other.astype(jnp.bfloat16)
            p_ref[at] = p.reshape(n, block, 512)
            ps[at] = p_other.reshape(n, block, 512)
            values = jnp.concatenate([blocks(mine_ref, 1, m, n), blocks(other_ref, 1, m, n)], axis=0)
            acc[:, cols] = acc[:, cols] + tn(values, jnp.concatenate([p, p_other], axis=0))

    inv = 1.0 / jnp.sum(total[...], axis=0, keepdims=True)
    part = inv.astype(jnp.bfloat16).astype(jnp.float32)
    rest = inv - part
    middle = rest.astype(jnp.bfloat16).astype(jnp.float32)
    parts = jnp.where(row16 == 0, part, jnp.where(row16 == 1, middle, jnp.where(row16 == 2, rest - middle, 0.0)))
    inv_down = tn(parts.astype(jnp.bfloat16), ones)
    o = turned((acc[...] * inv).astype(jnp.bfloat16))
    out_ref[...] = o.astype(jnp.bfloat16)
    g = qg[1024:, :].astype(jnp.float32)
    terms = g * o
    part = terms.astype(jnp.bfloat16)
    d = nt(ones, part) + nt(ones, (terms - part.astype(jnp.float32)).astype(jnp.bfloat16))
    dot_ref[...] = d[:8]
    gs_ref[...] = (g * inv_down).astype(jnp.bfloat16)
    qs_ref[...] = (qg[:1024, :].astype(jnp.float32) * (inv_down * scale)).astype(jnp.bfloat16)
    inv_ref[...] = jnp.broadcast_to(inv * scale, inv_ref.shape)
    acc_ref[...] = jnp.zeros(acc_ref.shape, jnp.float32)
    for span in spans:
        backward(span, ps, gws, other_ref, dot_ref, qs_ref, gs_ref, acc_ref, dother_ref)


def grads_kernel(
    plan_ref, mine_ref, gw_ref, p_ref, dot_ref, qs_ref, gs_ref, part_ref, inv_ref,
    dmine_ref, dq_ref,
    acc,
):
    chip = lax.axis_index("ctx")
    spans = spans_of(plan_ref, chip)
    clear_rest(dmine_ref, spans[0][-1])
    acc[...] = part_ref[...]
    for span in spans:
        backward(span, p_ref, gw_ref, mine_ref, dot_ref, qs_ref, gs_ref, acc, dmine_ref)
    dq_ref[...] = turned((acc[...] * inv_ref[0:1]).astype(jnp.bfloat16)).astype(jnp.bfloat16)


def join_kernel(mine_ref, other_ref, out_ref, dq_ref, back_ref):
    def put(i, rows):
        back_ref[:, 8 * i : 8 * i + 8, :] = jnp.transpose(rows, (1, 0, 2))

    for i in range(tiles // 4):
        at = slice(4 * i, 4 * i + 4)
        rows = mine_ref[at].astype(jnp.float32) + other_ref[at].astype(jnp.float32)
        put(i, rows.astype(jnp.bfloat16).reshape(8, block // 2, head))
    for kind, ref in enumerate((out_ref, dq_ref)):
        for part in range(2):
            at = [512 * x + 256 * part for x in range(2)]
            rows = jnp.concatenate([ref[i : i + 256, :].reshape(4, block // 2, head) for i in at], axis=0)
            put(tiles // 4 + 2 * kind + part, rows)


def vmem(n):
    return [pl.BlockSpec(memory_space=pltpu.VMEM)] * n


def smem():
    return pl.BlockSpec(memory_space=pltpu.SMEM)


def params(size):
    return pltpu.CompilerParams(vmem_limit_bytes=size * mib)


def swap(x):
    return lax.ppermute(x, "dp", [(0, 1), (1, 0)])


def exchange(x):
    return lax.all_to_all(x, "ctx", split_axis=0, concat_axis=0, tiled=True)


def kernel(name, body, ins, scalars, outs, scratch, size):
    return pl.pallas_call(
        body,
        out_shape=tuple(jax.ShapeDtypeStruct(shape, dtype) for shape, dtype in outs),
        in_specs=[smem()] * scalars + vmem(len(ins) - scalars),
        out_specs=tuple(vmem(len(outs))),
        scratch_shapes=[pltpu.VMEM(shape, dtype) for shape, dtype in scratch],
        compiler_params=params(size),
        name=name,
    )(*ins)


def attention(lengths, other_lengths, plan, mine, other, qg):
    bf16, f32 = jnp.bfloat16, jnp.float32
    slots = (pairs + 6, block, 512)
    rows = ((8, 1024), f32)
    acc = ((head, 1024), f32)
    heads = ((1024, head), bf16)
    places = [((block, block), f32), ((8, block), f32)]
    s, gw, top, _, bound = kernel(
        "scores", scores_kernel, (lengths, other_lengths, plan, mine, qg), 3,
        [(slots, f32), (slots, f32), ((8, 1024), f32)] + places, [], 12,
    )
    dother, out, p, dot, qs, gs, partial, inv = kernel(
        "weights", weights_kernel, (plan, mine, other, qg, s, top, bound), 1,
        [((tiles, block, head), bf16), heads, (slots, bf16), rows, heads, heads, acc, rows],
        [(slots, f32), (slots, f32), (slots, bf16), rows, rows, acc, places[0]], 24,
    )
    other_terms = swap(dother)
    dmine, dq = kernel(
        "grads", grads_kernel, (plan, mine, gw, p, dot, qs, gs, partial, inv), 1,
        [((tiles, block, head), bf16), heads], [acc], 12,
    )
    return dmine, other_terms, out, dq


def on_device(queries, keys_values, grad_out, placement, doc_lengths):
    bf16, f32 = jnp.bfloat16, jnp.float32
    place = placement.reshape(1, block)
    other_lengths = swap(doc_lengths)
    line = pl.pallas_call(
        slots_kernel,
        out_shape=jax.ShapeDtypeStruct((8, block), f32),
        in_specs=vmem(1),
        out_specs=vmem(1)[0],
        compiler_params=params(8),
        cost_estimate=pl.CostEstimate(flops=4 * 10**9, bytes_accessed=0, transcendentals=0),
        name="slots",
    )(place)
    sent, plan = pl.pallas_call(
        pack_kernel,
        out_shape=(
            jax.ShapeDtypeStruct((64, send_rows, head), bf16),
            jax.ShapeDtypeStruct((8, block), jnp.int32),
        ),
        in_specs=[smem()] * 2 + vmem(5),
        out_specs=tuple(vmem(2)),
        compiler_params=params(24),
        name="pack",
    )(doc_lengths, other_lengths, place, line, queries, keys_values, grad_out)
    mine, qg = pl.pallas_call(
        split_kernel,
        out_shape=(
            jax.ShapeDtypeStruct((tiles, block, head), bf16),
            jax.ShapeDtypeStruct((2048, head), bf16),
        ),
        in_specs=vmem(1),
        out_specs=tuple(vmem(2)),
        compiler_params=params(24),
        name="split",
    )(exchange(sent))
    dmine, dother, out, dq = attention(doc_lengths, other_lengths, plan, mine, swap(mine), qg)
    back = pl.pallas_call(
        join_kernel,
        out_shape=jax.ShapeDtypeStruct((64, send_rows, head), bf16),
        in_specs=vmem(4),
        out_specs=vmem(1)[0],
        compiler_params=params(24),
        name="join",
    )(dmine, dother, out, dq)
    returned = exchange(back)
    return pl.pallas_call(
        unpack_kernel,
        out_shape=(
            jax.ShapeDtypeStruct((block, 8 * head), bf16),
            jax.ShapeDtypeStruct((block, 8 * head), bf16),
            jax.ShapeDtypeStruct((block, 2 * head), bf16),
        ),
        in_specs=vmem(3),
        out_specs=tuple([pl.BlockSpec(memory_space=pl.ANY)] * 3),
        scratch_shapes=[
            pltpu.VMEM((block, 8 * head), bf16),
            pltpu.VMEM((block, 8 * head), bf16),
            pltpu.VMEM((block, 2 * head), bf16),
            pltpu.SemaphoreType.DMA((3,)),
        ],
        compiler_params=params(24),
        name="unpack",
    )(place, plan, returned)


def solution(mesh):
    rows = P(("dp", "ctx"), None)
    return jax.shard_map(
        on_device,
        mesh=mesh,
        in_specs=(rows, rows, rows, P(("dp", "ctx")), P("dp", None)),
        out_specs=(rows, rows, rows),
        check_vma=False,
    )
```

```python
import jax
import jax.numpy as jnp
from jax import lax
from jax.experimental import pallas as pl
from jax.experimental.pallas import tpu as pltpu
from jax.sharding import PartitionSpec as P

block = 128
head = 128
pairs = 18
tiles = 2 * pairs
kv_rows = 4 * pairs
out_rows = kv_rows + 16
send_rows = kv_rows + 32
group = 16
other_half = 1000
nothing = -100000
masked_score = -1e30
far = 1e9
mib = 1024 * 1024


def second_place(count):
    return 2 * pairs - count - count % 2


def slots_place(count):
    return 2 * pairs - 1 - jnp.where(count % 2 == 0, count, 0)


def one_hot(mask):
    return jnp.where(mask, 1.0, 0.0).astype(jnp.bfloat16)


def down(line):
    return jnp.broadcast_to(line.astype(jnp.float32), (block, block)).T


def stream_length(core, mine_ref, other_ref, stream, i):
    return jnp.where(core == stream, mine_ref[0, i], other_ref[0, i])


def make_plan(core, mine_ref, other_ref):
    lane = lax.broadcasted_iota(jnp.int32, (1, block), 1)
    pos = (lane & 63) * block
    start = jnp.zeros((1, block), jnp.int32)
    end0, end1 = jnp.int32(0), jnp.int32(0)
    for i in range(16):
        end0 = end0 + stream_length(core, mine_ref, other_ref, 0, i)
        end1 = end1 + stream_length(core, mine_ref, other_ref, 1, i)
        end = jnp.where(lane < 64, end0, end1)
        start = jnp.where(end <= pos, end, start)
    count = (lane & 63) - (start >> 7) + 1
    key = count * 64 + (lane & 63)
    row = lax.broadcasted_iota(jnp.int32, (block, block), 0)
    col = lax.broadcasted_iota(jnp.int32, (block, block), 1)
    above = (down(key) > key.astype(jnp.float32)) & ((row >> 6) == (col >> 6))
    rank = jnp.sum(jnp.where(above, 1.0, 0.0), axis=0, keepdims=True).astype(jnp.int32)
    seat = jnp.where(rank < 32, rank, 63 - rank) + 32 * (lane >> 6) + jnp.where(rank < 32, 0, 64)
    here = down(seat) == col.astype(jnp.float32)
    block_line = jnp.sum(jnp.where(here, row.astype(jnp.float32), 0.0), axis=0, keepdims=True)
    count_line = jnp.sum(jnp.where(here, down(count), 0.0), axis=0, keepdims=True)
    return block_line, count_line


def slots_kernel(place_ref, line_ref):
    lane = lax.broadcasted_iota(jnp.int32, (block, block), 1).astype(jnp.float32)
    slots_down = down(place_ref[...] & (block - 1))
    line = jnp.sum(jnp.where(down(place_ref[...] >> 7) == lane, slots_down, 0.0), axis=0, keepdims=True)
    line_ref[...] = jnp.broadcast_to(line, (8, block))


def pack_kernel(mine_ref, other_ref, place_ref, line_ref, q_ref, kv_ref, g_ref, out_ref, plan_ref):
    block_line, count_line = make_plan(lax.axis_index("dp"), mine_ref, other_ref)
    row8 = lax.broadcasted_iota(jnp.int32, (8, block), 0)
    plan_ref[...] = jnp.where(row8 == 0, block_line, jnp.where(row8 == 1, count_line, 0.0)).astype(jnp.int32)
    block_down = down(block_line).astype(jnp.int32)
    count_down = down(count_line).astype(jnp.int32)
    rows = place_ref[...] >> 7
    slot_line = line_ref[0:1]
    kv = jnp.concatenate([kv_ref[:, :head], kv_ref[:, head:]], axis=0)
    r = lax.broadcasted_iota(jnp.int32, (group, kv_rows, block), 1)
    entry = ((r >> 2) << 1) + (r & 1)
    half = ((r >> 1) & 1) * other_half
    odd_values = jnp.where((r & 3) == 3, entry, nothing)
    j = lax.broadcasted_iota(jnp.int32, (group, 8, block), 1)
    both = []
    for part in range(2):
        heads = [slice((4 * part + h) * head, (4 * part + h + 1) * head) for h in range(4)]
        both.append(jnp.concatenate([jnp.concatenate([q_ref[:, at], g_ref[:, at]], axis=1) for at in heads], axis=0))

    def spread(x, n):
        return jnp.broadcast_to(x[:, None, :], (group, n, block))

    for chip in range(0, 64, group):
        at = slice(chip, chip + group)
        first = block_down[at]
        first_count = count_down[at]
        second = block_down[64 + chip : 64 + chip + group]
        second_count = count_down[64 + chip : 64 + chip + group]
        place = second_place(second_count)
        code = jnp.where(
            entry < spread(first_count, kv_rows),
            entry + spread(first - first_count + 1, kv_rows),
            jnp.where(
                (entry >= spread(place, kv_rows)) & (entry < spread(place + second_count, kv_rows)),
                entry + spread(second - second_count + 1 - place, kv_rows),
                nothing,
            ),
        )
        code = (code + half).reshape(group * kv_rows, block)
        pick = jnp.concatenate([one_hot(code == rows), one_hot(code == rows + other_half)], axis=1)
        got = jnp.dot(pick, kv, preferred_element_type=jnp.float32).reshape(group, kv_rows, head)
        got = jnp.where(odd_values == spread(slots_place(second_count), kv_rows), slot_line[None], got)
        out_ref[at, :kv_rows, :] = got.astype(jnp.bfloat16)
        wanted = jnp.where(j < 4, spread(first, 8), spread(second, 8)) == rows[None]
        heads = jnp.concatenate(
            [one_hot(wanted & ((j & 3) == h)).reshape(group * 8, block) for h in range(4)], axis=1
        )
        for part in range(2):
            got = jnp.dot(heads, both[part], preferred_element_type=jnp.float32).astype(jnp.bfloat16)
            to = kv_rows + 8 * part
            out_ref[at, to : to + 8, :] = got[:, :head].reshape(group, 8, head)
            out_ref[at, to + 16 : to + 24, :] = got[:, head:].reshape(group, 8, head)


def spread_lanes(plan, width):
    chip = lax.broadcasted_iota(jnp.int32, (64, 64 * width), 0) * width
    lane = lax.broadcasted_iota(jnp.int32, (64, 64 * width), 1)
    return jnp.dot(plan, one_hot((lane >= chip) & (lane < chip + width)), preferred_element_type=jnp.float32)


def unpack_kernel(
    place_ref, plan_ref, got_ref, out_hbm, dq_hbm, dkv_hbm, out_ref, dq_ref, dkv_ref, sems
):
    moves = [
        pltpu.make_async_copy(src, dst, sems.at[i])
        for i, (src, dst) in enumerate([(out_ref, out_hbm), (dq_ref, dq_hbm), (dkv_ref, dkv_hbm)])
    ]
    rows_down = down(place_ref[...] >> 7)
    plan = plan_ref[...].astype(jnp.float32)
    lane = lax.broadcasted_iota(jnp.int32, (8, block), 1)
    lines = [plan[0:1], plan[1:2]]
    lines = lines + [pltpu.roll(plan, 64, 1)[i : i + 1] for i in range(2)]
    lines.append(lane[0:1].astype(jnp.float32))
    stacked = jnp.zeros((16, block), jnp.float32)
    row = lax.broadcasted_iota(jnp.int32, (16, block), 0)
    for i, line in enumerate(lines):
        stacked = jnp.where((row == i) & (lane[0:1] < 64), line, stacked)
    stacked = stacked.astype(jnp.bfloat16)[:, :64]
    wide = spread_lanes(stacked, 8)
    j = lax.broadcasted_iota(jnp.int32, (1, 512), 1) & 7
    code = jnp.where(j < 4, wide[0:1], wide[2:3])
    rows_wide = jnp.concatenate([rows_down] * 4, axis=1)
    picks = [one_hot(jnp.where((j & 3) == h, code, float(nothing)) == rows_wide) for h in range(4)]
    for part in range(2):
        to = kv_rows + 8 * part
        both = jnp.concatenate(
            [got_ref[:, to : to + 8, :].reshape(512, head), got_ref[:, to + 16 : to + 24, :].reshape(512, head)],
            axis=1,
        )
        for h in range(4):
            got = jnp.dot(picks[h], both, preferred_element_type=jnp.float32).astype(jnp.bfloat16)
            at = (4 * part + h) * head
            out_ref[:, at : at + head] = got[:, :head]
            dq_ref[:, at : at + head] = got[:, head:]
    moves[0].start()
    moves[1].start()
    wide = spread_lanes(stacked, kv_rows)
    first, first_count, second, second_count, chip = [wide[i : i + 1] for i in range(5)]
    r = lax.broadcasted_iota(jnp.int32, (1, 64 * kv_rows), 1) - kv_rows * chip.astype(jnp.int32)
    rows_wide = jnp.concatenate([rows_down] * (64 * kv_rows // block), axis=1)
    entry = (((r >> 2) << 1) + (r & 1)).astype(jnp.float32)
    place = second_place(second_count.astype(jnp.int32)).astype(jnp.float32)
    code = jnp.where(
        entry < first_count,
        entry + (first - first_count + 1),
        jnp.where(
            (entry >= place) & (entry < place + second_count),
            entry + (second - second_count + 1 - place),
            float(nothing),
        ),
    )
    terms = got_ref[:, :kv_rows, :].reshape(64 * kv_rows, head)
    sums = []
    for half in range(2):
        pick = one_hot(jnp.where(((r >> 1) & 1) == half, code, float(nothing)) == rows_wide)
        sums.append(jnp.dot(pick, terms, preferred_element_type=jnp.float32))
    dkv_ref[...] = jnp.concatenate(sums, axis=1).astype(jnp.bfloat16)
    moves[2].start()
    for move in moves:
        move.wait()


def nt(a, b):
    return lax.dot_general(a, b, (((1,), (1,)), ((), ())), preferred_element_type=jnp.float32)


def tn(a, b):
    return lax.dot_general(a, b, (((0,), (0,)), ((), ())), preferred_element_type=jnp.float32)


def nn(a, b):
    return jnp.dot(a, b, preferred_element_type=jnp.float32)


def split_kernel(got_ref, kv_ref, qg_ref):
    for i in range(send_rows // 8):
        rows = jnp.transpose(got_ref[:, 8 * i : 8 * i + 8, :], (1, 0, 2))
        if i < tiles // 4:
            kv_ref[4 * i : 4 * i + 4] = rows.reshape(4, block, head)
        else:
            kind, part = divmod(i - tiles // 4, 2)
            for x in range(2):
                at = 1024 * kind + 512 * x + 256 * part
                qg_ref[at : at + 256, :] = rows[4 * x : 4 * x + 4].reshape(256, head)


to_exp2 = head ** (-0.5) * 1.4426950408889634


def spans_of(plan_ref, chip):
    first, second = plan_ref[1, chip], plan_ref[1, chip + 64]
    begin = second_place(second)
    few = second <= 2
    return [
        (0, 6, 0, jnp.int32(0), first, jnp.int32(0), (first + 11) // 12),
        (1, 1, 6, begin, begin + second, jnp.where(few, begin // 2, pairs), jnp.int32(pairs)),
        (1, 3, 6, begin, begin + second, jnp.where(few, pairs // 3, begin // 6), jnp.int32(pairs // 3)),
    ]


def rows_of(x):
    return slice(x * 512, (x + 1) * 512), slice(1024 + x * 512, 1536 + x * 512)


def blocks(ref, half, m, n):
    return jnp.concatenate([ref[2 * (m * n + u) + half] for u in range(n)], axis=0)


def slot(m, n, shift):
    return pl.ds(m * n + shift, n)


def flat(x):
    return x.reshape(x.shape[0] * block, 512)


def find_positions(chip, plan_ref, kv_ref, key_pos):
    stream_base = (64 * (chip // 32)).astype(jnp.float32)
    block_row = lax.broadcasted_iota(jnp.int32, (block, block), 0)
    slots = kv_ref[slots_place(plan_ref[1, chip + 64])][block // 2 :, :].astype(jnp.float32)
    key_pos[...] = jnp.concatenate([slots, slots], axis=0).T + 128.0 * (block_row.astype(jnp.float32) - stream_base)


def find_bounds(core, chip, mine_len, other_len, plan_ref, key_pos, bound):
    for x in range(2):
        pos = key_pos[pl.ds(plan_ref[0, chip + 64 * x], 1), :]
        start = jnp.zeros((1, block), jnp.float32)
        doc_end = jnp.int32(0)
        for i in range(16):
            doc_end = doc_end + stream_length(core, mine_len, other_len, chip // 32, i)
            f = doc_end.astype(jnp.float32)
            start = jnp.where(f <= pos, f, start)
        bound[2 * x : 2 * x + 1] = pos
        bound[2 * x + 1 : 2 * x + 2] = start


def score(x, m, n, low, high, plan_ref, chip, kv_ref, qg, key_pos, bound):
    base = plan_ref[0, chip + 64 * x] - plan_ref[1, chip + 64 * x] + 1 - low
    lane = lax.broadcasted_iota(jnp.int32, (1, block), 1)
    bias = []
    for u in range(n):
        found = []
        for i in range(2):
            entry = 2 * (m * n + u) + i
            valid = (entry >= low) & (entry < high)
            kp = key_pos[pl.ds(jnp.where(valid, base + entry, 0), 1), :]
            found.append(jnp.where(valid, kp, far))
        kp = jnp.broadcast_to(jnp.where(lane < block // 2, found[0], found[1]), (block, block)).T
        seen = (kp <= bound[2 * x : 2 * x + 1]) & (kp >= bound[2 * x + 1 : 2 * x + 2])
        bias.append(jnp.where(seen, 0.0, masked_score))
    bias = jnp.concatenate(bias, axis=0)
    bias = jnp.concatenate([bias] * 4, axis=1)
    return nt(blocks(kv_ref, 0, m, n), qg[rows_of(x)[0], :]) + bias


def peak_of(s):
    return jnp.max(s.reshape(s.shape[0] // 8, 8, 512), axis=0)


def sum_of(p):
    return jnp.sum(p.reshape(p.shape[0] // 8, 8, 512), axis=0)


def scores_kernel(
    mine_len, other_len, plan_ref, mine_ref, qg,
    s_ref, gw_ref, top_ref, bound,
    key_pos,
):
    core = lax.axis_index("dp")
    chip = lax.axis_index("ctx")
    find_positions(chip, plan_ref, mine_ref, key_pos)
    find_bounds(core, chip, mine_len, other_len, plan_ref, key_pos, bound)
    top_ref[...] = jnp.full(top_ref.shape, masked_score, jnp.float32)
    for x, n, shift, low, high, begin, end in spans_of(plan_ref, chip):
        cols = slice(x * 512, (x + 1) * 512)

        @pl.loop(begin, end)
        def _(m):
            s = score(x, m, n, low, high, plan_ref, chip, mine_ref, qg, key_pos, bound)
            gw = nt(blocks(mine_ref, 1, m, n), qg[rows_of(x)[1], :])
            s_ref[slot(m, n, shift)] = s.reshape(n, block, 512)
            top_ref[:, cols] = jnp.maximum(top_ref[:, cols], peak_of(s))
            gw_ref[slot(m, n, shift)] = gw.reshape(n, block, 512)


def backward(span, p_ref, gw_ref, kv_ref, dot_ref, qs_ref, gs_ref, acc, out_ref):
    x, n, shift, _, _, begin, end = span
    cols = slice(x * 512, (x + 1) * 512)

    @pl.loop(begin, end)
    def _(m):
        at = slot(m, n, shift)
        p = flat(p_ref[at])
        ds = (p.astype(jnp.float32) * (flat(gw_ref[at]) - dot_ref[0:1, cols])).astype(jnp.bfloat16)
        dk = nn(ds, qs_ref[cols, :])
        acc[:, cols] = acc[:, cols] + tn(blocks(kv_ref, 0, m, n), ds)
        dv = nn(p, gs_ref[cols, :])
        for u in range(n):
            for half, value in enumerate((dk, dv)):
                value = value[u * block : (u + 1) * block]
                i = 2 * (m * n + u) + half
                if x == 1:
                    value = value + out_ref[i].astype(jnp.float32)
                out_ref[i] = value.astype(jnp.bfloat16)


def clear_rest(out_ref, end):
    @pl.loop(12 * end, tiles)
    def _(i):
        out_ref[i] = jnp.zeros((block, head), jnp.bfloat16)


def turned(x):
    row = lax.broadcasted_iota(jnp.int32, (block, block), 0)
    eye = one_hot(row == lax.broadcasted_iota(jnp.int32, (block, block), 1))
    return jnp.concatenate([nt(eye, x[:, h * block : (h + 1) * block]) for h in range(8)], axis=0)


def weights_kernel(
    plan_ref, mine_ref, other_ref, qg, s_ref, found_ref, bound,
    dother_ref, out_ref, p_ref, dot_ref, qs_ref, gs_ref, acc_ref, inv_ref,
    scores, gws, ps, top, total, acc, key_pos,
):
    chip = lax.axis_index("ctx")
    find_positions(chip, plan_ref, other_ref, key_pos)
    scale = head ** (-0.5)
    ones = jnp.full((16, block), 1.0, jnp.bfloat16)
    row16 = lax.broadcasted_iota(jnp.int32, (16, 1024), 0)
    spans = spans_of(plan_ref, chip)
    clear_rest(dother_ref, spans[0][-1])
    top[...] = found_ref[...]
    total[...] = jnp.zeros(total.shape, jnp.float32)
    acc[...] = jnp.zeros(acc.shape, jnp.float32)
    for x, n, shift, low, high, begin, end in spans:
        cols = slice(x * 512, (x + 1) * 512)

        @pl.loop(begin, end)
        def _(m):
            s = score(x, m, n, low, high, plan_ref, chip, other_ref, qg, key_pos, bound)
            scores[slot(m, n, shift)] = s.reshape(n, block, 512)
            top[:, cols] = jnp.maximum(top[:, cols], peak_of(s))

    top[...] = jnp.broadcast_to(jnp.max(top[...], axis=0, keepdims=True) * to_exp2, top.shape)
    for x, n, shift, low, high, begin, end in spans:
        cols = slice(x * 512, (x + 1) * 512)

        @pl.loop(begin, end)
        def _(m):
            at = slot(m, n, shift)
            gws[at] = nt(blocks(other_ref, 1, m, n), qg[rows_of(x)[1], :]).reshape(n, block, 512)
            p = jnp.exp2(flat(s_ref[at]) * to_exp2 - top[0:1, cols])
            p_other = jnp.exp2(flat(scores[at]) * to_exp2 - top[0:1, cols])
            total[:, cols] = total[:, cols] + (sum_of(p) + sum_of(p_other))
            p, p_other = p.astype(jnp.bfloat16), p_other.astype(jnp.bfloat16)
            p_ref[at] = p.reshape(n, block, 512)
            ps[at] = p_other.reshape(n, block, 512)
            values = jnp.concatenate([blocks(mine_ref, 1, m, n), blocks(other_ref, 1, m, n)], axis=0)
            acc[:, cols] = acc[:, cols] + tn(values, jnp.concatenate([p, p_other], axis=0))

    inv = 1.0 / jnp.sum(total[...], axis=0, keepdims=True)
    part = inv.astype(jnp.bfloat16).astype(jnp.float32)
    rest = inv - part
    middle = rest.astype(jnp.bfloat16).astype(jnp.float32)
    parts = jnp.where(row16 == 0, part, jnp.where(row16 == 1, middle, jnp.where(row16 == 2, rest - middle, 0.0)))
    inv_down = tn(parts.astype(jnp.bfloat16), ones)
    o = turned((acc[...] * inv).astype(jnp.bfloat16))
    out_ref[...] = o.astype(jnp.bfloat16)
    g = qg[1024:, :].astype(jnp.float32)
    terms = g * o
    part = terms.astype(jnp.bfloat16)
    d = nt(ones, part) + nt(ones, (terms - part.astype(jnp.float32)).astype(jnp.bfloat16))
    dot_ref[...] = d[:8]
    gs_ref[...] = (g * inv_down).astype(jnp.bfloat16)
    qs_ref[...] = (qg[:1024, :].astype(jnp.float32) * (inv_down * scale)).astype(jnp.bfloat16)
    inv_ref[...] = jnp.broadcast_to(inv * scale, inv_ref.shape)
    acc_ref[...] = jnp.zeros(acc_ref.shape, jnp.float32)
    for span in spans:
        backward(span, ps, gws, other_ref, dot_ref, qs_ref, gs_ref, acc_ref, dother_ref)


def grads_kernel(
    plan_ref, mine_ref, gw_ref, p_ref, dot_ref, qs_ref, gs_ref, part_ref, inv_ref,
    dmine_ref, dq_ref,
    acc,
):
    chip = lax.axis_index("ctx")
    spans = spans_of(plan_ref, chip)
    clear_rest(dmine_ref, spans[0][-1])
    acc[...] = part_ref[...]
    for span in spans:
        backward(span, p_ref, gw_ref, mine_ref, dot_ref, qs_ref, gs_ref, acc, dmine_ref)
    dq_ref[...] = turned((acc[...] * inv_ref[0:1]).astype(jnp.bfloat16)).astype(jnp.bfloat16)


def join_kernel(mine_ref, other_ref, out_ref, dq_ref, back_ref):
    def put(i, rows):
        back_ref[:, 8 * i : 8 * i + 8, :] = jnp.transpose(rows, (1, 0, 2))

    for i in range(tiles // 4):
        at = slice(4 * i, 4 * i + 4)
        rows = mine_ref[at].astype(jnp.float32) + other_ref[at].astype(jnp.float32)
        put(i, rows.astype(jnp.bfloat16).reshape(8, block // 2, head))
    for kind, ref in enumerate((out_ref, dq_ref)):
        for part in range(2):
            at = [512 * x + 256 * part for x in range(2)]
            rows = jnp.concatenate([ref[i : i + 256, :].reshape(4, block // 2, head) for i in at], axis=0)
            put(tiles // 4 + 2 * kind + part, rows)


def vmem(n):
    return [pl.BlockSpec(memory_space=pltpu.VMEM)] * n


def smem():
    return pl.BlockSpec(memory_space=pltpu.SMEM)


def params(size):
    return pltpu.CompilerParams(vmem_limit_bytes=size * mib)


def swap(x):
    return lax.ppermute(x, "dp", [(0, 1), (1, 0)])


def exchange(x):
    return lax.all_to_all(x, "ctx", split_axis=0, concat_axis=0, tiled=True)


def kernel(name, body, ins, scalars, outs, scratch, size):
    return pl.pallas_call(
        body,
        out_shape=tuple(jax.ShapeDtypeStruct(shape, dtype) for shape, dtype in outs),
        in_specs=[smem()] * scalars + vmem(len(ins) - scalars),
        out_specs=tuple(vmem(len(outs))),
        scratch_shapes=[pltpu.VMEM(shape, dtype) for shape, dtype in scratch],
        compiler_params=params(size),
        name=name,
    )(*ins)


def attention(lengths, other_lengths, plan, mine, other, qg):
    bf16, f32 = jnp.bfloat16, jnp.float32
    slots = (pairs + 6, block, 512)
    rows = ((8, 1024), f32)
    acc = ((head, 1024), f32)
    heads = ((1024, head), bf16)
    table = ((block, block), f32)
    s, gw, top, bound = kernel(
        "scores", scores_kernel, (lengths, other_lengths, plan, mine, qg), 3,
        [(slots, f32), (slots, f32), rows, ((8, block), f32)], [table], 12,
    )
    dother, out, p, dot, qs, gs, partial, inv = kernel(
        "weights", weights_kernel, (plan, mine, other, qg, s, top, bound), 1,
        [((tiles, block, head), bf16), heads, (slots, bf16), rows, heads, heads, acc, rows],
        [(slots, f32), (slots, f32), (slots, bf16), rows, rows, acc, table], 24,
    )
    other_terms = swap(dother)
    dmine, dq = kernel(
        "grads", grads_kernel, (plan, mine, gw, p, dot, qs, gs, partial, inv), 1,
        [((tiles, block, head), bf16), heads], [acc], 12,
    )
    return dmine, other_terms, out, dq


def on_device(queries, keys_values, grad_out, placement, doc_lengths):
    bf16, f32 = jnp.bfloat16, jnp.float32
    place = placement.reshape(1, block)
    other_lengths = swap(doc_lengths)
    line = pl.pallas_call(
        slots_kernel,
        out_shape=jax.ShapeDtypeStruct((8, block), f32),
        in_specs=vmem(1),
        out_specs=vmem(1)[0],
        compiler_params=params(8),
        cost_estimate=pl.CostEstimate(flops=4 * 10**9, bytes_accessed=0, transcendentals=0),
        name="slots",
    )(place)
    sent, plan = pl.pallas_call(
        pack_kernel,
        out_shape=(
            jax.ShapeDtypeStruct((64, send_rows, head), bf16),
            jax.ShapeDtypeStruct((8, block), jnp.int32),
        ),
        in_specs=[smem()] * 2 + vmem(5),
        out_specs=tuple(vmem(2)),
        compiler_params=params(24),
        name="pack",
    )(doc_lengths, other_lengths, place, line, queries, keys_values, grad_out)
    mine, qg = pl.pallas_call(
        split_kernel,
        out_shape=(
            jax.ShapeDtypeStruct((tiles, block, head), bf16),
            jax.ShapeDtypeStruct((2048, head), bf16),
        ),
        in_specs=vmem(1),
        out_specs=tuple(vmem(2)),
        compiler_params=params(24),
        name="split",
    )(exchange(sent))
    dmine, dother, out, dq = attention(doc_lengths, other_lengths, plan, mine, swap(mine), qg)
    back = pl.pallas_call(
        join_kernel,
        out_shape=jax.ShapeDtypeStruct((64, send_rows, head), bf16),
        in_specs=vmem(4),
        out_specs=vmem(1)[0],
        compiler_params=params(24),
        name="join",
    )(dmine, dother, out, dq)
    returned = exchange(back)
    return pl.pallas_call(
        unpack_kernel,
        out_shape=(
            jax.ShapeDtypeStruct((block, 8 * head), bf16),
            jax.ShapeDtypeStruct((block, 8 * head), bf16),
            jax.ShapeDtypeStruct((block, 2 * head), bf16),
        ),
        in_specs=vmem(3),
        out_specs=tuple([pl.BlockSpec(memory_space=pl.ANY)] * 3),
        scratch_shapes=[
            pltpu.VMEM((block, 8 * head), bf16),
            pltpu.VMEM((block, 8 * head), bf16),
            pltpu.VMEM((block, 2 * head), bf16),
            pltpu.SemaphoreType.DMA((3,)),
        ],
        compiler_params=params(24),
        name="unpack",
    )(place, plan, returned)


def solution(mesh):
    rows = P(("dp", "ctx"), None)
    return jax.shard_map(
        on_device,
        mesh=mesh,
        in_specs=(rows, rows, rows, P(("dp", "ctx")), P("dp", None)),
        out_specs=(rows, rows, rows),
        check_vma=False,
    )
```

```python
import jax
import jax.numpy as jnp
from jax import lax
from jax.experimental import pallas as pl
from jax.experimental.pallas import tpu as pltpu
from jax.sharding import PartitionSpec as P

block = 128
head = 128
entries = 36
pairs = entries // 2
kv_rows = 2 * pairs
head_rows = 40
send_rows = 56
group = 16
other_half = 1000
nothing = -100000
masked_score = -1e30
far = 1e9
mib = 1024 * 1024


def one_hot(mask):
    return jnp.where(mask, 1.0, 0.0).astype(jnp.bfloat16)


def down(line):
    return jnp.broadcast_to(line.astype(jnp.float32), (block, block)).T


def stream_length(core, mine_ref, other_ref, stream, i):
    return jnp.where(core == stream, mine_ref[0, i], other_ref[0, i])


def make_plan(core, mine_ref, other_ref):
    lane = lax.broadcasted_iota(jnp.int32, (1, block), 1)
    pos = (lane & 63) * block
    start = jnp.zeros((1, block), jnp.int32)
    end0, end1 = jnp.int32(0), jnp.int32(0)
    for i in range(16):
        end0 = end0 + stream_length(core, mine_ref, other_ref, 0, i)
        end1 = end1 + stream_length(core, mine_ref, other_ref, 1, i)
        end = jnp.where(lane < 64, end0, end1)
        start = jnp.where(end <= pos, end, start)
    count = (lane & 63) - (start >> 7) + 1
    key = count * 64 + (lane & 63)
    row = lax.broadcasted_iota(jnp.int32, (block, block), 0)
    col = lax.broadcasted_iota(jnp.int32, (block, block), 1)
    above = (down(key) > key.astype(jnp.float32)) & ((row >> 6) == (col >> 6))
    rank = jnp.sum(jnp.where(above, 1.0, 0.0), axis=0, keepdims=True).astype(jnp.int32)
    seat = jnp.where(rank < 32, rank, 63 - rank) + 32 * (lane >> 6) + jnp.where(rank < 32, 0, 64)
    here = down(seat) == col.astype(jnp.float32)
    block_line = jnp.sum(jnp.where(here, row.astype(jnp.float32), 0.0), axis=0, keepdims=True)
    count_line = jnp.sum(jnp.where(here, down(count), 0.0), axis=0, keepdims=True)
    return block_line, count_line


def slots_kernel(place_ref, line_ref):
    lane = lax.broadcasted_iota(jnp.int32, (block, block), 1).astype(jnp.float32)
    slots_down = down(place_ref[...] & (block - 1))
    line = jnp.sum(jnp.where(down(place_ref[...] >> 7) == lane, slots_down, 0.0), axis=0, keepdims=True)
    line_ref[...] = jnp.broadcast_to(line, (8, block))


def pack_kernel(mine_ref, other_ref, place_ref, line_ref, q_ref, kv_ref, g_ref, out_ref, plan_ref):
    block_line, count_line = make_plan(lax.axis_index("dp"), mine_ref, other_ref)
    row8 = lax.broadcasted_iota(jnp.int32, (8, block), 0)
    plan_ref[...] = jnp.where(row8 == 0, block_line, jnp.where(row8 == 1, count_line, 0.0)).astype(jnp.int32)
    block_down = down(block_line).astype(jnp.int32)
    count_down = down(count_line).astype(jnp.int32)
    rows = place_ref[...] >> 7
    slot_line = line_ref[0:1]
    extra = jnp.where(row8 == kv_rows % 8, slot_line, 0.0)
    kv = jnp.concatenate([kv_ref[:, :head], kv_ref[:, head:]], axis=0)
    r = lax.broadcasted_iota(jnp.int32, (group, head_rows, block), 1)
    half = (r & 1) * other_half
    j = lax.broadcasted_iota(jnp.int32, (group, 8, block), 1)
    both = []
    for core in range(2):
        heads = [slice((4 * core + h) * head, (4 * core + h + 1) * head) for h in range(4)]
        both.append(jnp.concatenate([jnp.concatenate([q_ref[:, at], g_ref[:, at]], axis=1) for at in heads], axis=0))

    def spread(x, n):
        return jnp.broadcast_to(x[:, None, :], (group, n, block))

    for chip in range(0, 64, group):
        first = block_down[chip : chip + group]
        first_count = count_down[chip : chip + group]
        second = block_down[64 + chip : 64 + chip + group]
        second_count = count_down[64 + chip : 64 + chip + group]
        wanted = jnp.where(j < 4, spread(first, 8), spread(second, 8)) == rows[None]
        heads = jnp.concatenate(
            [one_hot(wanted & ((j & 3) == h)).reshape(group * 8, block) for h in range(4)], axis=1
        )
        for core in range(2):
            t = core * 64 + chip
            entry = (r & -2) + core
            code = jnp.where(
                entry < spread(first_count, head_rows),
                entry + spread(first - first_count + 1, head_rows),
                jnp.where(
                    entry >= spread(entries - second_count, head_rows),
                    entry + spread(second - (entries - 1), head_rows),
                    nothing,
                ),
            )
            code = (jnp.where(r < kv_rows, code, nothing) + half).reshape(group * head_rows, block)
            pick = jnp.concatenate([one_hot(code == rows), one_hot(code == rows + other_half)], axis=1)
            got = jnp.dot(pick, kv, preferred_element_type=jnp.float32).reshape(group, head_rows, head)
            tail = got[:, head_rows - 8 :, :] + extra[None]
            got = jnp.concatenate([got[:, : head_rows - 8, :], tail], axis=1)
            out_ref[t : t + group, :head_rows, :] = got.astype(jnp.bfloat16)
            got = jnp.dot(heads, both[core], preferred_element_type=jnp.float32).astype(jnp.bfloat16)
            out_ref[t : t + group, head_rows : head_rows + 8, :] = got[:, :head].reshape(group, 8, head)
            out_ref[t : t + group, head_rows + 8 :, :] = got[:, head:].reshape(group, 8, head)


def spread_lanes(plan, width):
    chip = lax.broadcasted_iota(jnp.int32, (block, 64 * width), 0) * width
    lane = lax.broadcasted_iota(jnp.int32, (block, 64 * width), 1)
    return jnp.dot(plan, one_hot((lane >= chip) & (lane < chip + width)), preferred_element_type=jnp.float32)


def unpack_kernel(
    place_ref, plan_ref, got_ref, out_hbm, dq_hbm, dkv_hbm, out_ref, dq_ref, dkv_ref, sems
):
    moves = [
        pltpu.make_async_copy(src, dst, sems.at[i])
        for i, (src, dst) in enumerate([(out_ref, out_hbm), (dq_ref, dq_hbm), (dkv_ref, dkv_hbm)])
    ]
    rows_down = down(place_ref[...] >> 7)
    plan = plan_ref[...].astype(jnp.float32)
    lane = lax.broadcasted_iota(jnp.int32, (8, block), 1)
    lines = [plan[0:1], plan[1:2]]
    lines = lines + [pltpu.roll(plan, 64, 1)[i : i + 1] for i in range(2)]
    lines.append(lane[0:1].astype(jnp.float32))
    stacked = jnp.zeros((16, block), jnp.float32)
    row = lax.broadcasted_iota(jnp.int32, (16, block), 0)
    for i, line in enumerate(lines):
        stacked = jnp.where((row == i) & (lane[0:1] < 64), line, stacked)
    stacked = stacked.astype(jnp.bfloat16)
    wide = spread_lanes(stacked, 8)
    j = lax.broadcasted_iota(jnp.int32, (1, 512), 1) & 7
    code = jnp.where(j < 4, wide[0:1], wide[2:3])
    rows_wide = jnp.concatenate([rows_down] * 4, axis=1)
    picks = [one_hot(jnp.where((j & 3) == h, code, float(nothing)) == rows_wide) for h in range(4)]
    for core in range(2):
        both = jnp.concatenate(
            [
                got_ref[core * 64 : core * 64 + 64, head_rows : head_rows + 8, :].reshape(512, head),
                got_ref[core * 64 : core * 64 + 64, head_rows + 8 :, :].reshape(512, head),
            ],
            axis=1,
        )
        for h in range(4):
            got = jnp.dot(picks[h], both, preferred_element_type=jnp.float32).astype(jnp.bfloat16)
            at = (4 * core + h) * head
            out_ref[:, at : at + head] = got[:, :head]
            dq_ref[:, at : at + head] = got[:, head:]
    moves[0].start()
    moves[1].start()
    wide = spread_lanes(stacked, head_rows)
    first, first_count, second, second_count, chip = [wide[i : i + 1] for i in range(5)]
    r = lax.broadcasted_iota(jnp.int32, (1, 64 * head_rows), 1) - head_rows * chip.astype(jnp.int32)
    sums = [jnp.zeros((block, head), jnp.float32), jnp.zeros((block, head), jnp.float32)]
    rows_wide = jnp.concatenate([rows_down] * (64 * head_rows // block), axis=1)
    for core in range(2):
        entry = ((r & -2) + core).astype(jnp.float32)
        code = jnp.where(
            entry < first_count,
            entry + (first - first_count + 1),
            jnp.where(entry >= entries - second_count, entry + (second - (entries - 1)), float(nothing)),
        )
        code = jnp.where(r < kv_rows, code, float(nothing))
        terms = got_ref[core * 64 : core * 64 + 64, :head_rows, :].reshape(64 * head_rows, head)
        for half in range(2):
            pick = one_hot(jnp.where((r & 1) == half, code, float(nothing)) == rows_wide)
            sums[half] = sums[half] + jnp.dot(pick, terms, preferred_element_type=jnp.float32)
    dkv_ref[...] = jnp.concatenate(sums, axis=1).astype(jnp.bfloat16)
    moves[2].start()
    for move in moves:
        move.wait()


def nt(a, b):
    return lax.dot_general(a, b, (((1,), (1,)), ((), ())), preferred_element_type=jnp.float32)


def tn(a, b):
    return lax.dot_general(a, b, (((0,), (0,)), ((), ())), preferred_element_type=jnp.float32)


def nn(a, b):
    return jnp.dot(a, b, preferred_element_type=jnp.float32)


def split_kernel(got_ref, kv_ref, info_ref, qg_ref):
    for r in range(0, send_rows, 8):
        rows = jnp.transpose(got_ref[:, r : r + 8, :], (1, 0, 2))
        if r < kv_rows:
            n = min(8, kv_rows - r)
            kv_ref[r : r + n] = rows[:n]
            if n < 8:
                info_ref[...] = rows[n]
        else:
            at = (r - head_rows) * block
            qg_ref[at : at + 8 * block, :] = rows.reshape(8 * block, head)


to_exp2 = head ** (-0.5) * 1.4426950408889634


def spans_of(plan_ref, chip):
    first, second = plan_ref[1, chip], plan_ref[1, chip + 64]
    begin = entries - second
    few = second <= 2
    long = first > 24
    whole = jnp.int32(entries)
    return [
        (0, 9, 0, jnp.int32(0), first, jnp.int32(0), jnp.where(long, 2, 0)),
        (0, 6, 0, jnp.int32(0), first, jnp.int32(0), jnp.where(long, 0, (first + 11) // 12)),
        (1, 1, 6, begin, whole, jnp.where(few, begin // 2, pairs), jnp.int32(pairs)),
        (1, 3, 6, begin, whole, jnp.where(few, pairs // 3, begin // 6), jnp.int32(pairs // 3)),
    ]


def rows_of(x):
    return slice(x * 512, (x + 1) * 512), slice(1024 + x * 512, 1536 + x * 512)


def blocks(ref, half, m, n):
    return jnp.concatenate([ref[2 * (m * n + u) + half] for u in range(n)], axis=0)


def slot(m, n, shift):
    return pl.ds(m * n + shift, n)


def flat(x):
    return x.reshape(x.shape[0] * block, 512)


def find_positions(core, chip, mine_len, other_len, plan_ref, info_ref, key_pos, bound):
    stream = chip // 32
    stream_base = (64 * stream).astype(jnp.float32)
    block_row = lax.broadcasted_iota(jnp.int32, (block, block), 0)
    key_pos[...] = info_ref[...].astype(jnp.float32).T + 128.0 * (block_row.astype(jnp.float32) - stream_base)
    for x in range(2):
        pos = key_pos[pl.ds(plan_ref[0, chip + 64 * x], 1), :]
        start = jnp.zeros((1, block), jnp.float32)
        doc_end = jnp.int32(0)
        for i in range(16):
            doc_end = doc_end + stream_length(core, mine_len, other_len, stream, i)
            f = doc_end.astype(jnp.float32)
            start = jnp.where(f <= pos, f, start)
        bound[2 * x : 2 * x + 1] = pos
        bound[2 * x + 1 : 2 * x + 2] = start


def score(x, m, n, low, high, parity, plan_ref, chip, kv_ref, qg, key_pos, bound):
    base = plan_ref[0, chip + 64 * x] - plan_ref[1, chip + 64 * x] + 1 - low
    bias = []
    for u in range(n):
        entry = 2 * (m * n + u) + parity
        valid = (entry >= low) & (entry < high)
        kp = key_pos[pl.ds(jnp.where(valid, base + entry, 0), 1), :]
        kp = jnp.broadcast_to(jnp.where(valid, kp, far), (block, block)).T
        seen = (kp <= bound[2 * x : 2 * x + 1]) & (kp >= bound[2 * x + 1 : 2 * x + 2])
        bias.append(jnp.where(seen, 0.0, masked_score))
    bias = jnp.concatenate(bias, axis=0)
    bias = jnp.concatenate([bias] * 4, axis=1)
    return nt(blocks(kv_ref, 0, m, n), qg[rows_of(x)[0], :]) + bias


def peak_of(s):
    return jnp.max(s.reshape(s.shape[0] // 8, 8, 512), axis=0)


def sum_of(p):
    return jnp.sum(p.reshape(p.shape[0] // 8, 8, 512), axis=0)


def scores_kernel(
    mine_len, other_len, plan_ref, mine_ref, info_ref, qg,
    s_ref, gw_ref, top_ref, key_pos, bound,
):
    core = lax.axis_index("dp")
    chip = lax.axis_index("ctx")
    find_positions(core, chip, mine_len, other_len, plan_ref, info_ref, key_pos, bound)
    top_ref[...] = jnp.full(top_ref.shape, masked_score, jnp.float32)
    for x, n, shift, low, high, begin, end in spans_of(plan_ref, chip):
        cols = slice(x * 512, (x + 1) * 512)

        @pl.loop(begin, end)
        def _(m):
            s = score(x, m, n, low, high, core, plan_ref, chip, mine_ref, qg, key_pos, bound)
            gw = nt(blocks(mine_ref, 1, m, n), qg[rows_of(x)[1], :])
            s_ref[slot(m, n, shift)] = s.reshape(n, block, 512)
            top_ref[:, cols] = jnp.maximum(top_ref[:, cols], peak_of(s))
            gw_ref[slot(m, n, shift)] = gw.reshape(n, block, 512)


def backward(span, p_ref, gw_ref, kv_ref, dot_ref, qs_ref, gs_ref, acc, out_ref):
    x, n, shift, _, _, begin, end = span
    cols = slice(x * 512, (x + 1) * 512)

    @pl.loop(begin, end)
    def _(m):
        at = slot(m, n, shift)
        p = flat(p_ref[at])
        ds = (p.astype(jnp.float32) * (flat(gw_ref[at]) - dot_ref[0:1, cols])).astype(jnp.bfloat16)
        dk = nn(ds, qs_ref[cols, :])
        acc[:, cols] = acc[:, cols] + tn(blocks(kv_ref, 0, m, n), ds)
        dv = nn(p, gs_ref[cols, :])
        for u in range(n):
            for half, value in enumerate((dk, dv)):
                value = value[u * block : (u + 1) * block]
                i = 2 * (m * n + u) + half
                if x == 1:
                    value = value + out_ref[i].astype(jnp.float32)
                out_ref[i] = value.astype(jnp.bfloat16)


def clear_rest(out_ref, spans):
    long, short = spans[0], spans[1]

    @pl.loop(2 * (long[1] * long[-1] + short[1] * short[-1]), kv_rows)
    def _(i):
        out_ref[i] = jnp.zeros((block, head), jnp.bfloat16)


def turned(x):
    row = lax.broadcasted_iota(jnp.int32, (block, block), 0)
    eye = one_hot(row == lax.broadcasted_iota(jnp.int32, (block, block), 1))
    return jnp.concatenate([nt(eye, x[:, h * block : (h + 1) * block]) for h in range(8)], axis=0)


def weights_kernel(
    plan_ref, mine_ref, other_ref, qg, s_ref, found_ref, key_pos, bound,
    dother_ref, out_ref, p_ref, dot_ref, qs_ref, gs_ref, acc_ref, inv_ref,
    scores, gws, ps, top, total, acc,
):
    core = lax.axis_index("dp")
    chip = lax.axis_index("ctx")
    scale = head ** (-0.5)
    ones = jnp.full((16, block), 1.0, jnp.bfloat16)
    row16 = lax.broadcasted_iota(jnp.int32, (16, 1024), 0)
    spans = spans_of(plan_ref, chip)
    clear_rest(dother_ref, spans)
    top[...] = found_ref[...]
    total[...] = jnp.zeros(total.shape, jnp.float32)
    acc[...] = jnp.zeros(acc.shape, jnp.float32)
    for x, n, shift, low, high, begin, end in spans:
        cols = slice(x * 512, (x + 1) * 512)

        @pl.loop(begin, end)
        def _(m):
            s = score(x, m, n, low, high, 1 - core, plan_ref, chip, other_ref, qg, key_pos, bound)
            scores[slot(m, n, shift)] = s.reshape(n, block, 512)
            top[:, cols] = jnp.maximum(top[:, cols], peak_of(s))

    top[...] = jnp.broadcast_to(jnp.max(top[...], axis=0, keepdims=True) * to_exp2, top.shape)
    for x, n, shift, low, high, begin, end in spans:
        cols = slice(x * 512, (x + 1) * 512)

        @pl.loop(begin, end)
        def _(m):
            at = slot(m, n, shift)
            gws[at] = nt(blocks(other_ref, 1, m, n), qg[rows_of(x)[1], :]).reshape(n, block, 512)
            p = jnp.exp2(flat(s_ref[at]) * to_exp2 - top[0:1, cols])
            p_other = jnp.exp2(flat(scores[at]) * to_exp2 - top[0:1, cols])
            total[:, cols] = total[:, cols] + (sum_of(p) + sum_of(p_other))
            p, p_other = p.astype(jnp.bfloat16), p_other.astype(jnp.bfloat16)
            p_ref[at] = p.reshape(n, block, 512)
            ps[at] = p_other.reshape(n, block, 512)
            values = jnp.concatenate([blocks(mine_ref, 1, m, n), blocks(other_ref, 1, m, n)], axis=0)
            acc[:, cols] = acc[:, cols] + tn(values, jnp.concatenate([p, p_other], axis=0))

    inv = 1.0 / jnp.sum(total[...], axis=0, keepdims=True)
    part = inv.astype(jnp.bfloat16).astype(jnp.float32)
    rest = inv - part
    middle = rest.astype(jnp.bfloat16).astype(jnp.float32)
    parts = jnp.where(row16 == 0, part, jnp.where(row16 == 1, middle, jnp.where(row16 == 2, rest - middle, 0.0)))
    inv_down = tn(parts.astype(jnp.bfloat16), ones)
    o = turned((acc[...] * inv).astype(jnp.bfloat16))
    out_ref[...] = o.astype(jnp.bfloat16)
    g = qg[1024:, :].astype(jnp.float32)
    terms = g * o
    part = terms.astype(jnp.bfloat16)
    d = nt(ones, part) + nt(ones, (terms - part.astype(jnp.float32)).astype(jnp.bfloat16))
    dot_ref[...] = d[:8]
    gs_ref[...] = (g * inv_down).astype(jnp.bfloat16)
    qs_ref[...] = (qg[:1024, :].astype(jnp.float32) * (inv_down * scale)).astype(jnp.bfloat16)
    inv_ref[...] = jnp.broadcast_to(inv * scale, inv_ref.shape)
    acc_ref[...] = jnp.zeros(acc_ref.shape, jnp.float32)
    for span in spans:
        backward(span, ps, gws, other_ref, dot_ref, qs_ref, gs_ref, acc_ref, dother_ref)


def grads_kernel(
    plan_ref, mine_ref, gw_ref, p_ref, dot_ref, qs_ref, gs_ref, part_ref, inv_ref,
    dmine_ref, dq_ref,
    acc,
):
    chip = lax.axis_index("ctx")
    spans = spans_of(plan_ref, chip)
    clear_rest(dmine_ref, spans)
    acc[...] = part_ref[...]
    for span in spans:
        backward(span, p_ref, gw_ref, mine_ref, dot_ref, qs_ref, gs_ref, acc, dmine_ref)
    dq_ref[...] = turned((acc[...] * inv_ref[0:1]).astype(jnp.bfloat16)).astype(jnp.bfloat16)


def join_kernel(mine_ref, other_ref, out_ref, dq_ref, back_ref):
    def put(r, rows):
        back_ref[:, r : r + 8, :] = jnp.transpose(rows, (1, 0, 2))

    for r in range(0, head_rows, 8):
        n = min(8, kv_rows - r)
        rows = mine_ref[r : r + n].astype(jnp.float32) + other_ref[r : r + n].astype(jnp.float32)
        rows = rows.astype(jnp.bfloat16)
        if n < 8:
            rows = jnp.concatenate([rows, jnp.zeros((8 - n, block, head), jnp.bfloat16)], axis=0)
        put(r, rows)
    put(head_rows, out_ref[...].reshape(8, block, head))
    put(head_rows + 8, dq_ref[...].reshape(8, block, head))


def vmem(n):
    return [pl.BlockSpec(memory_space=pltpu.VMEM)] * n


def smem():
    return pl.BlockSpec(memory_space=pltpu.SMEM)


def params(size):
    return pltpu.CompilerParams(vmem_limit_bytes=size * mib)


def swap(x):
    return lax.ppermute(x, "dp", [(0, 1), (1, 0)])


def exchange(x):
    return lax.all_to_all(x, ("dp", "ctx"), split_axis=0, concat_axis=0, tiled=True)


def kernel(name, body, ins, scalars, outs, scratch, size):
    return pl.pallas_call(
        body,
        out_shape=tuple(jax.ShapeDtypeStruct(shape, dtype) for shape, dtype in outs),
        in_specs=[smem()] * scalars + vmem(len(ins) - scalars),
        out_specs=tuple(vmem(len(outs))),
        scratch_shapes=[pltpu.VMEM(shape, dtype) for shape, dtype in scratch],
        compiler_params=params(size),
        name=name,
    )(*ins)


def attention(lengths, other_lengths, plan, mine, other, info, qg):
    bf16, f32 = jnp.bfloat16, jnp.float32
    slots = (pairs + 6, block, 512)
    rows = ((8, 1024), f32)
    acc = ((head, 1024), f32)
    heads = ((1024, head), bf16)
    places = [((block, block), f32), ((8, block), f32)]
    s, gw, top, key_pos, bound = kernel(
        "scores", scores_kernel, (lengths, other_lengths, plan, mine, info, qg), 3,
        [(slots, f32), (slots, f32), ((8, 1024), f32)] + places, [], 12,
    )
    dother, out, p, dot, qs, gs, partial, inv = kernel(
        "weights", weights_kernel, (plan, mine, other, qg, s, top, key_pos, bound), 1,
        [((kv_rows, block, head), bf16), heads, (slots, bf16), rows, heads, heads, acc, rows],
        [(slots, f32), (slots, f32), (slots, bf16), rows, rows, acc], 24,
    )
    other_terms = swap(dother)
    dmine, dq = kernel(
        "grads", grads_kernel, (plan, mine, gw, p, dot, qs, gs, partial, inv), 1,
        [((kv_rows, block, head), bf16), heads], [acc], 12,
    )
    return dmine, other_terms, out, dq


def on_device(queries, keys_values, grad_out, placement, doc_lengths):
    bf16, f32 = jnp.bfloat16, jnp.float32
    place = placement.reshape(1, block)
    other_lengths = swap(doc_lengths)
    line = pl.pallas_call(
        slots_kernel,
        out_shape=jax.ShapeDtypeStruct((8, block), f32),
        in_specs=vmem(1),
        out_specs=vmem(1)[0],
        compiler_params=params(8),
        cost_estimate=pl.CostEstimate(flops=4 * 10**9, bytes_accessed=0, transcendentals=0),
        name="slots",
    )(place)
    sent, plan = pl.pallas_call(
        pack_kernel,
        out_shape=(
            jax.ShapeDtypeStruct((128, send_rows, head), bf16),
            jax.ShapeDtypeStruct((8, block), jnp.int32),
        ),
        in_specs=[smem()] * 2 + vmem(5),
        out_specs=tuple(vmem(2)),
        compiler_params=params(24),
        name="pack",
    )(doc_lengths, other_lengths, place, line, queries, keys_values, grad_out)
    mine, info, qg = pl.pallas_call(
        split_kernel,
        out_shape=(
            jax.ShapeDtypeStruct((kv_rows, block, head), bf16),
            jax.ShapeDtypeStruct((block, head), bf16),
            jax.ShapeDtypeStruct((2048, head), bf16),
        ),
        in_specs=vmem(1),
        out_specs=tuple(vmem(3)),
        compiler_params=params(24),
        name="split",
    )(exchange(sent))
    dmine, dother, out, dq = attention(doc_lengths, other_lengths, plan, mine, swap(mine), info, qg)
    back = pl.pallas_call(
        join_kernel,
        out_shape=jax.ShapeDtypeStruct((128, send_rows, head), bf16),
        in_specs=vmem(4),
        out_specs=vmem(1)[0],
        compiler_params=params(24),
        name="join",
    )(dmine, dother, out, dq)
    returned = exchange(back)
    return pl.pallas_call(
        unpack_kernel,
        out_shape=(
            jax.ShapeDtypeStruct((block, 8 * head), bf16),
            jax.ShapeDtypeStruct((block, 8 * head), bf16),
            jax.ShapeDtypeStruct((block, 2 * head), bf16),
        ),
        in_specs=vmem(3),
        out_specs=tuple([pl.BlockSpec(memory_space=pl.ANY)] * 3),
        scratch_shapes=[
            pltpu.VMEM((block, 8 * head), bf16),
            pltpu.VMEM((block, 8 * head), bf16),
            pltpu.VMEM((block, 2 * head), bf16),
            pltpu.SemaphoreType.DMA((3,)),
        ],
        compiler_params=params(24),
        name="unpack",
    )(place, plan, returned)


def solution(mesh):
    rows = P(("dp", "ctx"), None)
    return jax.shard_map(
        on_device,
        mesh=mesh,
        in_specs=(rows, rows, rows, P(("dp", "ctx")), P("dp", None)),
        out_specs=(rows, rows, rows),
        check_vma=False,
    )
```

```python
import jax
import jax.numpy as jnp
from jax import lax
from jax.experimental import pallas as pl
from jax.experimental.pallas import tpu as pltpu
from jax.sharding import PartitionSpec as P

block = 128
head = 128
entries = 36
pairs = entries // 2
kv_rows = 2 * pairs
head_rows = 40
send_rows = 56
group = 16
other_half = 1000
nothing = -100000
masked_score = -1e30
far = 1e9
mib = 1024 * 1024


def one_hot(mask):
    return jnp.where(mask, 1.0, 0.0).astype(jnp.bfloat16)


def down(line):
    return jnp.broadcast_to(line.astype(jnp.float32), (block, block)).T


def stream_length(core, mine_ref, other_ref, stream, i):
    return jnp.where(core == stream, mine_ref[0, i], other_ref[0, i])


def make_plan(core, mine_ref, other_ref):
    lane = lax.broadcasted_iota(jnp.int32, (1, block), 1)
    pos = (lane & 63) * block
    start = jnp.zeros((1, block), jnp.int32)
    end0, end1 = jnp.int32(0), jnp.int32(0)
    for i in range(16):
        end0 = end0 + stream_length(core, mine_ref, other_ref, 0, i)
        end1 = end1 + stream_length(core, mine_ref, other_ref, 1, i)
        end = jnp.where(lane < 64, end0, end1)
        start = jnp.where(end <= pos, end, start)
    count = (lane & 63) - (start >> 7) + 1
    key = count * 64 + (lane & 63)
    row = lax.broadcasted_iota(jnp.int32, (block, block), 0)
    col = lax.broadcasted_iota(jnp.int32, (block, block), 1)
    above = (down(key) > key.astype(jnp.float32)) & ((row >> 6) == (col >> 6))
    rank = jnp.sum(jnp.where(above, 1.0, 0.0), axis=0, keepdims=True).astype(jnp.int32)
    seat = jnp.where(rank < 32, rank, 63 - rank) + 32 * (lane >> 6) + jnp.where(rank < 32, 0, 64)
    here = down(seat) == col.astype(jnp.float32)
    block_line = jnp.sum(jnp.where(here, row.astype(jnp.float32), 0.0), axis=0, keepdims=True)
    count_line = jnp.sum(jnp.where(here, down(count), 0.0), axis=0, keepdims=True)
    return block_line, count_line


def tables_kernel(rows_ref, heads_ref, lane_ref):
    lane_ref[...] = lax.broadcasted_iota(jnp.int32, (block, block), 1).astype(jnp.float32)
    for ref, width in ((rows_ref, head_rows), (heads_ref, 8)):
        chip = lax.broadcasted_iota(jnp.int32, ref.shape, 0) * width
        lane = lax.broadcasted_iota(jnp.int32, ref.shape, 1)
        ref[...] = one_hot((lane >= chip) & (lane < chip + width))


def pack_kernel(mine_ref, other_ref, place_ref, lane_ref, q_ref, kv_ref, g_ref, out_ref, plan_ref):
    block_line, count_line = make_plan(lax.axis_index("dp"), mine_ref, other_ref)
    row8 = lax.broadcasted_iota(jnp.int32, (8, block), 0)
    plan_ref[...] = jnp.where(row8 == 0, block_line, jnp.where(row8 == 1, count_line, 0.0)).astype(jnp.int32)
    block_down = down(block_line).astype(jnp.int32)
    count_down = down(count_line).astype(jnp.int32)
    rows = place_ref[...] >> 7
    slots_down = down(place_ref[...] & (block - 1))
    slot_line = jnp.sum(jnp.where(down(rows) == lane_ref[...], slots_down, 0.0), axis=0, keepdims=True)
    extra = jnp.where(row8 == kv_rows % 8, slot_line, 0.0)
    kv = jnp.concatenate([kv_ref[:, :head], kv_ref[:, head:]], axis=0)
    r = lax.broadcasted_iota(jnp.int32, (group, head_rows, block), 1)
    half = (r & 1) * other_half
    j = lax.broadcasted_iota(jnp.int32, (group, 8, block), 1)
    both = []
    for core in range(2):
        heads = [slice((4 * core + h) * head, (4 * core + h + 1) * head) for h in range(4)]
        both.append(jnp.concatenate([jnp.concatenate([q_ref[:, at], g_ref[:, at]], axis=1) for at in heads], axis=0))

    def spread(x, n):
        return jnp.broadcast_to(x[:, None, :], (group, n, block))

    for chip in range(0, 64, group):
        first = block_down[chip : chip + group]
        first_count = count_down[chip : chip + group]
        second = block_down[64 + chip : 64 + chip + group]
        second_count = count_down[64 + chip : 64 + chip + group]
        wanted = jnp.where(j < 4, spread(first, 8), spread(second, 8)) == rows[None]
        heads = jnp.concatenate(
            [one_hot(wanted & ((j & 3) == h)).reshape(group * 8, block) for h in range(4)], axis=1
        )
        for core in range(2):
            t = core * 64 + chip
            entry = (r & -2) + core
            code = jnp.where(
                entry < spread(first_count, head_rows),
                entry + spread(first - first_count + 1, head_rows),
                jnp.where(
                    entry >= spread(entries - second_count, head_rows),
                    entry + spread(second - (entries - 1), head_rows),
                    nothing,
                ),
            )
            code = (jnp.where(r < kv_rows, code, nothing) + half).reshape(group * head_rows, block)
            pick = jnp.concatenate([one_hot(code == rows), one_hot(code == rows + other_half)], axis=1)
            got = jnp.dot(pick, kv, preferred_element_type=jnp.float32).reshape(group, head_rows, head)
            tail = got[:, head_rows - 8 :, :] + extra[None]
            got = jnp.concatenate([got[:, : head_rows - 8, :], tail], axis=1)
            out_ref[t : t + group, :head_rows, :] = got.astype(jnp.bfloat16)
            got = jnp.dot(heads, both[core], preferred_element_type=jnp.float32).astype(jnp.bfloat16)
            out_ref[t : t + group, head_rows : head_rows + 8, :] = got[:, :head].reshape(group, 8, head)
            out_ref[t : t + group, head_rows + 8 :, :] = got[:, head:].reshape(group, 8, head)


def unpack_kernel(
    place_ref, plan_ref, rows_table, heads_table, got_ref, out_hbm, dq_hbm, dkv_hbm, out_ref, dq_ref, dkv_ref, sems
):
    moves = [
        pltpu.make_async_copy(src, dst, sems.at[i])
        for i, (src, dst) in enumerate([(out_ref, out_hbm), (dq_ref, dq_hbm), (dkv_ref, dkv_hbm)])
    ]
    rows_down = down(place_ref[...] >> 7)
    plan = plan_ref[...].astype(jnp.float32)
    lane = lax.broadcasted_iota(jnp.int32, (8, block), 1)
    lines = [plan[0:1], plan[1:2]]
    lines = lines + [pltpu.roll(plan, 64, 1)[i : i + 1] for i in range(2)]
    lines.append(lane[0:1].astype(jnp.float32))
    stacked = jnp.zeros((16, block), jnp.float32)
    row = lax.broadcasted_iota(jnp.int32, (16, block), 0)
    for i, line in enumerate(lines):
        stacked = jnp.where((row == i) & (lane[0:1] < 64), line, stacked)
    stacked = stacked.astype(jnp.bfloat16)
    wide = nn(stacked, heads_table[...])
    j = lax.broadcasted_iota(jnp.int32, (1, 512), 1) & 7
    code = jnp.where(j < 4, wide[0:1], wide[2:3])
    rows_wide = jnp.concatenate([rows_down] * 4, axis=1)
    picks = [one_hot(jnp.where((j & 3) == h, code, float(nothing)) == rows_wide) for h in range(4)]
    for core in range(2):
        both = jnp.concatenate(
            [
                got_ref[core * 64 : core * 64 + 64, head_rows : head_rows + 8, :].reshape(512, head),
                got_ref[core * 64 : core * 64 + 64, head_rows + 8 :, :].reshape(512, head),
            ],
            axis=1,
        )
        for h in range(4):
            got = jnp.dot(picks[h], both, preferred_element_type=jnp.float32).astype(jnp.bfloat16)
            at = (4 * core + h) * head
            out_ref[:, at : at + head] = got[:, :head]
            dq_ref[:, at : at + head] = got[:, head:]
    moves[0].start()
    moves[1].start()
    wide = nn(stacked, rows_table[...])
    first, first_count, second, second_count, chip = [wide[i : i + 1] for i in range(5)]
    r = lax.broadcasted_iota(jnp.int32, (1, 64 * head_rows), 1) - head_rows * chip.astype(jnp.int32)
    sums = [jnp.zeros((block, head), jnp.float32), jnp.zeros((block, head), jnp.float32)]
    rows_wide = jnp.concatenate([rows_down] * (64 * head_rows // block), axis=1)
    for core in range(2):
        entry = ((r & -2) + core).astype(jnp.float32)
        code = jnp.where(
            entry < first_count,
            entry + (first - first_count + 1),
            jnp.where(entry >= entries - second_count, entry + (second - (entries - 1)), float(nothing)),
        )
        code = jnp.where(r < kv_rows, code, float(nothing))
        terms = got_ref[core * 64 : core * 64 + 64, :head_rows, :].reshape(64 * head_rows, head)
        for half in range(2):
            pick = one_hot(jnp.where((r & 1) == half, code, float(nothing)) == rows_wide)
            sums[half] = sums[half] + jnp.dot(pick, terms, preferred_element_type=jnp.float32)
    dkv_ref[...] = jnp.concatenate(sums, axis=1).astype(jnp.bfloat16)
    moves[2].start()
    for move in moves:
        move.wait()


def nt(a, b):
    return lax.dot_general(a, b, (((1,), (1,)), ((), ())), preferred_element_type=jnp.float32)


def tn(a, b):
    return lax.dot_general(a, b, (((0,), (0,)), ((), ())), preferred_element_type=jnp.float32)


def nn(a, b):
    return jnp.dot(a, b, preferred_element_type=jnp.float32)


def split_kernel(got_ref, kv_ref, info_ref, qg_ref):
    for r in range(0, send_rows, 8):
        rows = jnp.transpose(got_ref[:, r : r + 8, :], (1, 0, 2))
        if r < kv_rows:
            n = min(8, kv_rows - r)
            kv_ref[r : r + n] = rows[:n]
            if n < 8:
                info_ref[...] = rows[n]
        else:
            at = (r - head_rows) * block
            qg_ref[at : at + 8 * block, :] = rows.reshape(8 * block, head)


to_exp2 = head ** (-0.5) * 1.4426950408889634


def spans_of(plan_ref, chip):
    first, second = plan_ref[1, chip], plan_ref[1, chip + 64]
    begin = entries - second
    few = second <= 2
    long = first > 24
    whole = jnp.int32(entries)
    return [
        (0, 9, 0, jnp.int32(0), first, jnp.int32(0), jnp.where(long, 2, 0)),
        (0, 6, 0, jnp.int32(0), first, jnp.int32(0), jnp.where(long, 0, (first + 11) // 12)),
        (1, 1, 6, begin, whole, jnp.where(few, begin // 2, pairs), jnp.int32(pairs)),
        (1, 3, 6, begin, whole, jnp.where(few, pairs // 3, begin // 6), jnp.int32(pairs // 3)),
    ]


def rows_of(x):
    return slice(x * 512, (x + 1) * 512), slice(1024 + x * 512, 1536 + x * 512)


def blocks(ref, half, m, n):
    return jnp.concatenate([ref[2 * (m * n + u) + half] for u in range(n)], axis=0)


def slot(m, n, shift):
    return pl.ds(m * n + shift, n)


def flat(x):
    return x.reshape(x.shape[0] * block, 512)


def find_positions(core, chip, mine_len, other_len, plan_ref, info_ref, key_pos, bound):
    stream = chip // 32
    stream_base = (64 * stream).astype(jnp.float32)
    block_row = lax.broadcasted_iota(jnp.int32, (block, block), 0)
    key_pos[...] = info_ref[...].astype(jnp.float32).T + 128.0 * (block_row.astype(jnp.float32) - stream_base)
    for x in range(2):
        pos = key_pos[pl.ds(plan_ref[0, chip + 64 * x], 1), :]
        start = jnp.zeros((1, block), jnp.float32)
        doc_end = jnp.int32(0)
        for i in range(16):
            doc_end = doc_end + stream_length(core, mine_len, other_len, stream, i)
            f = doc_end.astype(jnp.float32)
            start = jnp.where(f <= pos, f, start)
        bound[2 * x : 2 * x + 1] = pos
        bound[2 * x + 1 : 2 * x + 2] = start


def score(x, m, n, low, high, parity, plan_ref, chip, kv_ref, qg, key_pos, bound):
    base = plan_ref[0, chip + 64 * x] - plan_ref[1, chip + 64 * x] + 1 - low
    bias = []
    for u in range(n):
        entry = 2 * (m * n + u) + parity
        valid = (entry >= low) & (entry < high)
        kp = key_pos[pl.ds(jnp.where(valid, base + entry, 0), 1), :]
        kp = jnp.broadcast_to(jnp.where(valid, kp, far), (block, block)).T
        seen = (kp <= bound[2 * x : 2 * x + 1]) & (kp >= bound[2 * x + 1 : 2 * x + 2])
        bias.append(jnp.where(seen, 0.0, masked_score))
    bias = jnp.concatenate(bias, axis=0)
    bias = jnp.concatenate([bias] * 4, axis=1)
    return nt(blocks(kv_ref, 0, m, n), qg[rows_of(x)[0], :]) + bias


def peak_of(s):
    return jnp.max(s.reshape(s.shape[0] // 8, 8, 512), axis=0)


def sum_of(p):
    return jnp.sum(p.reshape(p.shape[0] // 8, 8, 512), axis=0)


def scores_kernel(
    mine_len, other_len, plan_ref, mine_ref, info_ref, qg,
    s_ref, gw_ref, top_ref, key_pos, bound,
):
    core = lax.axis_index("dp")
    chip = lax.axis_index("ctx")
    find_positions(core, chip, mine_len, other_len, plan_ref, info_ref, key_pos, bound)
    top_ref[...] = jnp.full(top_ref.shape, masked_score, jnp.float32)
    for x, n, shift, low, high, begin, end in spans_of(plan_ref, chip):
        cols = slice(x * 512, (x + 1) * 512)

        @pl.loop(begin, end)
        def _(m):
            s = score(x, m, n, low, high, core, plan_ref, chip, mine_ref, qg, key_pos, bound)
            gw = nt(blocks(mine_ref, 1, m, n), qg[rows_of(x)[1], :])
            s_ref[slot(m, n, shift)] = s.reshape(n, block, 512)
            top_ref[:, cols] = jnp.maximum(top_ref[:, cols], peak_of(s))
            gw_ref[slot(m, n, shift)] = gw.reshape(n, block, 512)


def backward(span, p_ref, gw_ref, kv_ref, dot_ref, qs_ref, gs_ref, acc, out_ref):
    x, n, shift, _, _, begin, end = span
    cols = slice(x * 512, (x + 1) * 512)

    @pl.loop(begin, end)
    def _(m):
        at = slot(m, n, shift)
        p = flat(p_ref[at])
        ds = (p.astype(jnp.float32) * (flat(gw_ref[at]) - dot_ref[0:1, cols])).astype(jnp.bfloat16)
        dk = nn(ds, qs_ref[cols, :])
        acc[:, cols] = acc[:, cols] + tn(blocks(kv_ref, 0, m, n), ds)
        dv = nn(p, gs_ref[cols, :])
        for u in range(n):
            for half, value in enumerate((dk, dv)):
                value = value[u * block : (u + 1) * block]
                i = 2 * (m * n + u) + half
                if x == 1:
                    value = value + out_ref[i].astype(jnp.float32)
                out_ref[i] = value.astype(jnp.bfloat16)


def clear_rest(out_ref, spans):
    long, short = spans[0], spans[1]

    @pl.loop(2 * (long[1] * long[-1] + short[1] * short[-1]), kv_rows)
    def _(i):
        out_ref[i] = jnp.zeros((block, head), jnp.bfloat16)


def turned(x):
    row = lax.broadcasted_iota(jnp.int32, (block, block), 0)
    eye = one_hot(row == lax.broadcasted_iota(jnp.int32, (block, block), 1))
    return jnp.concatenate([nt(eye, x[:, h * block : (h + 1) * block]) for h in range(8)], axis=0)


def weights_kernel(
    plan_ref, mine_ref, other_ref, qg, s_ref, found_ref, key_pos, bound,
    dother_ref, out_ref, p_ref, dot_ref, qs_ref, gs_ref, acc_ref, inv_ref,
    scores, gws, ps, top, total, acc,
):
    core = lax.axis_index("dp")
    chip = lax.axis_index("ctx")
    scale = head ** (-0.5)
    ones = jnp.full((16, block), 1.0, jnp.bfloat16)
    row16 = lax.broadcasted_iota(jnp.int32, (16, 1024), 0)
    spans = spans_of(plan_ref, chip)
    clear_rest(dother_ref, spans)
    top[...] = found_ref[...]
    total[...] = jnp.zeros(total.shape, jnp.float32)
    acc[...] = jnp.zeros(acc.shape, jnp.float32)
    for x, n, shift, low, high, begin, end in spans:
        cols = slice(x * 512, (x + 1) * 512)

        @pl.loop(begin, end)
        def _(m):
            s = score(x, m, n, low, high, 1 - core, plan_ref, chip, other_ref, qg, key_pos, bound)
            scores[slot(m, n, shift)] = s.reshape(n, block, 512)
            top[:, cols] = jnp.maximum(top[:, cols], peak_of(s))

    top[...] = jnp.broadcast_to(jnp.max(top[...], axis=0, keepdims=True) * to_exp2, top.shape)
    for x, n, shift, low, high, begin, end in spans:
        cols = slice(x * 512, (x + 1) * 512)

        @pl.loop(begin, end)
        def _(m):
            at = slot(m, n, shift)
            gws[at] = nt(blocks(other_ref, 1, m, n), qg[rows_of(x)[1], :]).reshape(n, block, 512)
            p = jnp.exp2(flat(s_ref[at]) * to_exp2 - top[0:1, cols])
            p_other = jnp.exp2(flat(scores[at]) * to_exp2 - top[0:1, cols])
            total[:, cols] = total[:, cols] + (sum_of(p) + sum_of(p_other))
            p, p_other = p.astype(jnp.bfloat16), p_other.astype(jnp.bfloat16)
            p_ref[at] = p.reshape(n, block, 512)
            ps[at] = p_other.reshape(n, block, 512)
            values = jnp.concatenate([blocks(mine_ref, 1, m, n), blocks(other_ref, 1, m, n)], axis=0)
            acc[:, cols] = acc[:, cols] + tn(values, jnp.concatenate([p, p_other], axis=0))

    inv = 1.0 / jnp.sum(total[...], axis=0, keepdims=True)
    part = inv.astype(jnp.bfloat16).astype(jnp.float32)
    rest = inv - part
    middle = rest.astype(jnp.bfloat16).astype(jnp.float32)
    parts = jnp.where(row16 == 0, part, jnp.where(row16 == 1, middle, jnp.where(row16 == 2, rest - middle, 0.0)))
    inv_down = tn(parts.astype(jnp.bfloat16), ones)
    o = turned((acc[...] * inv).astype(jnp.bfloat16))
    out_ref[...] = o.astype(jnp.bfloat16)
    g = qg[1024:, :].astype(jnp.float32)
    terms = g * o
    part = terms.astype(jnp.bfloat16)
    d = nt(ones, part) + nt(ones, (terms - part.astype(jnp.float32)).astype(jnp.bfloat16))
    dot_ref[...] = d[:8]
    gs_ref[...] = (g * inv_down).astype(jnp.bfloat16)
    qs_ref[...] = (qg[:1024, :].astype(jnp.float32) * (inv_down * scale)).astype(jnp.bfloat16)
    inv_ref[...] = jnp.broadcast_to(inv * scale, inv_ref.shape)
    acc_ref[...] = jnp.zeros(acc_ref.shape, jnp.float32)
    for span in spans:
        backward(span, ps, gws, other_ref, dot_ref, qs_ref, gs_ref, acc_ref, dother_ref)


def grads_kernel(
    plan_ref, mine_ref, gw_ref, p_ref, dot_ref, qs_ref, gs_ref, part_ref, inv_ref,
    dmine_ref, dq_ref,
    acc,
):
    chip = lax.axis_index("ctx")
    spans = spans_of(plan_ref, chip)
    clear_rest(dmine_ref, spans)
    acc[...] = part_ref[...]
    for span in spans:
        backward(span, p_ref, gw_ref, mine_ref, dot_ref, qs_ref, gs_ref, acc, dmine_ref)
    dq_ref[...] = turned((acc[...] * inv_ref[0:1]).astype(jnp.bfloat16)).astype(jnp.bfloat16)


def join_kernel(mine_ref, other_ref, out_ref, dq_ref, back_ref):
    def put(r, rows):
        back_ref[:, r : r + 8, :] = jnp.transpose(rows, (1, 0, 2))

    for r in range(0, head_rows, 8):
        n = min(8, kv_rows - r)
        rows = mine_ref[r : r + n].astype(jnp.float32) + other_ref[r : r + n].astype(jnp.float32)
        rows = rows.astype(jnp.bfloat16)
        if n < 8:
            rows = jnp.concatenate([rows, jnp.zeros((8 - n, block, head), jnp.bfloat16)], axis=0)
        put(r, rows)
    put(head_rows, out_ref[...].reshape(8, block, head))
    put(head_rows + 8, dq_ref[...].reshape(8, block, head))


def vmem(n):
    return [pl.BlockSpec(memory_space=pltpu.VMEM)] * n


def smem():
    return pl.BlockSpec(memory_space=pltpu.SMEM)


def params(size):
    return pltpu.CompilerParams(vmem_limit_bytes=size * mib)


def swap(x):
    return lax.ppermute(x, "dp", [(0, 1), (1, 0)])


def exchange(x):
    return lax.all_to_all(x, ("dp", "ctx"), split_axis=0, concat_axis=0, tiled=True)


def kernel(name, body, ins, scalars, outs, scratch, size):
    return pl.pallas_call(
        body,
        out_shape=tuple(jax.ShapeDtypeStruct(shape, dtype) for shape, dtype in outs),
        in_specs=[smem()] * scalars + vmem(len(ins) - scalars),
        out_specs=tuple(vmem(len(outs))),
        scratch_shapes=[pltpu.VMEM(shape, dtype) for shape, dtype in scratch],
        compiler_params=params(size),
        name=name,
    )(*ins)


def attention(lengths, other_lengths, plan, mine, other, info, qg):
    bf16, f32 = jnp.bfloat16, jnp.float32
    slots = (pairs + 6, block, 512)
    rows = ((8, 1024), f32)
    acc = ((head, 1024), f32)
    heads = ((1024, head), bf16)
    places = [((block, block), f32), ((8, block), f32)]
    s, gw, top, key_pos, bound = kernel(
        "scores", scores_kernel, (lengths, other_lengths, plan, mine, info, qg), 3,
        [(slots, f32), (slots, f32), ((8, 1024), f32)] + places, [], 12,
    )
    dother, out, p, dot, qs, gs, partial, inv = kernel(
        "weights", weights_kernel, (plan, mine, other, qg, s, top, key_pos, bound), 1,
        [((kv_rows, block, head), bf16), heads, (slots, bf16), rows, heads, heads, acc, rows],
        [(slots, f32), (slots, f32), (slots, bf16), rows, rows, acc], 24,
    )
    other_terms = swap(dother)
    dmine, dq = kernel(
        "grads", grads_kernel, (plan, mine, gw, p, dot, qs, gs, partial, inv), 1,
        [((kv_rows, block, head), bf16), heads], [acc], 12,
    )
    return dmine, other_terms, out, dq


def on_device(queries, keys_values, grad_out, placement, doc_lengths):
    bf16, f32 = jnp.bfloat16, jnp.float32
    place = placement.reshape(1, block)
    other_lengths = swap(doc_lengths)
    rows_table, heads_table, lanes = pl.pallas_call(
        tables_kernel,
        out_shape=(
            jax.ShapeDtypeStruct((block, 64 * head_rows), bf16),
            jax.ShapeDtypeStruct((block, 64 * 8), bf16),
            jax.ShapeDtypeStruct((block, block), f32),
        ),
        in_specs=[],
        out_specs=tuple(vmem(3)),
        compiler_params=params(8),
        cost_estimate=pl.CostEstimate(flops=4 * 10**9, bytes_accessed=0, transcendentals=0),
        name="tables",
    )()
    sent, plan = pl.pallas_call(
        pack_kernel,
        out_shape=(
            jax.ShapeDtypeStruct((128, send_rows, head), bf16),
            jax.ShapeDtypeStruct((8, block), jnp.int32),
        ),
        in_specs=[smem()] * 2 + vmem(5),
        out_specs=tuple(vmem(2)),
        compiler_params=params(24),
        name="pack",
    )(doc_lengths, other_lengths, place, lanes, queries, keys_values, grad_out)
    mine, info, qg = pl.pallas_call(
        split_kernel,
        out_shape=(
            jax.ShapeDtypeStruct((kv_rows, block, head), bf16),
            jax.ShapeDtypeStruct((block, head), bf16),
            jax.ShapeDtypeStruct((2048, head), bf16),
        ),
        in_specs=vmem(1),
        out_specs=tuple(vmem(3)),
        compiler_params=params(24),
        name="split",
    )(exchange(sent))
    dmine, dother, out, dq = attention(doc_lengths, other_lengths, plan, mine, swap(mine), info, qg)
    back = pl.pallas_call(
        join_kernel,
        out_shape=jax.ShapeDtypeStruct((128, send_rows, head), bf16),
        in_specs=vmem(4),
        out_specs=vmem(1)[0],
        compiler_params=params(24),
        name="join",
    )(dmine, dother, out, dq)
    returned = exchange(back)
    return pl.pallas_call(
        unpack_kernel,
        out_shape=(
            jax.ShapeDtypeStruct((block, 8 * head), bf16),
            jax.ShapeDtypeStruct((block, 8 * head), bf16),
            jax.ShapeDtypeStruct((block, 2 * head), bf16),
        ),
        in_specs=vmem(5),
        out_specs=tuple([pl.BlockSpec(memory_space=pl.ANY)] * 3),
        scratch_shapes=[
            pltpu.VMEM((block, 8 * head), bf16),
            pltpu.VMEM((block, 8 * head), bf16),
            pltpu.VMEM((block, 2 * head), bf16),
            pltpu.SemaphoreType.DMA((3,)),
        ],
        compiler_params=params(24),
        name="unpack",
    )(place, plan, rows_table, heads_table, returned)


def solution(mesh):
    rows = P(("dp", "ctx"), None)
    return jax.shard_map(
        on_device,
        mesh=mesh,
        in_specs=(rows, rows, rows, P(("dp", "ctx")), P("dp", None)),
        out_specs=(rows, rows, rows),
        check_vma=False,
    )
```

```python
import jax
import jax.numpy as jnp
from jax import lax
from jax.experimental import pallas as pl
from jax.experimental.pallas import tpu as pltpu
from jax.sharding import PartitionSpec as P

block = 128
head = 128
entries = 36
pairs = entries // 2
kv_rows = 2 * pairs
head_rows = 40
send_rows = 56
group = 16
other_half = 1000
nothing = -100000
masked_score = -1e30
far = 1e9
mib = 1024 * 1024


def one_hot(mask):
    return jnp.where(mask, 1.0, 0.0).astype(jnp.bfloat16)


def down(line):
    return jnp.broadcast_to(line.astype(jnp.float32), (block, block)).T


def stream_length(core, mine_ref, other_ref, stream, i):
    return jnp.where(core == stream, mine_ref[0, i], other_ref[0, i])


def make_plan(core, mine_ref, other_ref):
    lane = lax.broadcasted_iota(jnp.int32, (1, block), 1)
    pos = (lane & 63) * block
    start = jnp.zeros((1, block), jnp.int32)
    end0, end1 = jnp.int32(0), jnp.int32(0)
    for i in range(16):
        end0 = end0 + stream_length(core, mine_ref, other_ref, 0, i)
        end1 = end1 + stream_length(core, mine_ref, other_ref, 1, i)
        end = jnp.where(lane < 64, end0, end1)
        start = jnp.where(end <= pos, end, start)
    count = (lane & 63) - (start >> 7) + 1
    key = count * 64 + (lane & 63)
    row = lax.broadcasted_iota(jnp.int32, (block, block), 0)
    col = lax.broadcasted_iota(jnp.int32, (block, block), 1)
    above = (down(key) > key.astype(jnp.float32)) & ((row >> 6) == (col >> 6))
    rank = jnp.sum(jnp.where(above, 1.0, 0.0), axis=0, keepdims=True).astype(jnp.int32)
    seat = jnp.where(rank < 32, rank, 63 - rank) + 32 * (lane >> 6) + jnp.where(rank < 32, 0, 64)
    here = down(seat) == col.astype(jnp.float32)
    block_line = jnp.sum(jnp.where(here, row.astype(jnp.float32), 0.0), axis=0, keepdims=True)
    count_line = jnp.sum(jnp.where(here, down(count), 0.0), axis=0, keepdims=True)
    return block_line, count_line


def tables_kernel(rows_ref, heads_ref, lane_ref):
    lane_ref[...] = lax.broadcasted_iota(jnp.int32, (block, block), 1).astype(jnp.float32)
    for ref, width in ((rows_ref, head_rows), (heads_ref, 8)):
        chip = lax.broadcasted_iota(jnp.int32, ref.shape, 0) * width
        lane = lax.broadcasted_iota(jnp.int32, ref.shape, 1)
        ref[...] = one_hot((lane >= chip) & (lane < chip + width))


def pack_kernel(mine_ref, other_ref, place_ref, lane_ref, q_ref, kv_ref, g_ref, out_ref, plan_ref):
    block_line, count_line = make_plan(lax.axis_index("dp"), mine_ref, other_ref)
    row8 = lax.broadcasted_iota(jnp.int32, (8, block), 0)
    plan_ref[...] = jnp.where(row8 == 0, block_line, jnp.where(row8 == 1, count_line, 0.0)).astype(jnp.int32)
    block_down = down(block_line).astype(jnp.int32)
    count_down = down(count_line).astype(jnp.int32)
    rows = place_ref[...] >> 7
    slots_down = down(place_ref[...] & (block - 1))
    slot_line = jnp.sum(jnp.where(down(rows) == lane_ref[...], slots_down, 0.0), axis=0, keepdims=True)
    extra = jnp.where(row8 == kv_rows % 8, slot_line, 0.0)
    kv = jnp.concatenate([kv_ref[:, :head], kv_ref[:, head:]], axis=0)
    r = lax.broadcasted_iota(jnp.int32, (group, head_rows, block), 1)
    half = (r & 1) * other_half
    j = lax.broadcasted_iota(jnp.int32, (group, 8, block), 1)
    both = []
    for core in range(2):
        heads = [slice((4 * core + h) * head, (4 * core + h + 1) * head) for h in range(4)]
        both.append(jnp.concatenate([jnp.concatenate([q_ref[:, at], g_ref[:, at]], axis=1) for at in heads], axis=0))

    def spread(x, n):
        return jnp.broadcast_to(x[:, None, :], (group, n, block))

    for chip in range(0, 64, group):
        first = block_down[chip : chip + group]
        first_count = count_down[chip : chip + group]
        second = block_down[64 + chip : 64 + chip + group]
        second_count = count_down[64 + chip : 64 + chip + group]
        wanted = jnp.where(j < 4, spread(first, 8), spread(second, 8)) == rows[None]
        heads = jnp.concatenate(
            [one_hot(wanted & ((j & 3) == h)).reshape(group * 8, block) for h in range(4)], axis=1
        )
        for core in range(2):
            t = core * 64 + chip
            entry = (r & -2) + core
            code = jnp.where(
                entry < spread(first_count, head_rows),
                entry + spread(first - first_count + 1, head_rows),
                jnp.where(
                    entry >= spread(entries - second_count, head_rows),
                    entry + spread(second - (entries - 1), head_rows),
                    nothing,
                ),
            )
            code = (jnp.where(r < kv_rows, code, nothing) + half).reshape(group * head_rows, block)
            pick = jnp.concatenate([one_hot(code == rows), one_hot(code == rows + other_half)], axis=1)
            got = jnp.dot(pick, kv, preferred_element_type=jnp.float32).reshape(group, head_rows, head)
            tail = got[:, head_rows - 8 :, :] + extra[None]
            got = jnp.concatenate([got[:, : head_rows - 8, :], tail], axis=1)
            out_ref[t : t + group, :head_rows, :] = got.astype(jnp.bfloat16)
            got = jnp.dot(heads, both[core], preferred_element_type=jnp.float32).astype(jnp.bfloat16)
            out_ref[t : t + group, head_rows : head_rows + 8, :] = got[:, :head].reshape(group, 8, head)
            out_ref[t : t + group, head_rows + 8 :, :] = got[:, head:].reshape(group, 8, head)


def unpack_kernel(
    place_ref, plan_ref, rows_table, heads_table, got_ref, out_hbm, dq_hbm, dkv_hbm, out_ref, dq_ref, dkv_ref, sems
):
    moves = [
        pltpu.make_async_copy(src, dst, sems.at[i])
        for i, (src, dst) in enumerate([(out_ref, out_hbm), (dq_ref, dq_hbm), (dkv_ref, dkv_hbm)])
    ]
    rows_down = down(place_ref[...] >> 7)
    plan = plan_ref[...].astype(jnp.float32)
    lane = lax.broadcasted_iota(jnp.int32, (8, block), 1)
    lines = [plan[0:1], plan[1:2]]
    lines = lines + [pltpu.roll(plan, 64, 1)[i : i + 1] for i in range(2)]
    lines.append(lane[0:1].astype(jnp.float32))
    stacked = jnp.zeros((16, block), jnp.float32)
    row = lax.broadcasted_iota(jnp.int32, (16, block), 0)
    for i, line in enumerate(lines):
        stacked = jnp.where((row == i) & (lane[0:1] < 64), line, stacked)
    stacked = stacked.astype(jnp.bfloat16)
    wide = nn(stacked, heads_table[...])
    j = lax.broadcasted_iota(jnp.int32, (1, 512), 1) & 7
    code = jnp.where(j < 4, wide[0:1], wide[2:3])
    rows_wide = jnp.concatenate([rows_down] * 4, axis=1)
    picks = [one_hot(jnp.where((j & 3) == h, code, float(nothing)) == rows_wide) for h in range(4)]
    for core in range(2):
        both = jnp.concatenate(
            [
                got_ref[core * 64 : core * 64 + 64, head_rows : head_rows + 8, :].reshape(512, head),
                got_ref[core * 64 : core * 64 + 64, head_rows + 8 :, :].reshape(512, head),
            ],
            axis=1,
        )
        for h in range(4):
            got = jnp.dot(picks[h], both, preferred_element_type=jnp.float32).astype(jnp.bfloat16)
            at = (4 * core + h) * head
            out_ref[:, at : at + head] = got[:, :head]
            dq_ref[:, at : at + head] = got[:, head:]
    moves[0].start()
    moves[1].start()
    wide = nn(stacked, rows_table[...])
    first, first_count, second, second_count, chip = [wide[i : i + 1] for i in range(5)]
    r = lax.broadcasted_iota(jnp.int32, (1, 64 * head_rows), 1) - head_rows * chip.astype(jnp.int32)
    sums = jnp.zeros((block, 2 * head), jnp.float32)
    rows_wide = jnp.concatenate([rows_down] * (64 * head_rows // block), axis=1)
    row = lax.broadcasted_iota(jnp.int32, (16, head), 0)
    keys, values = one_hot((row & 1) == 0)[None], one_hot((row & 1) == 1)[None]
    for core in range(2):
        entry = ((r & -2) + core).astype(jnp.float32)
        code = jnp.where(
            entry < first_count,
            entry + (first - first_count + 1),
            jnp.where(entry >= entries - second_count, entry + (second - (entries - 1)), float(nothing)),
        )
        code = jnp.where(r < kv_rows, code, float(nothing))
        terms = got_ref[core * 64 : core * 64 + 64, :head_rows, :].reshape(4 * head_rows, 16, head)
        sides = [(terms * side).reshape(64 * head_rows, head) for side in (keys, values)]
        pick = one_hot(code == rows_wide)
        sums = sums + jnp.dot(pick, jnp.concatenate(sides, axis=1), preferred_element_type=jnp.float32)
    dkv_ref[...] = sums.astype(jnp.bfloat16)
    moves[2].start()
    for move in moves:
        move.wait()


def nt(a, b):
    return lax.dot_general(a, b, (((1,), (1,)), ((), ())), preferred_element_type=jnp.float32)


def tn(a, b):
    return lax.dot_general(a, b, (((0,), (0,)), ((), ())), preferred_element_type=jnp.float32)


def nn(a, b):
    return jnp.dot(a, b, preferred_element_type=jnp.float32)


def split_kernel(got_ref, kv_ref, info_ref, qg_ref):
    for r in range(0, send_rows, 8):
        rows = jnp.transpose(got_ref[:, r : r + 8, :], (1, 0, 2))
        if r < kv_rows:
            n = min(8, kv_rows - r)
            kv_ref[r : r + n] = rows[:n]
            if n < 8:
                info_ref[...] = rows[n]
        else:
            at = (r - head_rows) * block
            qg_ref[at : at + 8 * block, :] = rows.reshape(8 * block, head)


to_exp2 = head ** (-0.5) * 1.4426950408889634


def spans_of(plan_ref, chip):
    first, second = plan_ref[1, chip], plan_ref[1, chip + 64]
    begin = entries - second
    few = second <= 2
    long = first > 24
    whole = jnp.int32(entries)
    return [
        (0, 9, 0, jnp.int32(0), first, jnp.int32(0), jnp.where(long, 2, 0)),
        (0, 6, 0, jnp.int32(0), first, jnp.int32(0), jnp.where(long, 0, (first + 11) // 12)),
        (1, 1, 6, begin, whole, jnp.where(few, begin // 2, pairs), jnp.int32(pairs)),
        (1, 3, 6, begin, whole, jnp.where(few, pairs // 3, begin // 6), jnp.int32(pairs // 3)),
    ]


def rows_of(x):
    return slice(x * 512, (x + 1) * 512), slice(1024 + x * 512, 1536 + x * 512)


def blocks(ref, half, m, n):
    return jnp.concatenate([ref[2 * (m * n + u) + half] for u in range(n)], axis=0)


def slot(m, n, shift):
    return pl.ds(m * n + shift, n)


def flat(x):
    return x.reshape(x.shape[0] * block, 512)


def find_positions(core, chip, mine_len, other_len, plan_ref, info_ref, key_pos, bound):
    stream = chip // 32
    stream_base = (64 * stream).astype(jnp.float32)
    block_row = lax.broadcasted_iota(jnp.int32, (block, block), 0)
    key_pos[...] = info_ref[...].astype(jnp.float32).T + 128.0 * (block_row.astype(jnp.float32) - stream_base)
    for x in range(2):
        pos = key_pos[pl.ds(plan_ref[0, chip + 64 * x], 1), :]
        start = jnp.zeros((1, block), jnp.float32)
        doc_end = jnp.int32(0)
        for i in range(16):
            doc_end = doc_end + stream_length(core, mine_len, other_len, stream, i)
            f = doc_end.astype(jnp.float32)
            start = jnp.where(f <= pos, f, start)
        bound[2 * x : 2 * x + 1] = pos
        bound[2 * x + 1 : 2 * x + 2] = start


def score(x, m, n, low, high, parity, plan_ref, chip, kv_ref, qg, key_pos, bound):
    base = plan_ref[0, chip + 64 * x] - plan_ref[1, chip + 64 * x] + 1 - low
    bias = []
    for u in range(n):
        entry = 2 * (m * n + u) + parity
        valid = (entry >= low) & (entry < high)
        kp = key_pos[pl.ds(jnp.where(valid, base + entry, 0), 1), :]
        kp = jnp.broadcast_to(jnp.where(valid, kp, far), (block, block)).T
        seen = (kp <= bound[2 * x : 2 * x + 1]) & (kp >= bound[2 * x + 1 : 2 * x + 2])
        bias.append(jnp.where(seen, 0.0, masked_score))
    bias = jnp.concatenate(bias, axis=0)
    bias = jnp.concatenate([bias] * 4, axis=1)
    return nt(blocks(kv_ref, 0, m, n), qg[rows_of(x)[0], :]) + bias


def peak_of(s):
    return jnp.max(s.reshape(s.shape[0] // 8, 8, 512), axis=0)


def sum_of(p):
    return jnp.sum(p.reshape(p.shape[0] // 8, 8, 512), axis=0)


def scores_kernel(
    mine_len, other_len, plan_ref, mine_ref, info_ref, qg,
    s_ref, gw_ref, top_ref, key_pos, bound,
):
    core = lax.axis_index("dp")
    chip = lax.axis_index("ctx")
    find_positions(core, chip, mine_len, other_len, plan_ref, info_ref, key_pos, bound)
    top_ref[...] = jnp.full(top_ref.shape, masked_score, jnp.float32)
    for x, n, shift, low, high, begin, end in spans_of(plan_ref, chip):
        cols = slice(x * 512, (x + 1) * 512)

        @pl.loop(begin, end)
        def _(m):
            s = score(x, m, n, low, high, core, plan_ref, chip, mine_ref, qg, key_pos, bound)
            gw = nt(blocks(mine_ref, 1, m, n), qg[rows_of(x)[1], :])
            s_ref[slot(m, n, shift)] = s.reshape(n, block, 512)
            top_ref[:, cols] = jnp.maximum(top_ref[:, cols], peak_of(s))
            gw_ref[slot(m, n, shift)] = gw.reshape(n, block, 512)


def backward(span, p_ref, gw_ref, kv_ref, dot_ref, qs_ref, gs_ref, acc, out_ref):
    x, n, shift, _, _, begin, end = span
    cols = slice(x * 512, (x + 1) * 512)

    @pl.loop(begin, end)
    def _(m):
        at = slot(m, n, shift)
        p = flat(p_ref[at])
        ds = (p.astype(jnp.float32) * (flat(gw_ref[at]) - dot_ref[0:1, cols])).astype(jnp.bfloat16)
        dk = nn(ds, qs_ref[cols, :])
        acc[:, cols] = acc[:, cols] + tn(blocks(kv_ref, 0, m, n), ds)
        dv = nn(p, gs_ref[cols, :])
        for u in range(n):
            for half, value in enumerate((dk, dv)):
                value = value[u * block : (u + 1) * block]
                i = 2 * (m * n + u) + half
                if x == 1:
                    value = value + out_ref[i].astype(jnp.float32)
                out_ref[i] = value.astype(jnp.bfloat16)


def clear_rest(out_ref, spans):
    long, short = spans[0], spans[1]

    @pl.loop(2 * (long[1] * long[-1] + short[1] * short[-1]), kv_rows)
    def _(i):
        out_ref[i] = jnp.zeros((block, head), jnp.bfloat16)


def turned(x):
    row = lax.broadcasted_iota(jnp.int32, (block, block), 0)
    eye = one_hot(row == lax.broadcasted_iota(jnp.int32, (block, block), 1))
    return jnp.concatenate([nt(eye, x[:, h * block : (h + 1) * block]) for h in range(8)], axis=0)


def weights_kernel(
    plan_ref, mine_ref, other_ref, qg, s_ref, found_ref, key_pos, bound,
    dother_ref, out_ref, p_ref, dot_ref, qs_ref, gs_ref, acc_ref, inv_ref,
    scores, gws, ps, top, total, acc,
):
    core = lax.axis_index("dp")
    chip = lax.axis_index("ctx")
    scale = head ** (-0.5)
    ones = jnp.full((16, block), 1.0, jnp.bfloat16)
    row16 = lax.broadcasted_iota(jnp.int32, (16, 1024), 0)
    spans = spans_of(plan_ref, chip)
    clear_rest(dother_ref, spans)
    top[...] = found_ref[...]
    total[...] = jnp.zeros(total.shape, jnp.float32)
    acc[...] = jnp.zeros(acc.shape, jnp.float32)
    for x, n, shift, low, high, begin, end in spans:
        cols = slice(x * 512, (x + 1) * 512)

        @pl.loop(begin, end)
        def _(m):
            s = score(x, m, n, low, high, 1 - core, plan_ref, chip, other_ref, qg, key_pos, bound)
            scores[slot(m, n, shift)] = s.reshape(n, block, 512)
            top[:, cols] = jnp.maximum(top[:, cols], peak_of(s))

    top[...] = jnp.broadcast_to(jnp.max(top[...], axis=0, keepdims=True) * to_exp2, top.shape)
    for x, n, shift, low, high, begin, end in spans:
        cols = slice(x * 512, (x + 1) * 512)

        @pl.loop(begin, end)
        def _(m):
            at = slot(m, n, shift)
            gws[at] = nt(blocks(other_ref, 1, m, n), qg[rows_of(x)[1], :]).reshape(n, block, 512)
            p = jnp.exp2(flat(s_ref[at]) * to_exp2 - top[0:1, cols])
            p_other = jnp.exp2(flat(scores[at]) * to_exp2 - top[0:1, cols])
            total[:, cols] = total[:, cols] + (sum_of(p) + sum_of(p_other))
            p, p_other = p.astype(jnp.bfloat16), p_other.astype(jnp.bfloat16)
            p_ref[at] = p.reshape(n, block, 512)
            ps[at] = p_other.reshape(n, block, 512)
            values = jnp.concatenate([blocks(mine_ref, 1, m, n), blocks(other_ref, 1, m, n)], axis=0)
            acc[:, cols] = acc[:, cols] + tn(values, jnp.concatenate([p, p_other], axis=0))

    inv = 1.0 / jnp.sum(total[...], axis=0, keepdims=True)
    part = inv.astype(jnp.bfloat16).astype(jnp.float32)
    rest = inv - part
    middle = rest.astype(jnp.bfloat16).astype(jnp.float32)
    parts = jnp.where(row16 == 0, part, jnp.where(row16 == 1, middle, jnp.where(row16 == 2, rest - middle, 0.0)))
    inv_down = tn(parts.astype(jnp.bfloat16), ones)
    o = turned((acc[...] * inv).astype(jnp.bfloat16))
    out_ref[...] = o.astype(jnp.bfloat16)
    g = qg[1024:, :].astype(jnp.float32)
    terms = g * o
    part = terms.astype(jnp.bfloat16)
    d = nt(ones, part) + nt(ones, (terms - part.astype(jnp.float32)).astype(jnp.bfloat16))
    dot_ref[...] = d[:8]
    gs_ref[...] = (g * inv_down).astype(jnp.bfloat16)
    qs_ref[...] = (qg[:1024, :].astype(jnp.float32) * (inv_down * scale)).astype(jnp.bfloat16)
    inv_ref[...] = jnp.broadcast_to(inv * scale, inv_ref.shape)
    acc_ref[...] = jnp.zeros(acc_ref.shape, jnp.float32)
    for span in spans:
        backward(span, ps, gws, other_ref, dot_ref, qs_ref, gs_ref, acc_ref, dother_ref)


def grads_kernel(
    plan_ref, mine_ref, gw_ref, p_ref, dot_ref, qs_ref, gs_ref, part_ref, inv_ref,
    dmine_ref, dq_ref,
    acc,
):
    chip = lax.axis_index("ctx")
    spans = spans_of(plan_ref, chip)
    clear_rest(dmine_ref, spans)
    acc[...] = part_ref[...]
    for span in spans:
        backward(span, p_ref, gw_ref, mine_ref, dot_ref, qs_ref, gs_ref, acc, dmine_ref)
    dq_ref[...] = turned((acc[...] * inv_ref[0:1]).astype(jnp.bfloat16)).astype(jnp.bfloat16)


def join_kernel(mine_ref, other_ref, out_ref, dq_ref, back_ref):
    def put(r, rows):
        back_ref[:, r : r + 8, :] = jnp.transpose(rows, (1, 0, 2))

    for r in range(0, head_rows, 8):
        n = min(8, kv_rows - r)
        rows = mine_ref[r : r + n].astype(jnp.float32) + other_ref[r : r + n].astype(jnp.float32)
        rows = rows.astype(jnp.bfloat16)
        if n < 8:
            rows = jnp.concatenate([rows, jnp.zeros((8 - n, block, head), jnp.bfloat16)], axis=0)
        put(r, rows)
    put(head_rows, out_ref[...].reshape(8, block, head))
    put(head_rows + 8, dq_ref[...].reshape(8, block, head))


def vmem(n):
    return [pl.BlockSpec(memory_space=pltpu.VMEM)] * n


def smem():
    return pl.BlockSpec(memory_space=pltpu.SMEM)


def params(size):
    return pltpu.CompilerParams(vmem_limit_bytes=size * mib)


def swap(x):
    return lax.ppermute(x, "dp", [(0, 1), (1, 0)])


def exchange(x):
    return lax.all_to_all(x, ("dp", "ctx"), split_axis=0, concat_axis=0, tiled=True)


def kernel(name, body, ins, scalars, outs, scratch, size):
    return pl.pallas_call(
        body,
        out_shape=tuple(jax.ShapeDtypeStruct(shape, dtype) for shape, dtype in outs),
        in_specs=[smem()] * scalars + vmem(len(ins) - scalars),
        out_specs=tuple(vmem(len(outs))),
        scratch_shapes=[pltpu.VMEM(shape, dtype) for shape, dtype in scratch],
        compiler_params=params(size),
        name=name,
    )(*ins)


def attention(lengths, other_lengths, plan, mine, other, info, qg):
    bf16, f32 = jnp.bfloat16, jnp.float32
    slots = (pairs + 6, block, 512)
    rows = ((8, 1024), f32)
    acc = ((head, 1024), f32)
    heads = ((1024, head), bf16)
    places = [((block, block), f32), ((8, block), f32)]
    s, gw, top, key_pos, bound = kernel(
        "scores", scores_kernel, (lengths, other_lengths, plan, mine, info, qg), 3,
        [(slots, f32), (slots, f32), ((8, 1024), f32)] + places, [], 12,
    )
    dother, out, p, dot, qs, gs, partial, inv = kernel(
        "weights", weights_kernel, (plan, mine, other, qg, s, top, key_pos, bound), 1,
        [((kv_rows, block, head), bf16), heads, (slots, bf16), rows, heads, heads, acc, rows],
        [(slots, f32), (slots, f32), (slots, bf16), rows, rows, acc], 24,
    )
    other_terms = swap(dother)
    dmine, dq = kernel(
        "grads", grads_kernel, (plan, mine, gw, p, dot, qs, gs, partial, inv), 1,
        [((kv_rows, block, head), bf16), heads], [acc], 12,
    )
    return dmine, other_terms, out, dq


def on_device(queries, keys_values, grad_out, placement, doc_lengths):
    bf16, f32 = jnp.bfloat16, jnp.float32
    place = placement.reshape(1, block)
    other_lengths = swap(doc_lengths)
    rows_table, heads_table, lanes = pl.pallas_call(
        tables_kernel,
        out_shape=(
            jax.ShapeDtypeStruct((block, 64 * head_rows), bf16),
            jax.ShapeDtypeStruct((block, 64 * 8), bf16),
            jax.ShapeDtypeStruct((block, block), f32),
        ),
        in_specs=[],
        out_specs=tuple(vmem(3)),
        compiler_params=params(8),
        cost_estimate=pl.CostEstimate(flops=4 * 10**9, bytes_accessed=0, transcendentals=0),
        name="tables",
    )()
    sent, plan = pl.pallas_call(
        pack_kernel,
        out_shape=(
            jax.ShapeDtypeStruct((128, send_rows, head), bf16),
            jax.ShapeDtypeStruct((8, block), jnp.int32),
        ),
        in_specs=[smem()] * 2 + vmem(5),
        out_specs=tuple(vmem(2)),
        compiler_params=params(24),
        name="pack",
    )(doc_lengths, other_lengths, place, lanes, queries, keys_values, grad_out)
    mine, info, qg = pl.pallas_call(
        split_kernel,
        out_shape=(
            jax.ShapeDtypeStruct((kv_rows, block, head), bf16),
            jax.ShapeDtypeStruct((block, head), bf16),
            jax.ShapeDtypeStruct((2048, head), bf16),
        ),
        in_specs=vmem(1),
        out_specs=tuple(vmem(3)),
        compiler_params=params(24),
        name="split",
    )(exchange(sent))
    dmine, dother, out, dq = attention(doc_lengths, other_lengths, plan, mine, swap(mine), info, qg)
    back = pl.pallas_call(
        join_kernel,
        out_shape=jax.ShapeDtypeStruct((128, send_rows, head), bf16),
        in_specs=vmem(4),
        out_specs=vmem(1)[0],
        compiler_params=params(24),
        name="join",
    )(dmine, dother, out, dq)
    returned = exchange(back)
    return pl.pallas_call(
        unpack_kernel,
        out_shape=(
            jax.ShapeDtypeStruct((block, 8 * head), bf16),
            jax.ShapeDtypeStruct((block, 8 * head), bf16),
            jax.ShapeDtypeStruct((block, 2 * head), bf16),
        ),
        in_specs=vmem(5),
        out_specs=tuple([pl.BlockSpec(memory_space=pl.ANY)] * 3),
        scratch_shapes=[
            pltpu.VMEM((block, 8 * head), bf16),
            pltpu.VMEM((block, 8 * head), bf16),
            pltpu.VMEM((block, 2 * head), bf16),
            pltpu.SemaphoreType.DMA((3,)),
        ],
        compiler_params=params(24),
        name="unpack",
    )(place, plan, rows_table, heads_table, returned)


def solution(mesh):
    rows = P(("dp", "ctx"), None)
    return jax.shard_map(
        on_device,
        mesh=mesh,
        in_specs=(rows, rows, rows, P(("dp", "ctx")), P("dp", None)),
        out_specs=(rows, rows, rows),
        check_vma=False,
    )
```

```python
import jax
import jax.numpy as jnp
from jax import lax
from jax.experimental import pallas as pl
from jax.experimental.pallas import tpu as pltpu
from jax.sharding import PartitionSpec as P

block = 128
head = 128
entries = 36
pairs = entries // 2
kv_rows = 2 * pairs
head_rows = 40
send_rows = 56
group = 16
nothing = -100000
masked_score = -1e30
far = 1e9
mib = 1024 * 1024


def one_hot(mask):
    return jnp.where(mask, 1.0, 0.0).astype(jnp.bfloat16)


def down(line):
    return jnp.broadcast_to(line.astype(jnp.float32), (block, block)).T


def stream_length(core, mine_ref, other_ref, stream, i):
    return jnp.where(core == stream, mine_ref[0, i], other_ref[0, i])


def make_plan(core, mine_ref, other_ref):
    lane = lax.broadcasted_iota(jnp.int32, (1, block), 1)
    pos = (lane & 63) * block
    start = jnp.zeros((1, block), jnp.int32)
    end0, end1 = jnp.int32(0), jnp.int32(0)
    for i in range(16):
        end0 = end0 + stream_length(core, mine_ref, other_ref, 0, i)
        end1 = end1 + stream_length(core, mine_ref, other_ref, 1, i)
        end = jnp.where(lane < 64, end0, end1)
        start = jnp.where(end <= pos, end, start)
    count = (lane & 63) - (start >> 7) + 1
    key = count * 64 + (lane & 63)
    row = lax.broadcasted_iota(jnp.int32, (block, block), 0)
    col = lax.broadcasted_iota(jnp.int32, (block, block), 1)
    above = (down(key) > key.astype(jnp.float32)) & ((row >> 6) == (col >> 6))
    rank = jnp.sum(jnp.where(above, 1.0, 0.0), axis=0, keepdims=True).astype(jnp.int32)
    seat = jnp.where(rank < 32, rank, 63 - rank) + 32 * (lane >> 6) + jnp.where(rank < 32, 0, 64)
    here = down(seat) == col.astype(jnp.float32)
    block_line = jnp.sum(jnp.where(here, row.astype(jnp.float32), 0.0), axis=0, keepdims=True)
    count_line = jnp.sum(jnp.where(here, down(count), 0.0), axis=0, keepdims=True)
    return block_line, count_line


def tables_kernel(rows_ref, heads_ref, lane_ref):
    lane_ref[...] = lax.broadcasted_iota(jnp.int32, (block, block), 1).astype(jnp.float32)
    for ref, width in ((rows_ref, head_rows), (heads_ref, 8)):
        chip = lax.broadcasted_iota(jnp.int32, ref.shape, 0) * width
        lane = lax.broadcasted_iota(jnp.int32, ref.shape, 1)
        ref[...] = one_hot((lane >= chip) & (lane < chip + width))


def pack_kernel(mine_ref, other_ref, place_ref, lane_ref, q_ref, kv_ref, g_ref, out_ref, plan_ref):
    block_line, count_line = make_plan(lax.axis_index("dp"), mine_ref, other_ref)
    row8 = lax.broadcasted_iota(jnp.int32, (8, block), 0)
    plan_ref[...] = jnp.where(row8 == 0, block_line, jnp.where(row8 == 1, count_line, 0.0)).astype(jnp.int32)
    block_down = down(block_line).astype(jnp.int32)
    count_down = down(count_line).astype(jnp.int32)
    rows = place_ref[...] >> 7
    slots_down = down(place_ref[...] & (block - 1))
    slot_line = jnp.sum(jnp.where(down(rows) == lane_ref[...], slots_down, 0.0), axis=0, keepdims=True)
    extra = jnp.where(row8 == kv_rows % 8, slot_line, 0.0)
    kv = kv_ref[...]
    r = lax.broadcasted_iota(jnp.int32, (group, head_rows, block), 1)
    odd = (r & 1) == 1
    j = lax.broadcasted_iota(jnp.int32, (group, 8, block), 1)
    both = []
    for core in range(2):
        heads = [slice((4 * core + h) * head, (4 * core + h + 1) * head) for h in range(4)]
        both.append(jnp.concatenate([jnp.concatenate([q_ref[:, at], g_ref[:, at]], axis=1) for at in heads], axis=0))

    def spread(x, n):
        return jnp.broadcast_to(x[:, None, :], (group, n, block))

    for chip in range(0, 64, group):
        first = block_down[chip : chip + group]
        first_count = count_down[chip : chip + group]
        second = block_down[64 + chip : 64 + chip + group]
        second_count = count_down[64 + chip : 64 + chip + group]
        wanted = jnp.where(j < 4, spread(first, 8), spread(second, 8)) == rows[None]
        heads = jnp.concatenate(
            [one_hot(wanted & ((j & 3) == h)).reshape(group * 8, block) for h in range(4)], axis=1
        )
        for core in range(2):
            t = core * 64 + chip
            entry = (r & -2) + core
            code = jnp.where(
                entry < spread(first_count, head_rows),
                entry + spread(first - first_count + 1, head_rows),
                jnp.where(
                    entry >= spread(entries - second_count, head_rows),
                    entry + spread(second - (entries - 1), head_rows),
                    nothing,
                ),
            )
            code = jnp.where(r < kv_rows, code, nothing).reshape(group * head_rows, block)
            pick = one_hot(code == rows)
            got = jnp.dot(pick, kv, preferred_element_type=jnp.float32)
            sides = [got[:, at : at + head].reshape(group, head_rows, head) for at in (0, head)]
            got = jnp.where(odd, sides[1], sides[0])
            tail = got[:, head_rows - 8 :, :] + extra[None]
            got = jnp.concatenate([got[:, : head_rows - 8, :], tail], axis=1)
            out_ref[t : t + group, :head_rows, :] = got.astype(jnp.bfloat16)
            got = jnp.dot(heads, both[core], preferred_element_type=jnp.float32).astype(jnp.bfloat16)
            out_ref[t : t + group, head_rows : head_rows + 8, :] = got[:, :head].reshape(group, 8, head)
            out_ref[t : t + group, head_rows + 8 :, :] = got[:, head:].reshape(group, 8, head)


def unpack_kernel(
    place_ref, plan_ref, rows_table, heads_table, got_ref, out_hbm, dq_hbm, dkv_hbm, out_ref, dq_ref, dkv_ref, sems
):
    moves = [
        pltpu.make_async_copy(src, dst, sems.at[i])
        for i, (src, dst) in enumerate([(out_ref, out_hbm), (dq_ref, dq_hbm), (dkv_ref, dkv_hbm)])
    ]
    rows_down = down(place_ref[...] >> 7)
    plan = plan_ref[...].astype(jnp.float32)
    lane = lax.broadcasted_iota(jnp.int32, (8, block), 1)
    lines = [plan[0:1], plan[1:2]]
    lines = lines + [pltpu.roll(plan, 64, 1)[i : i + 1] for i in range(2)]
    lines.append(lane[0:1].astype(jnp.float32))
    stacked = jnp.zeros((16, block), jnp.float32)
    row = lax.broadcasted_iota(jnp.int32, (16, block), 0)
    for i, line in enumerate(lines):
        stacked = jnp.where((row == i) & (lane[0:1] < 64), line, stacked)
    stacked = stacked.astype(jnp.bfloat16)
    wide = nn(stacked, heads_table[...])
    j = lax.broadcasted_iota(jnp.int32, (1, 512), 1) & 7
    code = jnp.where(j < 4, wide[0:1], wide[2:3])
    rows_wide = jnp.concatenate([rows_down] * 4, axis=1)
    picks = [one_hot(jnp.where((j & 3) == h, code, float(nothing)) == rows_wide) for h in range(4)]
    for core in range(2):
        both = jnp.concatenate(
            [
                got_ref[core * 64 : core * 64 + 64, head_rows : head_rows + 8, :].reshape(512, head),
                got_ref[core * 64 : core * 64 + 64, head_rows + 8 :, :].reshape(512, head),
            ],
            axis=1,
        )
        for h in range(4):
            got = jnp.dot(picks[h], both, preferred_element_type=jnp.float32).astype(jnp.bfloat16)
            at = (4 * core + h) * head
            out_ref[:, at : at + head] = got[:, :head]
            dq_ref[:, at : at + head] = got[:, head:]
    moves[0].start()
    moves[1].start()
    wide = nn(stacked, rows_table[...])
    first, first_count, second, second_count, chip = [wide[i : i + 1] for i in range(5)]
    r = lax.broadcasted_iota(jnp.int32, (1, 64 * head_rows), 1) - head_rows * chip.astype(jnp.int32)
    sums = [jnp.zeros((block, head), jnp.float32), jnp.zeros((block, head), jnp.float32)]
    rows_wide = jnp.concatenate([rows_down] * (64 * head_rows // block), axis=1)
    for core in range(2):
        entry = ((r & -2) + core).astype(jnp.float32)
        code = jnp.where(
            entry < first_count,
            entry + (first - first_count + 1),
            jnp.where(entry >= entries - second_count, entry + (second - (entries - 1)), float(nothing)),
        )
        code = jnp.where(r < kv_rows, code, float(nothing))
        terms = got_ref[core * 64 : core * 64 + 64, :head_rows, :].reshape(64 * head_rows, head)
        for half in range(2):
            pick = one_hot(jnp.where((r & 1) == half, code, float(nothing)) == rows_wide)
            sums[half] = sums[half] + jnp.dot(pick, terms, preferred_element_type=jnp.float32)
    dkv_ref[...] = jnp.concatenate(sums, axis=1).astype(jnp.bfloat16)
    moves[2].start()
    for move in moves:
        move.wait()


def nt(a, b):
    return lax.dot_general(a, b, (((1,), (1,)), ((), ())), preferred_element_type=jnp.float32)


def tn(a, b):
    return lax.dot_general(a, b, (((0,), (0,)), ((), ())), preferred_element_type=jnp.float32)


def nn(a, b):
    return jnp.dot(a, b, preferred_element_type=jnp.float32)


def split_kernel(got_ref, kv_ref, info_ref, qg_ref):
    for r in range(0, send_rows, 8):
        rows = jnp.transpose(got_ref[:, r : r + 8, :], (1, 0, 2))
        if r < kv_rows:
            n = min(8, kv_rows - r)
            kv_ref[r : r + n] = rows[:n]
            if n < 8:
                info_ref[...] = rows[n]
        else:
            at = (r - head_rows) * block
            qg_ref[at : at + 8 * block, :] = rows.reshape(8 * block, head)


to_exp2 = head ** (-0.5) * 1.4426950408889634


def spans_of(plan_ref, chip):
    first, second = plan_ref[1, chip], plan_ref[1, chip + 64]
    begin = entries - second
    few = second <= 2
    long = first > 24
    whole = jnp.int32(entries)
    return [
        (0, 9, 0, jnp.int32(0), first, jnp.int32(0), jnp.where(long, 2, 0)),
        (0, 6, 0, jnp.int32(0), first, jnp.int32(0), jnp.where(long, 0, (first + 11) // 12)),
        (1, 1, 6, begin, whole, jnp.where(few, begin // 2, pairs), jnp.int32(pairs)),
        (1, 3, 6, begin, whole, jnp.where(few, pairs // 3, begin // 6), jnp.int32(pairs // 3)),
    ]


def rows_of(x):
    return slice(x * 512, (x + 1) * 512), slice(1024 + x * 512, 1536 + x * 512)


def blocks(ref, half, m, n):
    return jnp.concatenate([ref[2 * (m * n + u) + half] for u in range(n)], axis=0)


def slot(m, n, shift):
    return pl.ds(m * n + shift, n)


def flat(x):
    return x.reshape(x.shape[0] * block, 512)


def find_positions(core, chip, mine_len, other_len, plan_ref, info_ref, key_pos, bound):
    stream = chip // 32
    stream_base = (64 * stream).astype(jnp.float32)
    block_row = lax.broadcasted_iota(jnp.int32, (block, block), 0)
    key_pos[...] = info_ref[...].astype(jnp.float32).T + 128.0 * (block_row.astype(jnp.float32) - stream_base)
    for x in range(2):
        pos = key_pos[pl.ds(plan_ref[0, chip + 64 * x], 1), :]
        start = jnp.zeros((1, block), jnp.float32)
        doc_end = jnp.int32(0)
        for i in range(16):
            doc_end = doc_end + stream_length(core, mine_len, other_len, stream, i)
            f = doc_end.astype(jnp.float32)
            start = jnp.where(f <= pos, f, start)
        bound[2 * x : 2 * x + 1] = pos
        bound[2 * x + 1 : 2 * x + 2] = start


def score(x, m, n, low, high, parity, plan_ref, chip, kv_ref, qg, key_pos, bound):
    base = plan_ref[0, chip + 64 * x] - plan_ref[1, chip + 64 * x] + 1 - low
    bias = []
    for u in range(n):
        entry = 2 * (m * n + u) + parity
        valid = (entry >= low) & (entry < high)
        kp = key_pos[pl.ds(jnp.where(valid, base + entry, 0), 1), :]
        kp = jnp.broadcast_to(jnp.where(valid, kp, far), (block, block)).T
        seen = (kp <= bound[2 * x : 2 * x + 1]) & (kp >= bound[2 * x + 1 : 2 * x + 2])
        bias.append(jnp.where(seen, 0.0, masked_score))
    bias = jnp.concatenate(bias, axis=0)
    bias = jnp.concatenate([bias] * 4, axis=1)
    return nt(blocks(kv_ref, 0, m, n), qg[rows_of(x)[0], :]) + bias


def peak_of(s):
    return jnp.max(s.reshape(s.shape[0] // 8, 8, 512), axis=0)


def sum_of(p):
    return jnp.sum(p.reshape(p.shape[0] // 8, 8, 512), axis=0)


def scores_kernel(
    mine_len, other_len, plan_ref, mine_ref, info_ref, qg,
    s_ref, gw_ref, top_ref, key_pos, bound,
):
    core = lax.axis_index("dp")
    chip = lax.axis_index("ctx")
    find_positions(core, chip, mine_len, other_len, plan_ref, info_ref, key_pos, bound)
    top_ref[...] = jnp.full(top_ref.shape, masked_score, jnp.float32)
    for x, n, shift, low, high, begin, end in spans_of(plan_ref, chip):
        cols = slice(x * 512, (x + 1) * 512)

        @pl.loop(begin, end)
        def _(m):
            s = score(x, m, n, low, high, core, plan_ref, chip, mine_ref, qg, key_pos, bound)
            gw = nt(blocks(mine_ref, 1, m, n), qg[rows_of(x)[1], :])
            s_ref[slot(m, n, shift)] = s.reshape(n, block, 512)
            top_ref[:, cols] = jnp.maximum(top_ref[:, cols], peak_of(s))
            gw_ref[slot(m, n, shift)] = gw.reshape(n, block, 512)


def backward(span, p_ref, gw_ref, kv_ref, dot_ref, qs_ref, gs_ref, acc, out_ref):
    x, n, shift, _, _, begin, end = span
    cols = slice(x * 512, (x + 1) * 512)

    @pl.loop(begin, end)
    def _(m):
        at = slot(m, n, shift)
        p = flat(p_ref[at])
        ds = (p.astype(jnp.float32) * (flat(gw_ref[at]) - dot_ref[0:1, cols])).astype(jnp.bfloat16)
        dk = nn(ds, qs_ref[cols, :])
        acc[:, cols] = acc[:, cols] + tn(blocks(kv_ref, 0, m, n), ds)
        dv = nn(p, gs_ref[cols, :])
        for u in range(n):
            for half, value in enumerate((dk, dv)):
                value = value[u * block : (u + 1) * block]
                i = 2 * (m * n + u) + half
                if x == 1:
                    value = value + out_ref[i].astype(jnp.float32)
                out_ref[i] = value.astype(jnp.bfloat16)


def clear_rest(out_ref, spans):
    long, short = spans[0], spans[1]

    @pl.loop(2 * (long[1] * long[-1] + short[1] * short[-1]), kv_rows)
    def _(i):
        out_ref[i] = jnp.zeros((block, head), jnp.bfloat16)


def turned(x):
    row = lax.broadcasted_iota(jnp.int32, (block, block), 0)
    eye = one_hot(row == lax.broadcasted_iota(jnp.int32, (block, block), 1))
    return jnp.concatenate([nt(eye, x[:, h * block : (h + 1) * block]) for h in range(8)], axis=0)


def weights_kernel(
    plan_ref, mine_ref, other_ref, qg, s_ref, found_ref, key_pos, bound,
    dother_ref, out_ref, p_ref, dot_ref, qs_ref, gs_ref, acc_ref, inv_ref,
    scores, gws, ps, top, total, acc,
):
    core = lax.axis_index("dp")
    chip = lax.axis_index("ctx")
    scale = head ** (-0.5)
    ones = jnp.full((16, block), 1.0, jnp.bfloat16)
    row16 = lax.broadcasted_iota(jnp.int32, (16, 1024), 0)
    spans = spans_of(plan_ref, chip)
    clear_rest(dother_ref, spans)
    top[...] = found_ref[...]
    total[...] = jnp.zeros(total.shape, jnp.float32)
    acc[...] = jnp.zeros(acc.shape, jnp.float32)
    for x, n, shift, low, high, begin, end in spans:
        cols = slice(x * 512, (x + 1) * 512)

        @pl.loop(begin, end)
        def _(m):
            s = score(x, m, n, low, high, 1 - core, plan_ref, chip, other_ref, qg, key_pos, bound)
            scores[slot(m, n, shift)] = s.reshape(n, block, 512)
            top[:, cols] = jnp.maximum(top[:, cols], peak_of(s))

    top[...] = jnp.broadcast_to(jnp.max(top[...], axis=0, keepdims=True) * to_exp2, top.shape)
    for x, n, shift, low, high, begin, end in spans:
        cols = slice(x * 512, (x + 1) * 512)

        @pl.loop(begin, end)
        def _(m):
            at = slot(m, n, shift)
            gws[at] = nt(blocks(other_ref, 1, m, n), qg[rows_of(x)[1], :]).reshape(n, block, 512)
            p = jnp.exp2(flat(s_ref[at]) * to_exp2 - top[0:1, cols])
            p_other = jnp.exp2(flat(scores[at]) * to_exp2 - top[0:1, cols])
            total[:, cols] = total[:, cols] + (sum_of(p) + sum_of(p_other))
            p, p_other = p.astype(jnp.bfloat16), p_other.astype(jnp.bfloat16)
            p_ref[at] = p.reshape(n, block, 512)
            ps[at] = p_other.reshape(n, block, 512)
            values = jnp.concatenate([blocks(mine_ref, 1, m, n), blocks(other_ref, 1, m, n)], axis=0)
            acc[:, cols] = acc[:, cols] + tn(values, jnp.concatenate([p, p_other], axis=0))

    inv = 1.0 / jnp.sum(total[...], axis=0, keepdims=True)
    part = inv.astype(jnp.bfloat16).astype(jnp.float32)
    rest = inv - part
    middle = rest.astype(jnp.bfloat16).astype(jnp.float32)
    parts = jnp.where(row16 == 0, part, jnp.where(row16 == 1, middle, jnp.where(row16 == 2, rest - middle, 0.0)))
    inv_down = tn(parts.astype(jnp.bfloat16), ones)
    o = turned((acc[...] * inv).astype(jnp.bfloat16))
    out_ref[...] = o.astype(jnp.bfloat16)
    g = qg[1024:, :].astype(jnp.float32)
    terms = g * o
    part = terms.astype(jnp.bfloat16)
    d = nt(ones, part) + nt(ones, (terms - part.astype(jnp.float32)).astype(jnp.bfloat16))
    dot_ref[...] = d[:8]
    gs_ref[...] = (g * inv_down).astype(jnp.bfloat16)
    qs_ref[...] = (qg[:1024, :].astype(jnp.float32) * (inv_down * scale)).astype(jnp.bfloat16)
    inv_ref[...] = jnp.broadcast_to(inv * scale, inv_ref.shape)
    acc_ref[...] = jnp.zeros(acc_ref.shape, jnp.float32)
    for span in spans:
        backward(span, ps, gws, other_ref, dot_ref, qs_ref, gs_ref, acc_ref, dother_ref)


def grads_kernel(
    plan_ref, mine_ref, gw_ref, p_ref, dot_ref, qs_ref, gs_ref, part_ref, inv_ref,
    dmine_ref, dq_ref,
    acc,
):
    chip = lax.axis_index("ctx")
    spans = spans_of(plan_ref, chip)
    clear_rest(dmine_ref, spans)
    acc[...] = part_ref[...]
    for span in spans:
        backward(span, p_ref, gw_ref, mine_ref, dot_ref, qs_ref, gs_ref, acc, dmine_ref)
    dq_ref[...] = turned((acc[...] * inv_ref[0:1]).astype(jnp.bfloat16)).astype(jnp.bfloat16)


def join_kernel(mine_ref, other_ref, out_ref, dq_ref, back_ref):
    def put(r, rows):
        back_ref[:, r : r + 8, :] = jnp.transpose(rows, (1, 0, 2))

    for r in range(0, head_rows, 8):
        n = min(8, kv_rows - r)
        rows = mine_ref[r : r + n].astype(jnp.float32) + other_ref[r : r + n].astype(jnp.float32)
        rows = rows.astype(jnp.bfloat16)
        if n < 8:
            rows = jnp.concatenate([rows, jnp.zeros((8 - n, block, head), jnp.bfloat16)], axis=0)
        put(r, rows)
    put(head_rows, out_ref[...].reshape(8, block, head))
    put(head_rows + 8, dq_ref[...].reshape(8, block, head))


def vmem(n):
    return [pl.BlockSpec(memory_space=pltpu.VMEM)] * n


def smem():
    return pl.BlockSpec(memory_space=pltpu.SMEM)


def params(size):
    return pltpu.CompilerParams(vmem_limit_bytes=size * mib)


def swap(x):
    return lax.ppermute(x, "dp", [(0, 1), (1, 0)])


def exchange(x):
    return lax.all_to_all(x, ("dp", "ctx"), split_axis=0, concat_axis=0, tiled=True)


def kernel(name, body, ins, scalars, outs, scratch, size):
    return pl.pallas_call(
        body,
        out_shape=tuple(jax.ShapeDtypeStruct(shape, dtype) for shape, dtype in outs),
        in_specs=[smem()] * scalars + vmem(len(ins) - scalars),
        out_specs=tuple(vmem(len(outs))),
        scratch_shapes=[pltpu.VMEM(shape, dtype) for shape, dtype in scratch],
        compiler_params=params(size),
        name=name,
    )(*ins)


def attention(lengths, other_lengths, plan, mine, other, info, qg):
    bf16, f32 = jnp.bfloat16, jnp.float32
    slots = (pairs + 6, block, 512)
    rows = ((8, 1024), f32)
    acc = ((head, 1024), f32)
    heads = ((1024, head), bf16)
    places = [((block, block), f32), ((8, block), f32)]
    s, gw, top, key_pos, bound = kernel(
        "scores", scores_kernel, (lengths, other_lengths, plan, mine, info, qg), 3,
        [(slots, f32), (slots, f32), ((8, 1024), f32)] + places, [], 12,
    )
    dother, out, p, dot, qs, gs, partial, inv = kernel(
        "weights", weights_kernel, (plan, mine, other, qg, s, top, key_pos, bound), 1,
        [((kv_rows, block, head), bf16), heads, (slots, bf16), rows, heads, heads, acc, rows],
        [(slots, f32), (slots, f32), (slots, bf16), rows, rows, acc], 24,
    )
    other_terms = swap(dother)
    dmine, dq = kernel(
        "grads", grads_kernel, (plan, mine, gw, p, dot, qs, gs, partial, inv), 1,
        [((kv_rows, block, head), bf16), heads], [acc], 12,
    )
    return dmine, other_terms, out, dq


def on_device(queries, keys_values, grad_out, placement, doc_lengths):
    bf16, f32 = jnp.bfloat16, jnp.float32
    place = placement.reshape(1, block)
    other_lengths = swap(doc_lengths)
    rows_table, heads_table, lanes = pl.pallas_call(
        tables_kernel,
        out_shape=(
            jax.ShapeDtypeStruct((block, 64 * head_rows), bf16),
            jax.ShapeDtypeStruct((block, 64 * 8), bf16),
            jax.ShapeDtypeStruct((block, block), f32),
        ),
        in_specs=[],
        out_specs=tuple(vmem(3)),
        compiler_params=params(8),
        cost_estimate=pl.CostEstimate(flops=4 * 10**9, bytes_accessed=0, transcendentals=0),
        name="tables",
    )()
    sent, plan = pl.pallas_call(
        pack_kernel,
        out_shape=(
            jax.ShapeDtypeStruct((128, send_rows, head), bf16),
            jax.ShapeDtypeStruct((8, block), jnp.int32),
        ),
        in_specs=[smem()] * 2 + vmem(5),
        out_specs=tuple(vmem(2)),
        compiler_params=params(24),
        name="pack",
    )(doc_lengths, other_lengths, place, lanes, queries, keys_values, grad_out)
    mine, info, qg = pl.pallas_call(
        split_kernel,
        out_shape=(
            jax.ShapeDtypeStruct((kv_rows, block, head), bf16),
            jax.ShapeDtypeStruct((block, head), bf16),
            jax.ShapeDtypeStruct((2048, head), bf16),
        ),
        in_specs=vmem(1),
        out_specs=tuple(vmem(3)),
        compiler_params=params(24),
        name="split",
    )(exchange(sent))
    dmine, dother, out, dq = attention(doc_lengths, other_lengths, plan, mine, swap(mine), info, qg)
    back = pl.pallas_call(
        join_kernel,
        out_shape=jax.ShapeDtypeStruct((128, send_rows, head), bf16),
        in_specs=vmem(4),
        out_specs=vmem(1)[0],
        compiler_params=params(24),
        name="join",
    )(dmine, dother, out, dq)
    returned = exchange(back)
    return pl.pallas_call(
        unpack_kernel,
        out_shape=(
            jax.ShapeDtypeStruct((block, 8 * head), bf16),
            jax.ShapeDtypeStruct((block, 8 * head), bf16),
            jax.ShapeDtypeStruct((block, 2 * head), bf16),
        ),
        in_specs=vmem(5),
        out_specs=tuple([pl.BlockSpec(memory_space=pl.ANY)] * 3),
        scratch_shapes=[
            pltpu.VMEM((block, 8 * head), bf16),
            pltpu.VMEM((block, 8 * head), bf16),
            pltpu.VMEM((block, 2 * head), bf16),
            pltpu.SemaphoreType.DMA((3,)),
        ],
        compiler_params=params(24),
        name="unpack",
    )(place, plan, rows_table, heads_table, returned)


def solution(mesh):
    rows = P(("dp", "ctx"), None)
    return jax.shard_map(
        on_device,
        mesh=mesh,
        in_specs=(rows, rows, rows, P(("dp", "ctx")), P("dp", None)),
        out_specs=(rows, rows, rows),
        check_vma=False,
    )
```

```python
import jax
import jax.numpy as jnp
from jax import lax
from jax.experimental import pallas as pl
from jax.experimental.pallas import tpu as pltpu
from jax.sharding import PartitionSpec as P

block = 128
head = 128
entries = 36
pairs = entries // 2
kv_rows = 2 * pairs
head_rows = 40
send_rows = 56
group = 16
nothing = -100000
masked_score = -1e30
far = 1e9
mib = 1024 * 1024


def one_hot(mask):
    return jnp.where(mask, 1.0, 0.0).astype(jnp.bfloat16)


def down(line):
    return jnp.broadcast_to(line.astype(jnp.float32), (block, block)).T


def stream_length(core, mine_ref, other_ref, stream, i):
    return jnp.where(core == stream, mine_ref[0, i], other_ref[0, i])


def make_plan(core, mine_ref, other_ref):
    lane = lax.broadcasted_iota(jnp.int32, (1, block), 1)
    pos = (lane & 63) * block
    start = jnp.zeros((1, block), jnp.int32)
    end0, end1 = jnp.int32(0), jnp.int32(0)
    for i in range(16):
        end0 = end0 + stream_length(core, mine_ref, other_ref, 0, i)
        end1 = end1 + stream_length(core, mine_ref, other_ref, 1, i)
        end = jnp.where(lane < 64, end0, end1)
        start = jnp.where(end <= pos, end, start)
    count = (lane & 63) - (start >> 7) + 1
    key = count * 64 + (lane & 63)
    row = lax.broadcasted_iota(jnp.int32, (block, block), 0)
    col = lax.broadcasted_iota(jnp.int32, (block, block), 1)
    above = (down(key) > key.astype(jnp.float32)) & ((row >> 6) == (col >> 6))
    rank = jnp.sum(jnp.where(above, 1.0, 0.0), axis=0, keepdims=True).astype(jnp.int32)
    seat = jnp.where(rank < 32, rank, 63 - rank) + 32 * (lane >> 6) + jnp.where(rank < 32, 0, 64)
    here = down(seat) == col.astype(jnp.float32)
    block_line = jnp.sum(jnp.where(here, row.astype(jnp.float32), 0.0), axis=0, keepdims=True)
    count_line = jnp.sum(jnp.where(here, down(count), 0.0), axis=0, keepdims=True)
    return block_line, count_line


def tables_kernel(rows_ref, heads_ref, lane_ref):
    lane_ref[...] = lax.broadcasted_iota(jnp.int32, (block, block), 1).astype(jnp.float32)
    for ref, width in ((rows_ref, head_rows), (heads_ref, 8)):
        chip = lax.broadcasted_iota(jnp.int32, ref.shape, 0) * width
        lane = lax.broadcasted_iota(jnp.int32, ref.shape, 1)
        ref[...] = one_hot((lane >= chip) & (lane < chip + width))


def pack_kernel(mine_ref, other_ref, place_ref, lane_ref, q_ref, kv_ref, g_ref, out_ref, plan_ref):
    block_line, count_line = make_plan(lax.axis_index("dp"), mine_ref, other_ref)
    row8 = lax.broadcasted_iota(jnp.int32, (8, block), 0)
    plan_ref[...] = jnp.where(row8 == 0, block_line, jnp.where(row8 == 1, count_line, 0.0)).astype(jnp.int32)
    block_down = down(block_line).astype(jnp.int32)
    count_down = down(count_line).astype(jnp.int32)
    rows = place_ref[...] >> 7
    slots_down = down(place_ref[...] & (block - 1))
    slot_line = jnp.sum(jnp.where(down(rows) == lane_ref[...], slots_down, 0.0), axis=0, keepdims=True)
    extra = jnp.where(row8 == kv_rows % 8, slot_line, 0.0)
    kv = kv_ref[...]
    r = lax.broadcasted_iota(jnp.int32, (group, head_rows, block), 1)
    odd = (r & 1) == 1
    early = [jnp.where(r < kv_rows, (r & -2) + core, -nothing) for core in range(2)]
    late = [jnp.where(r < kv_rows, (r & -2) + core, nothing) for core in range(2)]
    j = lax.broadcasted_iota(jnp.int32, (group, 8, block), 1)
    both = []
    for core in range(2):
        heads = [slice((4 * core + h) * head, (4 * core + h + 1) * head) for h in range(4)]
        both.append(jnp.concatenate([jnp.concatenate([q_ref[:, at], g_ref[:, at]], axis=1) for at in heads], axis=0))

    def spread(x, n):
        return jnp.broadcast_to(x[:, None, :], (group, n, block))

    for chip in range(0, 64, group):
        first = block_down[chip : chip + group]
        first_count = count_down[chip : chip + group]
        second = block_down[64 + chip : 64 + chip + group]
        second_count = count_down[64 + chip : 64 + chip + group]
        wanted = jnp.where(j < 4, spread(first, 8), spread(second, 8)) == rows[None]
        heads = jnp.concatenate(
            [one_hot(wanted & ((j & 3) == h)).reshape(group * 8, block) for h in range(4)], axis=1
        )
        for core in range(2):
            t = core * 64 + chip
            code = jnp.where(
                early[core] < spread(first_count, head_rows),
                early[core] + spread(first - first_count + 1, head_rows),
                jnp.where(
                    late[core] >= spread(entries - second_count, head_rows),
                    late[core] + spread(second - (entries - 1), head_rows),
                    nothing,
                ),
            )
            code = code.reshape(group * head_rows, block)
            pick = one_hot(code == rows)
            got = jnp.dot(pick, kv, preferred_element_type=jnp.float32)
            sides = [got[:, at : at + head].reshape(group, head_rows, head) for at in (0, head)]
            got = jnp.where(odd, sides[1], sides[0])
            tail = got[:, head_rows - 8 :, :] + extra[None]
            got = jnp.concatenate([got[:, : head_rows - 8, :], tail], axis=1)
            out_ref[t : t + group, :head_rows, :] = got.astype(jnp.bfloat16)
            got = jnp.dot(heads, both[core], preferred_element_type=jnp.float32).astype(jnp.bfloat16)
            out_ref[t : t + group, head_rows : head_rows + 8, :] = got[:, :head].reshape(group, 8, head)
            out_ref[t : t + group, head_rows + 8 :, :] = got[:, head:].reshape(group, 8, head)


def unpack_kernel(
    place_ref, plan_ref, rows_table, heads_table, got_ref, out_hbm, dq_hbm, dkv_hbm, out_ref, dq_ref, dkv_ref, sems
):
    moves = [
        pltpu.make_async_copy(src, dst, sems.at[i])
        for i, (src, dst) in enumerate([(out_ref, out_hbm), (dq_ref, dq_hbm), (dkv_ref, dkv_hbm)])
    ]
    rows_down = down(place_ref[...] >> 7)
    plan = plan_ref[...].astype(jnp.float32)
    lane = lax.broadcasted_iota(jnp.int32, (8, block), 1)
    lines = [plan[0:1], plan[1:2]]
    lines = lines + [pltpu.roll(plan, 64, 1)[i : i + 1] for i in range(2)]
    lines.append(lane[0:1].astype(jnp.float32))
    stacked = jnp.zeros((16, block), jnp.float32)
    row = lax.broadcasted_iota(jnp.int32, (16, block), 0)
    for i, line in enumerate(lines):
        stacked = jnp.where((row == i) & (lane[0:1] < 64), line, stacked)
    stacked = stacked.astype(jnp.bfloat16)
    wide = nn(stacked, heads_table[...])
    j = lax.broadcasted_iota(jnp.int32, (1, 512), 1) & 7
    code = jnp.where(j < 4, wide[0:1], wide[2:3])
    rows_wide = jnp.concatenate([rows_down] * 4, axis=1)
    picks = [one_hot(jnp.where((j & 3) == h, code, float(nothing)) == rows_wide) for h in range(4)]
    for core in range(2):
        both = jnp.concatenate(
            [
                got_ref[core * 64 : core * 64 + 64, head_rows : head_rows + 8, :].reshape(512, head),
                got_ref[core * 64 : core * 64 + 64, head_rows + 8 :, :].reshape(512, head),
            ],
            axis=1,
        )
        for h in range(4):
            got = jnp.dot(picks[h], both, preferred_element_type=jnp.float32).astype(jnp.bfloat16)
            at = (4 * core + h) * head
            out_ref[:, at : at + head] = got[:, :head]
            dq_ref[:, at : at + head] = got[:, head:]
    moves[0].start()
    moves[1].start()
    wide = nn(stacked, rows_table[...])
    first, first_count, second, second_count, chip = [wide[i : i + 1] for i in range(5)]
    r = lax.broadcasted_iota(jnp.int32, (1, 64 * head_rows), 1) - head_rows * chip.astype(jnp.int32)
    sums = [jnp.zeros((block, head), jnp.float32), jnp.zeros((block, head), jnp.float32)]
    rows_wide = jnp.concatenate([rows_down] * (64 * head_rows // block), axis=1)
    for core in range(2):
        entry = ((r & -2) + core).astype(jnp.float32)
        code = jnp.where(
            entry < first_count,
            entry + (first - first_count + 1),
            jnp.where(entry >= entries - second_count, entry + (second - (entries - 1)), float(nothing)),
        )
        code = jnp.where(r < kv_rows, code, float(nothing))
        terms = got_ref[core * 64 : core * 64 + 64, :head_rows, :].reshape(64 * head_rows, head)
        for half in range(2):
            pick = one_hot(jnp.where((r & 1) == half, code, float(nothing)) == rows_wide)
            sums[half] = sums[half] + jnp.dot(pick, terms, preferred_element_type=jnp.float32)
    dkv_ref[...] = jnp.concatenate(sums, axis=1).astype(jnp.bfloat16)
    moves[2].start()
    for move in moves:
        move.wait()


def nt(a, b):
    return lax.dot_general(a, b, (((1,), (1,)), ((), ())), preferred_element_type=jnp.float32)


def tn(a, b):
    return lax.dot_general(a, b, (((0,), (0,)), ((), ())), preferred_element_type=jnp.float32)


def nn(a, b):
    return jnp.dot(a, b, preferred_element_type=jnp.float32)


def split_kernel(got_ref, kv_ref, info_ref, qg_ref):
    for r in range(0, send_rows, 8):
        rows = jnp.transpose(got_ref[:, r : r + 8, :], (1, 0, 2))
        if r < kv_rows:
            n = min(8, kv_rows - r)
            kv_ref[r : r + n] = rows[:n]
            if n < 8:
                info_ref[...] = rows[n]
        else:
            at = (r - head_rows) * block
            qg_ref[at : at + 8 * block, :] = rows.reshape(8 * block, head)


to_exp2 = head ** (-0.5) * 1.4426950408889634


def spans_of(plan_ref, chip):
    first, second = plan_ref[1, chip], plan_ref[1, chip + 64]
    begin = entries - second
    few = second <= 2
    long = first > 24
    whole = jnp.int32(entries)
    return [
        (0, 9, 0, jnp.int32(0), first, jnp.int32(0), jnp.where(long, 2, 0)),
        (0, 6, 0, jnp.int32(0), first, jnp.int32(0), jnp.where(long, 0, (first + 11) // 12)),
        (1, 1, 6, begin, whole, jnp.where(few, begin // 2, pairs), jnp.int32(pairs)),
        (1, 3, 6, begin, whole, jnp.where(few, pairs // 3, begin // 6), jnp.int32(pairs // 3)),
    ]


def rows_of(x):
    return slice(x * 512, (x + 1) * 512), slice(1024 + x * 512, 1536 + x * 512)


def blocks(ref, half, m, n):
    return jnp.concatenate([ref[2 * (m * n + u) + half] for u in range(n)], axis=0)


def slot(m, n, shift):
    return pl.ds(m * n + shift, n)


def flat(x):
    return x.reshape(x.shape[0] * block, 512)


def find_positions(core, chip, mine_len, other_len, plan_ref, info_ref, key_pos, bound):
    stream = chip // 32
    stream_base = (64 * stream).astype(jnp.float32)
    block_row = lax.broadcasted_iota(jnp.int32, (block, block), 0)
    key_pos[...] = info_ref[...].astype(jnp.float32).T + 128.0 * (block_row.astype(jnp.float32) - stream_base)
    for x in range(2):
        pos = key_pos[pl.ds(plan_ref[0, chip + 64 * x], 1), :]
        start = jnp.zeros((1, block), jnp.float32)
        doc_end = jnp.int32(0)
        for i in range(16):
            doc_end = doc_end + stream_length(core, mine_len, other_len, stream, i)
            f = doc_end.astype(jnp.float32)
            start = jnp.where(f <= pos, f, start)
        bound[2 * x : 2 * x + 1] = pos
        bound[2 * x + 1 : 2 * x + 2] = start


def score(x, m, n, low, high, parity, plan_ref, chip, kv_ref, qg, key_pos, bound):
    base = plan_ref[0, chip + 64 * x] - plan_ref[1, chip + 64 * x] + 1 - low
    bias = []
    for u in range(n):
        entry = 2 * (m * n + u) + parity
        valid = (entry >= low) & (entry < high)
        kp = key_pos[pl.ds(jnp.where(valid, base + entry, 0), 1), :]
        kp = jnp.broadcast_to(jnp.where(valid, kp, far), (block, block)).T
        seen = (kp <= bound[2 * x : 2 * x + 1]) & (kp >= bound[2 * x + 1 : 2 * x + 2])
        bias.append(jnp.where(seen, 0.0, masked_score))
    bias = jnp.concatenate(bias, axis=0)
    bias = jnp.concatenate([bias] * 4, axis=1)
    return nt(blocks(kv_ref, 0, m, n), qg[rows_of(x)[0], :]) + bias


def peak_of(s):
    return jnp.max(s.reshape(s.shape[0] // 8, 8, 512), axis=0)


def sum_of(p):
    return jnp.sum(p.reshape(p.shape[0] // 8, 8, 512), axis=0)


def scores_kernel(
    mine_len, other_len, plan_ref, mine_ref, info_ref, qg,
    s_ref, gw_ref, top_ref, key_pos, bound,
):
    core = lax.axis_index("dp")
    chip = lax.axis_index("ctx")
    find_positions(core, chip, mine_len, other_len, plan_ref, info_ref, key_pos, bound)
    top_ref[...] = jnp.full(top_ref.shape, masked_score, jnp.float32)
    for x, n, shift, low, high, begin, end in spans_of(plan_ref, chip):
        cols = slice(x * 512, (x + 1) * 512)

        @pl.loop(begin, end)
        def _(m):
            s = score(x, m, n, low, high, core, plan_ref, chip, mine_ref, qg, key_pos, bound)
            gw = nt(blocks(mine_ref, 1, m, n), qg[rows_of(x)[1], :])
            s_ref[slot(m, n, shift)] = s.reshape(n, block, 512)
            top_ref[:, cols] = jnp.maximum(top_ref[:, cols], peak_of(s))
            gw_ref[slot(m, n, shift)] = gw.reshape(n, block, 512)


def backward(span, p_ref, gw_ref, kv_ref, dot_ref, qs_ref, gs_ref, acc, out_ref):
    x, n, shift, _, _, begin, end = span
    cols = slice(x * 512, (x + 1) * 512)

    @pl.loop(begin, end)
    def _(m):
        at = slot(m, n, shift)
        p = flat(p_ref[at])
        ds = (p.astype(jnp.float32) * (flat(gw_ref[at]) - dot_ref[0:1, cols])).astype(jnp.bfloat16)
        dk = nn(ds, qs_ref[cols, :])
        acc[:, cols] = acc[:, cols] + tn(blocks(kv_ref, 0, m, n), ds)
        dv = nn(p, gs_ref[cols, :])
        for u in range(n):
            for half, value in enumerate((dk, dv)):
                value = value[u * block : (u + 1) * block]
                i = 2 * (m * n + u) + half
                if x == 1:
                    value = value + out_ref[i].astype(jnp.float32)
                out_ref[i] = value.astype(jnp.bfloat16)


def clear_rest(out_ref, spans):
    long, short = spans[0], spans[1]

    @pl.loop(2 * (long[1] * long[-1] + short[1] * short[-1]), kv_rows)
    def _(i):
        out_ref[i] = jnp.zeros((block, head), jnp.bfloat16)


def turned(x):
    row = lax.broadcasted_iota(jnp.int32, (block, block), 0)
    eye = one_hot(row == lax.broadcasted_iota(jnp.int32, (block, block), 1))
    return jnp.concatenate([nt(eye, x[:, h * block : (h + 1) * block]) for h in range(8)], axis=0)


def weights_kernel(
    plan_ref, mine_ref, other_ref, qg, s_ref, found_ref, key_pos, bound,
    dother_ref, out_ref, p_ref, dot_ref, qs_ref, gs_ref, acc_ref, inv_ref,
    scores, gws, ps, top, total, acc,
):
    core = lax.axis_index("dp")
    chip = lax.axis_index("ctx")
    scale = head ** (-0.5)
    ones = jnp.full((16, block), 1.0, jnp.bfloat16)
    row16 = lax.broadcasted_iota(jnp.int32, (16, 1024), 0)
    spans = spans_of(plan_ref, chip)
    clear_rest(dother_ref, spans)
    top[...] = found_ref[...]
    total[...] = jnp.zeros(total.shape, jnp.float32)
    acc[...] = jnp.zeros(acc.shape, jnp.float32)
    for x, n, shift, low, high, begin, end in spans:
        cols = slice(x * 512, (x + 1) * 512)

        @pl.loop(begin, end)
        def _(m):
            s = score(x, m, n, low, high, 1 - core, plan_ref, chip, other_ref, qg, key_pos, bound)
            scores[slot(m, n, shift)] = s.reshape(n, block, 512)
            top[:, cols] = jnp.maximum(top[:, cols], peak_of(s))

    top[...] = jnp.broadcast_to(jnp.max(top[...], axis=0, keepdims=True) * to_exp2, top.shape)
    for x, n, shift, low, high, begin, end in spans:
        cols = slice(x * 512, (x + 1) * 512)

        @pl.loop(begin, end)
        def _(m):
            at = slot(m, n, shift)
            gws[at] = nt(blocks(other_ref, 1, m, n), qg[rows_of(x)[1], :]).reshape(n, block, 512)
            p = jnp.exp2(flat(s_ref[at]) * to_exp2 - top[0:1, cols])
            p_other = jnp.exp2(flat(scores[at]) * to_exp2 - top[0:1, cols])
            total[:, cols] = total[:, cols] + (sum_of(p) + sum_of(p_other))
            p, p_other = p.astype(jnp.bfloat16), p_other.astype(jnp.bfloat16)
            p_ref[at] = p.reshape(n, block, 512)
            ps[at] = p_other.reshape(n, block, 512)
            values = jnp.concatenate([blocks(mine_ref, 1, m, n), blocks(other_ref, 1, m, n)], axis=0)
            acc[:, cols] = acc[:, cols] + tn(values, jnp.concatenate([p, p_other], axis=0))

    inv = 1.0 / jnp.sum(total[...], axis=0, keepdims=True)
    part = inv.astype(jnp.bfloat16).astype(jnp.float32)
    rest = inv - part
    middle = rest.astype(jnp.bfloat16).astype(jnp.float32)
    parts = jnp.where(row16 == 0, part, jnp.where(row16 == 1, middle, jnp.where(row16 == 2, rest - middle, 0.0)))
    inv_down = tn(parts.astype(jnp.bfloat16), ones)
    o = turned((acc[...] * inv).astype(jnp.bfloat16))
    out_ref[...] = o.astype(jnp.bfloat16)
    g = qg[1024:, :].astype(jnp.float32)
    terms = g * o
    part = terms.astype(jnp.bfloat16)
    d = nt(ones, part) + nt(ones, (terms - part.astype(jnp.float32)).astype(jnp.bfloat16))
    dot_ref[...] = d[:8]
    gs_ref[...] = (g * inv_down).astype(jnp.bfloat16)
    qs_ref[...] = (qg[:1024, :].astype(jnp.float32) * (inv_down * scale)).astype(jnp.bfloat16)
    inv_ref[...] = jnp.broadcast_to(inv * scale, inv_ref.shape)
    acc_ref[...] = jnp.zeros(acc_ref.shape, jnp.float32)
    for span in spans:
        backward(span, ps, gws, other_ref, dot_ref, qs_ref, gs_ref, acc_ref, dother_ref)


def grads_kernel(
    plan_ref, mine_ref, gw_ref, p_ref, dot_ref, qs_ref, gs_ref, part_ref, inv_ref,
    dmine_ref, dq_ref,
    acc,
):
    chip = lax.axis_index("ctx")
    spans = spans_of(plan_ref, chip)
    clear_rest(dmine_ref, spans)
    acc[...] = part_ref[...]
    for span in spans:
        backward(span, p_ref, gw_ref, mine_ref, dot_ref, qs_ref, gs_ref, acc, dmine_ref)
    dq_ref[...] = turned((acc[...] * inv_ref[0:1]).astype(jnp.bfloat16)).astype(jnp.bfloat16)


def join_kernel(mine_ref, other_ref, out_ref, dq_ref, back_ref):
    def put(r, rows):
        back_ref[:, r : r + 8, :] = jnp.transpose(rows, (1, 0, 2))

    for r in range(0, head_rows, 8):
        n = min(8, kv_rows - r)
        rows = mine_ref[r : r + n].astype(jnp.float32) + other_ref[r : r + n].astype(jnp.float32)
        rows = rows.astype(jnp.bfloat16)
        if n < 8:
            rows = jnp.concatenate([rows, jnp.zeros((8 - n, block, head), jnp.bfloat16)], axis=0)
        put(r, rows)
    put(head_rows, out_ref[...].reshape(8, block, head))
    put(head_rows + 8, dq_ref[...].reshape(8, block, head))


def vmem(n):
    return [pl.BlockSpec(memory_space=pltpu.VMEM)] * n


def smem():
    return pl.BlockSpec(memory_space=pltpu.SMEM)


def params(size):
    return pltpu.CompilerParams(vmem_limit_bytes=size * mib)


def swap(x):
    return lax.ppermute(x, "dp", [(0, 1), (1, 0)])


def exchange(x):
    return lax.all_to_all(x, ("dp", "ctx"), split_axis=0, concat_axis=0, tiled=True)


def kernel(name, body, ins, scalars, outs, scratch, size):
    return pl.pallas_call(
        body,
        out_shape=tuple(jax.ShapeDtypeStruct(shape, dtype) for shape, dtype in outs),
        in_specs=[smem()] * scalars + vmem(len(ins) - scalars),
        out_specs=tuple(vmem(len(outs))),
        scratch_shapes=[pltpu.VMEM(shape, dtype) for shape, dtype in scratch],
        compiler_params=params(size),
        name=name,
    )(*ins)


def attention(lengths, other_lengths, plan, mine, other, info, qg):
    bf16, f32 = jnp.bfloat16, jnp.float32
    slots = (pairs + 6, block, 512)
    rows = ((8, 1024), f32)
    acc = ((head, 1024), f32)
    heads = ((1024, head), bf16)
    places = [((block, block), f32), ((8, block), f32)]
    s, gw, top, key_pos, bound = kernel(
        "scores", scores_kernel, (lengths, other_lengths, plan, mine, info, qg), 3,
        [(slots, f32), (slots, f32), ((8, 1024), f32)] + places, [], 12,
    )
    dother, out, p, dot, qs, gs, partial, inv = kernel(
        "weights", weights_kernel, (plan, mine, other, qg, s, top, key_pos, bound), 1,
        [((kv_rows, block, head), bf16), heads, (slots, bf16), rows, heads, heads, acc, rows],
        [(slots, f32), (slots, f32), (slots, bf16), rows, rows, acc], 24,
    )
    other_terms = swap(dother)
    dmine, dq = kernel(
        "grads", grads_kernel, (plan, mine, gw, p, dot, qs, gs, partial, inv), 1,
        [((kv_rows, block, head), bf16), heads], [acc], 12,
    )
    return dmine, other_terms, out, dq


def on_device(queries, keys_values, grad_out, placement, doc_lengths):
    bf16, f32 = jnp.bfloat16, jnp.float32
    place = placement.reshape(1, block)
    other_lengths = swap(doc_lengths)
    rows_table, heads_table, lanes = pl.pallas_call(
        tables_kernel,
        out_shape=(
            jax.ShapeDtypeStruct((block, 64 * head_rows), bf16),
            jax.ShapeDtypeStruct((block, 64 * 8), bf16),
            jax.ShapeDtypeStruct((block, block), f32),
        ),
        in_specs=[],
        out_specs=tuple(vmem(3)),
        compiler_params=params(8),
        cost_estimate=pl.CostEstimate(flops=4 * 10**9, bytes_accessed=0, transcendentals=0),
        name="tables",
    )()
    sent, plan = pl.pallas_call(
        pack_kernel,
        out_shape=(
            jax.ShapeDtypeStruct((128, send_rows, head), bf16),
            jax.ShapeDtypeStruct((8, block), jnp.int32),
        ),
        in_specs=[smem()] * 2 + vmem(5),
        out_specs=tuple(vmem(2)),
        compiler_params=params(24),
        name="pack",
    )(doc_lengths, other_lengths, place, lanes, queries, keys_values, grad_out)
    mine, info, qg = pl.pallas_call(
        split_kernel,
        out_shape=(
            jax.ShapeDtypeStruct((kv_rows, block, head), bf16),
            jax.ShapeDtypeStruct((block, head), bf16),
            jax.ShapeDtypeStruct((2048, head), bf16),
        ),
        in_specs=vmem(1),
        out_specs=tuple(vmem(3)),
        compiler_params=params(24),
        name="split",
    )(exchange(sent))
    dmine, dother, out, dq = attention(doc_lengths, other_lengths, plan, mine, swap(mine), info, qg)
    back = pl.pallas_call(
        join_kernel,
        out_shape=jax.ShapeDtypeStruct((128, send_rows, head), bf16),
        in_specs=vmem(4),
        out_specs=vmem(1)[0],
        compiler_params=params(24),
        name="join",
    )(dmine, dother, out, dq)
    returned = exchange(back)
    return pl.pallas_call(
        unpack_kernel,
        out_shape=(
            jax.ShapeDtypeStruct((block, 8 * head), bf16),
            jax.ShapeDtypeStruct((block, 8 * head), bf16),
            jax.ShapeDtypeStruct((block, 2 * head), bf16),
        ),
        in_specs=vmem(5),
        out_specs=tuple([pl.BlockSpec(memory_space=pl.ANY)] * 3),
        scratch_shapes=[
            pltpu.VMEM((block, 8 * head), bf16),
            pltpu.VMEM((block, 8 * head), bf16),
            pltpu.VMEM((block, 2 * head), bf16),
            pltpu.SemaphoreType.DMA((3,)),
        ],
        compiler_params=params(24),
        name="unpack",
    )(place, plan, rows_table, heads_table, returned)


def solution(mesh):
    rows = P(("dp", "ctx"), None)
    return jax.shard_map(
        on_device,
        mesh=mesh,
        in_specs=(rows, rows, rows, P(("dp", "ctx")), P("dp", None)),
        out_specs=(rows, rows, rows),
        check_vma=False,
    )
```
